32 devices in a mesh: grp: 4 (over y, x), gx: 2 (over core), gy: 4 (over z).
Axes of the slice: x: 2, y: 2, z: 4, core: 2. Of those that a mesh axis runs over, the one named last changes fastest.
Arguments:
- source_term: float32 [16, 64, 1024], P('gx', 'gy', 'grp'), may hold values from -6 to 6
- conductivity: float32 [16, 64, 1024], P('gx', 'gy', 'grp'), may hold values from 0.5 to 4
- initial_field: float32 [16, 64, 1024], P('gx', 'gy', 'grp'), may hold values from -6 to 6
Outputs:
- solution: float32 [16, 64, 1024], P('gx', 'gy', 'grp')
The draws below stay inside these ranges and needn't reach their ends.
All inputs are finite; a program needn't handle non-finite values.
Results may differ from the reference program's by a relative error of at most 0.0001.
Values sent between devices are 32-bit elements; how exact they have to be, the bound alone decides.
No kernel may reach another device: no remote copies, remote signals or barrier semaphores. Data moves between devices by JAX's collectives and lax.ppermute only.
A program may use at most 64 MiB of HBM per device.

```python
import math
import jax
import jax.numpy as jnp

ITERS = 2
NX = 16
NY = 64
NZ = 1024


def shard_levels(key, dims, cuts, least, largest):
    loudness = 1.0
    for dim, blocks in cuts:
        draws = jax.random.uniform(jax.random.fold_in(jax.random.fold_in(key, 6), dim), (blocks,), jnp.float32, least / len(cuts), largest / len(cuts))
        loudness = loudness * jnp.repeat(jnp.exp(draws), dims[dim] // blocks).reshape((-1,) + (1,) * (len(dims) - 1 - dim))
    return loudness


def normal_values(own_key, shape, scale, bound, cuts=(), dtype=jnp.bfloat16):
    loudness = shard_levels(own_key, shape, cuts, -0.22, 0.18) if cuts else 1.0
    array = jax.random.normal(own_key, shape, jnp.float32) * scale * loudness
    return jnp.minimum(jnp.maximum(array, -bound), bound).astype(dtype)


def setup_inputs(seed: int = 0) -> dict:
    arg_keys = jax.random.split(jax.random.key(seed), 4)
    return {
        "source_term": normal_values(arg_keys[0], (NX, NY, NZ), 1.0, 6.0, ((0, 2), (1, 4), (2, 4)), jnp.float32),
        "conductivity": jnp.clip(jnp.exp(math.log(4.0) - 2.0794415 * jax.random.uniform(arg_keys[1], (NX, NY, NZ), jnp.float32) ** shard_levels(arg_keys[1], (NX, NY, NZ), ((0, 2), (1, 4), (2, 4)), -0.2, 0.2)), 0.5, 4.0),
        "initial_field": normal_values(arg_keys[2], (NX, NY, NZ), 1.0, 6.0, ((0, 2), (1, 4), (2, 4)), jnp.float32),
    }


FIRST_RATE = 0.8
CARRY_RATE = 9.0 / 41.0
FRESH_RATE = 40.0 / 41.0


def neighbours(padded):
    return [padded[:-2, 1:-1, 1:-1], padded[2:, 1:-1, 1:-1],
            padded[1:-1, :-2, 1:-1], padded[1:-1, 2:, 1:-1],
            padded[1:-1, 1:-1, :-2], padded[1:-1, 1:-1, 2:]]


def apply_operator(field_pad, cond_pad):
    center_field = field_pad[1:-1, 1:-1, 1:-1]
    center_cond = cond_pad[1:-1, 1:-1, 1:-1]
    result = jnp.zeros_like(center_field)
    for near_field, near_cond in zip(neighbours(field_pad), neighbours(cond_pad)):
        result = result + 0.5 * (center_cond + near_cond) * (center_field - near_field)
    return result


def diagonal_of(cond_pad):
    center_cond = cond_pad[1:-1, 1:-1, 1:-1]
    result = jnp.zeros_like(center_cond)
    for near_cond in neighbours(cond_pad):
        result = result + 0.5 * (center_cond + near_cond)
    return result


def block_mean(field):
    sizea, sizeb, sizec = field.shape
    return field.reshape(sizea // 2, 2, sizeb // 2, 2, sizec // 2, 2).mean(axis=(1, 3, 5))


def prolong(coarse):
    sizea, sizeb, sizec = coarse.shape
    spread = jnp.broadcast_to(coarse[:, None, :, None, :, None], (sizea, 2, sizeb, 2, sizec, 2))
    return spread.reshape(2 * sizea, 2 * sizeb, 2 * sizec)


def smooth(residual, cond_pad, scale):
    diagonal = scale * diagonal_of(cond_pad)
    first = FIRST_RATE * residual / diagonal
    image = scale * apply_operator(jnp.pad(first, 1), cond_pad)
    second = CARRY_RATE * first + FRESH_RATE * (residual - image) / diagonal
    return first + second


def reference(source_term, conductivity, initial_field):
    cond_pad = jnp.pad(conductivity, 1)
    coarse_pad = jnp.pad(block_mean(conductivity), 1)
    field = initial_field
    for iteration in range(ITERS):
        residual = source_term - apply_operator(jnp.pad(field, 1), cond_pad)
        fine_corr = smooth(residual, cond_pad, 1.0)
        coarse_corr = smooth(block_mean(residual), coarse_pad, 0.25)
        field = field + fine_corr + prolong(coarse_corr)
    return field
```

```python
import functools

import jax
import jax.numpy as jnp
from jax import lax
from jax.experimental import pallas as pl
from jax.experimental.pallas import tpu as pltpu
from jax.sharding import PartitionSpec as P

ITERS = 2
HALO = 4 * ITERS
LANES = 128
KEEP = 48.0 / 41.0
SPREAD = 32.0 / 41.0
VMEM = pl.BlockSpec(memory_space=pltpu.VMEM)


def ahead(v, axis, n=1):
    return pltpu.roll(v, v.shape[axis] - n, axis)


def behind(v, axis, n=1):
    return pltpu.roll(v, n, axis)


def swaps(axis, count):
    rounds = []
    for start in (0, 1):
        pairs = [(i, i + 1) for i in range(start, count - 1, 2)]
        if pairs:
            rounds.append(pairs + [(j, i) for i, j in pairs])
    return rounds


def is_odd(axis):
    return lax.rem(lax.axis_index(axis), 2)


def pack_rows(s, c, f, first, second):
    odd = is_odd("gy")
    last = s.shape[1] - HALO
    row_a = pl.multiple_of((1 - odd) * last, 8)
    row_b = pl.multiple_of(odd * last, 8)
    for a, ref in enumerate((s, c, f)):
        first[a] = ref[:, pl.ds(row_a, HALO), :]
        second[a] = ref[:, pl.ds(row_b, HALO), :]


def slots(rows):
    return [(a, g, a * (rows // 8) + g) for a in range(3) for g in range(rows // 8)]


def pack_columns(s, c, f, got_a, got_b, block, first, second):
    odd_y = is_odd("gy")
    odd_z = is_odd("grp")
    depth, own, width = s.shape
    rows = own + 2 * HALO
    for a, ref in enumerate((s, c, f)):
        block[a, :, HALO : HALO + own, :] = ref[...]
        from_a, from_b = got_a[a], got_b[a]
        block[a, :, 0:HALO, :] = jnp.where(odd_y == 1, from_a, from_b)
        block[a, :, HALO + own : rows, :] = jnp.where(odd_y == 1, from_b, from_a)
    lane = lax.broadcasted_iota(jnp.int32, (8, LANES), 1)

    def plane(p, carry):
        heads = [jnp.zeros((8, LANES), jnp.float32) for _ in range(first.shape[0])]
        tails = list(heads)
        for a, g, slot in slots(rows):
            at = 8 * (slot % 16)
            mine = (lane >= at) & (lane < at + HALO)
            head = pltpu.roll(block[a, p, 8 * g : 8 * g + 8, 0:LANES], at, 1)
            tail = pltpu.roll(
                block[a, p, 8 * g : 8 * g + 8, width - LANES : width], (at + HALO) % LANES, 1
            )
            heads[slot // 16] = jnp.where(mine, head, heads[slot // 16])
            tails[slot // 16] = jnp.where(mine, tail, tails[slot // 16])
        for t, (head, tail) in enumerate(zip(heads, tails)):
            first[t, p] = jnp.where(odd_z == 1, head, tail)
            second[t, p] = jnp.where(odd_z == 1, tail, head)
        return carry

    lax.fori_loop(0, depth, plane, 0)


def solve(cells, own_at, own, out):
    (src, cond, field, wx, wy, wz, inv, sum8, cwx, cwy, cwz, cinv, res, q, cq, err) = cells
    total = cond.shape[0]
    rows, lanes = cond.shape[1:]

    def reach(halo):
        low = max(1, own_at - halo)
        high = min(total, own_at + own + halo)
        return (low + 1) // 2, (high + 1) // 2

    zero = jnp.zeros((rows, lanes), jnp.float32)
    for ref in (q, cq, err, sum8):
        ref[0] = zero

    def gather8(k, carry):
        t = cond[2 * k - 1] + cond[2 * k]
        t = t + ahead(t, 0)
        sum8[k] = t + ahead(t, 1)
        return carry

    lax.fori_loop(*reach(HALO), gather8, 0)

    def weights(c, below, above, step):
        x = c + above
        y = c + ahead(c, 0, step)
        z = c + ahead(c, 1, step)
        k = (c + below + x) + (y + behind(y, 0, step)) + (z + behind(z, 1, step))
        return x, y, z, jnp.where(c > 0.0, 1.0 / k, 0.0)

    def setup(k, carry):
        for p in (2 * k - 1, 2 * k):
            wx[p], wy[p], wz[p], inv[p] = weights(cond[p], cond[p - 1], cond[p + 1], 1)
        cwx[k], cwy[k], cwz[k], cinv[k] = weights(sum8[k], sum8[k - 1], sum8[k + 1], 2)
        return carry

    low, high = reach(HALO - 2)
    wx[2 * low - 2] = cond[2 * low - 2] + cond[2 * low - 1]
    cwx[low - 1] = sum8[low - 1] + sum8[low]
    lax.fori_loop(low, high, setup, 0)

    row = lax.broadcasted_iota(jnp.int32, (rows, lanes), 0)
    lane = lax.broadcasted_iota(jnp.int32, (rows, lanes), 1)
    even_row = lax.rem(row, 2) == 0
    even_lane = lax.rem(lane, 2) == 0

    def image(v, p):
        here = v[p]
        across = wx[p - 1] * (here - v[p - 1]) - wx[p] * (v[p + 1] - here)
        fy = wy[p] * (ahead(here, 0) - here)
        fz = wz[p] * (ahead(here, 1) - here)
        return across + (behind(fy, 0) - fy) + (behind(fz, 1) - fz)

    def spread(v, p, x, y, z, step):
        here = v[p]
        n = x[p - 1] * v[p - 1] + x[p] * v[p + 1]
        n = n + (y[p] * ahead(here, 0, step) + behind(y[p] * here, 0, step))
        return n + (z[p] * ahead(here, 1, step) + behind(z[p] * here, 1, step))

    def smooth(v, p, x, y, z, diag, step):
        return KEEP * v[p] + SPREAD * (diag[p] * spread(v, p, x, y, z, step))

    for it in range(ITERS):
        halo = 4 * (ITERS - 1 - it)

        def residuals(k, carry, it=it):
            both = None
            for p in (2 * k - 1, 2 * k):
                if it == 0:
                    r = 2.0 * src[p] - image(field, p)
                else:
                    r = res[p] - image(err, p)
                res[p] = r
                q[p] = r * inv[p]
                both = r if both is None else both + r
            both = both + ahead(both, 0)
            both = both + ahead(both, 1)
            cq[k] = (4.0 * both) * cinv[k]
            return carry

        lax.fori_loop(*reach(halo + 2), residuals, 0)

        def corrections(k, carry, it=it):
            coarse = smooth(cq, k, cwx, cwy, cwz, cinv, 2)
            coarse = jnp.where(even_lane, coarse, behind(coarse, 1))
            coarse = jnp.where(even_row, coarse, behind(coarse, 0))
            for p in (2 * k - 1, 2 * k):
                e = smooth(q, p, wx, wy, wz, inv, 1) + coarse
                if it < ITERS - 1:
                    err[p] = err[p] + e if it else e
                else:
                    out(p, field[p] + (err[p] + e if it else e))
            return carry

        lax.fori_loop(*reach(halo), corrections, 0)


def finish(reflect, n_x, *refs):
    block = refs[0]
    near = refs[1 : 1 + n_x]
    got = refs[1 + n_x : 3 + n_x]
    near_got = refs[3 + n_x : 3 + 2 * n_x]
    result = refs[3 + 2 * n_x]
    cells = refs[4 + 2 * n_x :]
    _, depth, rows, width = block.shape
    odd_x = is_odd("gx")
    odd_z = is_odd("grp")
    own_at = 1 if reflect else 1 + HALO
    tiles = [cells[0], cells[1], cells[2]]
    lane = lax.broadcasted_iota(jnp.int32, (8, LANES), 1)

    def place(src, src_a, src_b, p_from, p_to):
        for a in range(3):
            tiles[a][p_to, :, 0:width] = src[a, p_from]
        for t in range(src_a.shape[0]):
            va, vb = src_a[t, p_from], src_b[t, p_from]
            upper = jnp.where(odd_z == 1, vb, va)
            lower = jnp.where(odd_z == 1, va, vb)
            for a, g, slot in slots(rows):
                if slot // 16 == t:
                    at = 8 * (slot % 16)
                    right = pltpu.roll(upper, (LANES - at) % LANES, 1)
                    left = pltpu.roll(lower, (2 * LANES - HALO - at) % LANES, 1)
                    tile = jnp.where(lane >= LANES - HALO, left, 0.0)
                    tile = jnp.where(lane < HALO, right, tile)
                    tiles[a][p_to, 8 * g : 8 * g + 8, width : width + LANES] = tile

    zero = jnp.zeros(tiles[0].shape[1:], jnp.float32)
    for tile in tiles:
        tile[0] = zero

    def own_plane(p, carry):
        to = jnp.where(odd_x == 1, depth - 1 - p, p) if reflect else p
        place(block, got[0], got[1], p, own_at + to)
        return carry

    lax.fori_loop(0, depth, own_plane, 0)

    def near_plane(p, carry):
        if reflect:
            at = jnp.where(odd_x == 1, depth - 1 - p, p)
            place(near[0], near_got[0].at[0], near_got[0].at[1], at, 1 + depth + p)
        else:
            for i in range(2):
                above = odd_x == i
                at = jnp.where(above, p, depth - HALO + p)
                to = jnp.where(above, own_at + depth + p, 1 + p)
                place(near[i], near_got[i].at[0], near_got[i].at[1], at, to)
        return carry

    lax.fori_loop(0, HALO, near_plane, 0)

    def out(p, v):
        at = p - own_at
        if reflect:
            at = jnp.where(odd_x == 1, depth - 1 - at, at)
        result[at] = v[HALO : rows - HALO, 0:width]

    solve(cells, own_at, depth, out)


def shards(sizes, source_term, conductivity, initial_field):
    depth, own, width = source_term.shape
    rows = own + 2 * HALO
    f32 = jnp.float32
    params = pltpu.CompilerParams(vmem_limit_bytes=48 * 1024 * 1024)
    args = (source_term, conductivity, initial_field)

    face = jax.ShapeDtypeStruct((3, depth, HALO, width), f32)
    msgs = pl.pallas_call(
        pack_rows, out_shape=(face, face), in_specs=[VMEM] * 3, out_specs=(VMEM, VMEM),
        compiler_params=params, name="pack_rows",
    )(*args)

    def exchange(values, axis):
        found = [lax.ppermute(v, axis, pairs) for v, pairs in zip(values, swaps(axis, sizes[axis]))]
        return found + [jnp.zeros_like(v) for v in values[len(found) :]]

    got = exchange(msgs, "gy")
    n_tiles = -(-3 * (rows // 8) // 16)
    strip = jax.ShapeDtypeStruct((n_tiles, depth, 8, LANES), f32)
    block, *cols = pl.pallas_call(
        pack_columns,
        out_shape=(jax.ShapeDtypeStruct((3, depth, rows, width), f32), strip, strip),
        in_specs=[VMEM] * 5, out_specs=(VMEM,) * 3,
        compiler_params=params, name="pack_columns",
    )(*args, *got)

    reflect = sizes["gx"] == 2
    n_x = 1 if reflect else 2
    got = exchange(cols, "grp")
    near = exchange([block] * n_x, "gx")
    near_got = exchange([jnp.stack(got)] * n_x, "gx")

    total = 1 + depth + HALO * n_x + 1
    lanes = width + LANES
    fine = pltpu.VMEM((total, rows, lanes), f32)
    coarse = pltpu.VMEM((total // 2 + 1, rows, lanes), f32)
    return pl.pallas_call(
        functools.partial(finish, reflect, n_x),
        out_shape=jax.ShapeDtypeStruct(source_term.shape, f32),
        in_specs=[VMEM] * (3 + 2 * n_x), out_specs=VMEM,
        scratch_shapes=[fine] * 7 + [coarse] * 5 + [fine] * 2 + [coarse] + [fine],
        compiler_params=params, name="finish",
    )(block, *near, *got, *near_got)


def solution(mesh):
    spec = P("gx", "gy", "grp")
    return jax.shard_map(
        functools.partial(shards, dict(mesh.shape)),
        mesh=mesh,
        in_specs=(spec,) * 3,
        out_specs=spec,
        check_vma=False,
    )
```

```python
import functools

import jax
import jax.numpy as jnp
from jax import lax
from jax.experimental import pallas as pl
from jax.experimental.pallas import tpu as pltpu
from jax.sharding import PartitionSpec as P

ITERS = 2
HALO = 4 * ITERS
LANES = 128
KEEP = 48.0 / 41.0
SPREAD = 32.0 / 41.0
VMEM = pl.BlockSpec(memory_space=pltpu.VMEM)


def ahead(v, axis, n=1):
    return pltpu.roll(v, v.shape[axis] - n, axis)


def behind(v, axis, n=1):
    return pltpu.roll(v, n, axis)


def swaps(axis, count):
    rounds = []
    for start in (0, 1):
        pairs = [(i, i + 1) for i in range(start, count - 1, 2)]
        if pairs:
            rounds.append(pairs + [(j, i) for i, j in pairs])
    return rounds


def is_odd(axis):
    return lax.rem(lax.axis_index(axis), 2)


def pack_rows(own, first, second):
    odd = is_odd("gy")
    last = own.shape[2] - HALO
    first[...] = own[:, :, pl.ds(pl.multiple_of((1 - odd) * last, 8), HALO), :]
    second[...] = own[:, :, pl.ds(pl.multiple_of(odd * last, 8), HALO), :]


def slots(rows):
    return [(a, g, a * (rows // 8) + g) for a in range(3) for g in range(rows // 8)]


def pack_columns(own, got_a, got_b, rim, first, second):
    odd_y = is_odd("gy")
    odd_z = is_odd("grp")
    _, depth, inner, width = own.shape
    groups = inner // 8 + 2
    lane = lax.broadcasted_iota(jnp.int32, (8, LANES), 1)

    def plane(p, carry):
        heads = [jnp.zeros((8, LANES), jnp.float32) for _ in range(first.shape[0])]
        tails = list(heads)
        for a, g, slot in slots(8 * groups):
            if g == 0 or g == groups - 1:
                from_a, from_b = got_a[a, p], got_b[a, p]
                above = odd_y == (1 if g == 0 else 0)
                strip = jnp.where(above, from_a, from_b)
                rim[0 if g == 0 else 1, a, p] = strip
                head, tail = strip[:, 0:LANES], strip[:, width - LANES : width]
            else:
                head = own[a, p, 8 * g - 8 : 8 * g, 0:LANES]
                tail = own[a, p, 8 * g - 8 : 8 * g, width - LANES : width]
            at = 8 * (slot % 16)
            mine = (lane >= at) & (lane < at + HALO)
            head = pltpu.roll(head, at, 1)
            tail = pltpu.roll(tail, (at + HALO) % LANES, 1)
            heads[slot // 16] = jnp.where(mine, head, heads[slot // 16])
            tails[slot // 16] = jnp.where(mine, tail, tails[slot // 16])
        for t, (head, tail) in enumerate(zip(heads, tails)):
            first[t, p] = jnp.where(odd_z == 1, head, tail)
            second[t, p] = jnp.where(odd_z == 1, tail, head)
        return carry

    lax.fori_loop(0, depth, plane, 0)


def solve(cells, own_at, own, out):
    (src, cond, field, wx, wy, wz, inv, sum8, cwx, cwy, cwz, cinv, res, q, cq, err) = cells
    total = cond.shape[0]
    rows, lanes = cond.shape[1:]

    def reach(halo):
        low = max(1, own_at - halo)
        high = min(total, own_at + own + halo)
        return (low + 1) // 2, (high + 1) // 2

    zero = jnp.zeros((rows, lanes), jnp.float32)
    for ref in (q, cq, err, sum8):
        ref[0] = zero

    def gather8(k, carry):
        t = cond[2 * k - 1] + cond[2 * k]
        t = t + ahead(t, 0)
        sum8[k] = t + ahead(t, 1)
        return carry

    lax.fori_loop(*reach(HALO), gather8, 0)

    def weights(c, below, above, step):
        x = c + above
        y = c + ahead(c, 0, step)
        z = c + ahead(c, 1, step)
        k = (c + below + x) + (y + behind(y, 0, step)) + (z + behind(z, 1, step))
        return x, y, z, jnp.where(c > 0.0, 1.0 / k, 0.0)

    def setup(k, carry):
        for p in (2 * k - 1, 2 * k):
            wx[p], wy[p], wz[p], inv[p] = weights(cond[p], cond[p - 1], cond[p + 1], 1)
        cwx[k], cwy[k], cwz[k], cinv[k] = weights(sum8[k], sum8[k - 1], sum8[k + 1], 2)
        return carry

    low, high = reach(HALO - 2)
    wx[2 * low - 2] = cond[2 * low - 2] + cond[2 * low - 1]
    cwx[low - 1] = sum8[low - 1] + sum8[low]
    lax.fori_loop(low, high, setup, 0)

    row = lax.broadcasted_iota(jnp.int32, (rows, lanes), 0)
    lane = lax.broadcasted_iota(jnp.int32, (rows, lanes), 1)
    even_row = lax.rem(row, 2) == 0
    even_lane = lax.rem(lane, 2) == 0

    def image(v, p):
        here = v[p]
        across = wx[p - 1] * (here - v[p - 1]) - wx[p] * (v[p + 1] - here)
        fy = wy[p] * (ahead(here, 0) - here)
        fz = wz[p] * (ahead(here, 1) - here)
        return across + (behind(fy, 0) - fy) + (behind(fz, 1) - fz)

    def spread(v, p, x, y, z, step):
        here = v[p]
        n = x[p - 1] * v[p - 1] + x[p] * v[p + 1]
        n = n + (y[p] * ahead(here, 0, step) + behind(y[p] * here, 0, step))
        return n + (z[p] * ahead(here, 1, step) + behind(z[p] * here, 1, step))

    def smooth(v, p, x, y, z, diag, step):
        return KEEP * v[p] + SPREAD * (diag[p] * spread(v, p, x, y, z, step))

    for it in range(ITERS):
        halo = 4 * (ITERS - 1 - it)

        def residuals(k, carry, it=it):
            both = None
            for p in (2 * k - 1, 2 * k):
                if it == 0:
                    r = 2.0 * src[p] - image(field, p)
                else:
                    r = res[p] - image(err, p)
                res[p] = r
                q[p] = r * inv[p]
                both = r if both is None else both + r
            both = both + ahead(both, 0)
            both = both + ahead(both, 1)
            cq[k] = (4.0 * both) * cinv[k]
            return carry

        lax.fori_loop(*reach(halo + 2), residuals, 0)

        def corrections(k, carry, it=it):
            coarse = smooth(cq, k, cwx, cwy, cwz, cinv, 2)
            coarse = jnp.where(even_lane, coarse, behind(coarse, 1))
            coarse = jnp.where(even_row, coarse, behind(coarse, 0))
            for p in (2 * k - 1, 2 * k):
                e = smooth(q, p, wx, wy, wz, inv, 1) + coarse
                if it < ITERS - 1:
                    err[p] = err[p] + e if it else e
                else:
                    out(p, field[p] + (err[p] + e if it else e))
            return carry

        lax.fori_loop(*reach(halo), corrections, 0)


def layout(reflect, depth):
    return (1, depth + HALO + 2) if reflect else (1 + HALO, depth + 2 * HALO + 2)


def each_plane(reflect, depth, place):
    odd_x = is_odd("gx")
    own_at, _ = layout(reflect, depth)

    def own_plane(p, carry):
        to = jnp.where(odd_x == 1, depth - 1 - p, p) if reflect else p
        place(None, p, own_at + to)
        return carry

    lax.fori_loop(0, depth, own_plane, 0)

    def near_plane(p, carry):
        if reflect:
            place(0, jnp.where(odd_x == 1, depth - 1 - p, p), own_at + depth + p)
            return carry
        for i in range(2):
            above = odd_x == i
            at = jnp.where(above, p, depth - HALO + p)
            place(i, at, jnp.where(above, own_at + depth + p, 1 + p))
        return carry

    lax.fori_loop(0, HALO, near_plane, 0)


def out_plane(reflect, depth, p):
    own_at, _ = layout(reflect, depth)
    at = p - own_at
    return jnp.where(is_odd("gx") == 1, depth - 1 - at, at) if reflect else at


def interior(reflect, n_x, *refs):
    own, rim = refs[0], refs[1]
    near, near_rim = refs[2 : 2 + n_x], refs[2 + n_x : 2 + 2 * n_x]
    result, ends = refs[2 + 2 * n_x : 4 + 2 * n_x]
    cells = refs[4 + 2 * n_x :]
    _, depth, inner, width = own.shape
    rows = inner + 2 * HALO
    lane = lax.broadcasted_iota(jnp.int32, (rows, LANES), 1)

    def place(i, p_from, p_to):
        block, halo = (own, rim) if i is None else (near[i], near_rim[i])
        for a in range(3):
            tile = cells[a]
            tile[p_to, 0:HALO, :] = halo[0, a, p_from]
            tile[p_to, HALO : HALO + inner, :] = block[a, p_from]
            tile[p_to, HALO + inner : rows, :] = halo[1, a, p_from]
            head = pltpu.roll(tile[p_to, :, 0:LANES], LANES // 2, 1)
            tail = tile[p_to, :, width - LANES : width]
            end = jnp.where((lane >= LANES // 2) & (lane < LANES // 2 + 2 * HALO), head, 0.0)
            ends[a, p_to] = jnp.where(lane >= LANES - 2 * HALO, tail, end)

    own_at, total = layout(reflect, depth)
    for a in range(3):
        for p in (0, total - 1):
            cells[a][p] = jnp.zeros((rows, width), jnp.float32)
            ends[a, p] = jnp.zeros((rows, LANES), jnp.float32)
    each_plane(reflect, depth, place)

    def out(p, v):
        result[out_plane(reflect, depth, p)] = v[HALO : rows - HALO, :]

    solve(cells, own_at, depth, out)


def edges(reflect, n_x, *refs):
    ends, inside, got_a, got_b = refs[:4]
    near_got = refs[4 : 4 + n_x]
    result = refs[4 + n_x]
    cells = refs[5 + n_x :]
    depth, inner, width = inside.shape
    rows = inner + 2 * HALO
    odd_z = is_odd("grp")
    lane = lax.broadcasted_iota(jnp.int32, (8, LANES), 1)
    in_right = lane < HALO
    in_left = (lane >= LANES // 2 - HALO) & (lane < LANES // 2)

    def place(i, p_from, p_to):
        for t in range(got_a.shape[0]):
            if i is None:
                va, vb = got_a[t, p_from], got_b[t, p_from]
            else:
                va, vb = near_got[i][0, t, p_from], near_got[i][1, t, p_from]
            upper = jnp.where(odd_z == 1, vb, va)
            lower = jnp.where(odd_z == 1, va, vb)
            for a, g, slot in slots(rows):
                if slot // 16 == t:
                    at = 8 * (slot % 16)
                    right = pltpu.roll(upper, (LANES - at) % LANES, 1)
                    left = pltpu.roll(lower, (LANES + LANES // 2 - HALO - at) % LANES, 1)
                    tile = ends[a, p_to, 8 * g : 8 * g + 8, :]
                    tile = jnp.where(in_left, left, tile)
                    cells[a][p_to, 8 * g : 8 * g + 8, :] = jnp.where(in_right, right, tile)

    own_at, total = layout(reflect, depth)
    for a in range(3):
        for p in (0, total - 1):
            cells[a][p] = ends[a, p]
    each_plane(reflect, depth, place)
    result[...] = inside[...]
    wide = lax.broadcasted_iota(jnp.int32, (inner, LANES), 1)

    def out(p, v):
        at = out_plane(reflect, depth, p)
        v = v[HALO : rows - HALO, :]
        head = pltpu.roll(v, LANES // 2, 1)
        result[at, :, 0:LANES] = jnp.where(wide < HALO, head, result[at, :, 0:LANES])
        tail = result[at, :, width - LANES : width]
        result[at, :, width - LANES : width] = jnp.where(wide >= LANES - HALO, v, tail)

    solve(cells, own_at, depth, out)


def shards(sizes, source_term, conductivity, initial_field):
    depth, inner, width = source_term.shape
    rows = inner + 2 * HALO
    f32 = jnp.float32
    params = pltpu.CompilerParams(vmem_limit_bytes=48 * 1024 * 1024)
    args = (source_term, conductivity, initial_field)

    def exchange(values, axis):
        found = [lax.ppermute(v, axis, pairs) for v, pairs in zip(values, swaps(axis, sizes[axis]))]
        return found + [jnp.zeros_like(v) for v in values[len(found) :]]

    def work(lanes):
        total = layout(reflect, depth)[1]
        fine = pltpu.VMEM((total, rows, lanes), f32)
        coarse = pltpu.VMEM((total // 2 + 1, rows, lanes), f32)
        return [fine] * 7 + [coarse] * 5 + [fine] * 2 + [coarse] + [fine]

    reflect = sizes["gx"] == 2
    n_x = 1 if reflect else 2
    face = jax.ShapeDtypeStruct((3, depth, HALO, width), f32)
    own = jnp.stack(args)
    msgs = pl.pallas_call(
        pack_rows, out_shape=(face, face), in_specs=[VMEM], out_specs=(VMEM, VMEM),
        compiler_params=params, name="pack_rows",
    )(own)
    got = exchange(msgs, "gy")
    near = exchange([own] * n_x, "gx")

    n_tiles = -(-3 * (rows // 8) // 16)
    strip = jax.ShapeDtypeStruct((n_tiles, depth, 8, LANES), f32)
    rim, *cols = pl.pallas_call(
        pack_columns,
        out_shape=(jax.ShapeDtypeStruct((2, 3, depth, HALO, width), f32), strip, strip),
        in_specs=[VMEM] * 3, out_specs=(VMEM,) * 3,
        compiler_params=params, name="pack_columns",
    )(own, *got)
    got = exchange(cols, "grp")
    near_rim = exchange([rim] * n_x, "gx")

    block = jax.ShapeDtypeStruct(source_term.shape, f32)
    total = layout(reflect, depth)[1]
    inside, ends = pl.pallas_call(
        functools.partial(interior, reflect, n_x),
        out_shape=(block, jax.ShapeDtypeStruct((3, total, rows, LANES), f32)),
        in_specs=[VMEM] * (2 + 2 * n_x), out_specs=(VMEM, VMEM), scratch_shapes=work(width),
        compiler_params=params, name="interior",
        cost_estimate=pl.CostEstimate(flops=20_000_000, bytes_accessed=20_000_000, transcendentals=0),
    )(own, rim, *near, *near_rim)
    inside, ends, got = lax.optimization_barrier((inside, ends, got))
    near_got = exchange([jnp.stack(got)] * n_x, "gx")
    return pl.pallas_call(
        functools.partial(edges, reflect, n_x),
        out_shape=block,
        in_specs=[VMEM] * (4 + n_x), out_specs=VMEM, scratch_shapes=work(LANES),
        compiler_params=params, name="edges",
    )(ends, inside, *got, *near_got)


def solution(mesh):
    spec = P("gx", "gy", "grp")
    return jax.shard_map(
        functools.partial(shards, dict(mesh.shape)),
        mesh=mesh,
        in_specs=(spec,) * 3,
        out_specs=spec,
        check_vma=False,
    )
```

```python
import functools

import jax
import jax.numpy as jnp
from jax import lax
from jax.experimental import pallas as pl
from jax.experimental.pallas import tpu as pltpu
from jax.sharding import PartitionSpec as P

ITERS = 2
HALO = 4 * ITERS
LANES = 128
KEEP = 48.0 / 41.0
SPREAD = 32.0 / 41.0
VMEM = pl.BlockSpec(memory_space=pltpu.VMEM)


def ahead(v, axis, n=1):
    return pltpu.roll(v, v.shape[axis] - n, axis)


def behind(v, axis, n=1):
    return pltpu.roll(v, n, axis)


def swaps(axis, count):
    rounds = []
    for start in (0, 1):
        pairs = [(i, i + 1) for i in range(start, count - 1, 2)]
        if pairs:
            rounds.append(pairs + [(j, i) for i, j in pairs])
    return rounds


def is_odd(axis):
    return lax.rem(lax.axis_index(axis), 2)


def pack_rows(own, first, second):
    odd = is_odd("gy")
    last = own.shape[2] - HALO
    first[...] = own[:, :, pl.ds(pl.multiple_of((1 - odd) * last, 8), HALO), :]
    second[...] = own[:, :, pl.ds(pl.multiple_of(odd * last, 8), HALO), :]


def slots(rows):
    return [(a, g, a * (rows // 8) + g) for a in range(3) for g in range(rows // 8)]


def pack_columns(own, got_a, got_b, rim, first, second):
    odd_y = is_odd("gy")
    odd_z = is_odd("grp")
    _, depth, inner, width = own.shape
    groups = inner // 8 + 2
    lane = lax.broadcasted_iota(jnp.int32, (8, LANES), 1)

    def plane(p, carry):
        heads = [jnp.zeros((8, LANES), jnp.float32) for _ in range(first.shape[0])]
        tails = list(heads)
        for a, g, slot in slots(8 * groups):
            if g == 0 or g == groups - 1:
                from_a, from_b = got_a[a, p], got_b[a, p]
                above = odd_y == (1 if g == 0 else 0)
                strip = jnp.where(above, from_a, from_b)
                rim[0 if g == 0 else 1, a, p] = strip
                head, tail = strip[:, 0:LANES], strip[:, width - LANES : width]
            else:
                head = own[a, p, 8 * g - 8 : 8 * g, 0:LANES]
                tail = own[a, p, 8 * g - 8 : 8 * g, width - LANES : width]
            at = 8 * (slot % 16)
            mine = (lane >= at) & (lane < at + HALO)
            head = pltpu.roll(head, at, 1)
            tail = pltpu.roll(tail, (at + HALO) % LANES, 1)
            heads[slot // 16] = jnp.where(mine, head, heads[slot // 16])
            tails[slot // 16] = jnp.where(mine, tail, tails[slot // 16])
        for t, (head, tail) in enumerate(zip(heads, tails)):
            first[t, p] = jnp.where(odd_z == 1, head, tail)
            second[t, p] = jnp.where(odd_z == 1, tail, head)
        return carry

    lax.fori_loop(0, depth, plane, 0)


def solve(cells, own_at, own, out):
    (src, cond, field, wx, wy, wz, inv, sum8, cwx, cwy, cwz, cinv, res, q, cq, err) = cells
    total = cond.shape[0]
    rows, lanes = cond.shape[1:]

    def reach(halo):
        low = max(1, own_at - halo)
        high = min(total, own_at + own + halo)
        return (low + 1) // 2, (high + 1) // 2

    zero = jnp.zeros((rows, lanes), jnp.float32)
    for ref in (q, cq, err, sum8):
        ref[0] = zero

    def gather8(k, carry):
        t = cond[2 * k - 1] + cond[2 * k]
        t = t + ahead(t, 0)
        sum8[k] = t + ahead(t, 1)
        return carry

    lax.fori_loop(*reach(HALO), gather8, 0, unroll=True)

    def weights(c, below, above, step):
        x = c + above
        y = c + ahead(c, 0, step)
        z = c + ahead(c, 1, step)
        k = (c + below + x) + (y + behind(y, 0, step)) + (z + behind(z, 1, step))
        return x, y, z, jnp.where(c > 0.0, 1.0 / k, 0.0)

    def setup(k, carry):
        for p in (2 * k - 1, 2 * k):
            wx[p], wy[p], wz[p], inv[p] = weights(cond[p], cond[p - 1], cond[p + 1], 1)
        cwx[k], cwy[k], cwz[k], cinv[k] = weights(sum8[k], sum8[k - 1], sum8[k + 1], 2)
        return carry

    low, high = reach(HALO - 2)
    wx[2 * low - 2] = cond[2 * low - 2] + cond[2 * low - 1]
    cwx[low - 1] = sum8[low - 1] + sum8[low]
    lax.fori_loop(low, high, setup, 0, unroll=True)

    row = lax.broadcasted_iota(jnp.int32, (rows, lanes), 0)
    lane = lax.broadcasted_iota(jnp.int32, (rows, lanes), 1)
    even_row = lax.rem(row, 2) == 0
    even_lane = lax.rem(lane, 2) == 0

    def image(v, p):
        here = v[p]
        across = wx[p - 1] * (here - v[p - 1]) - wx[p] * (v[p + 1] - here)
        fy = wy[p] * (ahead(here, 0) - here)
        fz = wz[p] * (ahead(here, 1) - here)
        return across + (behind(fy, 0) - fy) + (behind(fz, 1) - fz)

    def spread(v, p, x, y, z, step):
        here = v[p]
        n = x[p - 1] * v[p - 1] + x[p] * v[p + 1]
        n = n + (y[p] * ahead(here, 0, step) + behind(y[p] * here, 0, step))
        return n + (z[p] * ahead(here, 1, step) + behind(z[p] * here, 1, step))

    def smooth(v, p, x, y, z, diag, step):
        return KEEP * v[p] + SPREAD * (diag[p] * spread(v, p, x, y, z, step))

    for it in range(ITERS):
        halo = 4 * (ITERS - 1 - it)

        def residuals(k, carry, it=it):
            both = None
            for p in (2 * k - 1, 2 * k):
                if it == 0:
                    r = 2.0 * src[p] - image(field, p)
                else:
                    r = res[p] - image(err, p)
                res[p] = r
                q[p] = r * inv[p]
                both = r if both is None else both + r
            both = both + ahead(both, 0)
            both = both + ahead(both, 1)
            cq[k] = (4.0 * both) * cinv[k]
            return carry

        lax.fori_loop(*reach(halo + 2), residuals, 0, unroll=True)

        def corrections(k, carry, it=it):
            coarse = smooth(cq, k, cwx, cwy, cwz, cinv, 2)
            coarse = jnp.where(even_lane, coarse, behind(coarse, 1))
            coarse = jnp.where(even_row, coarse, behind(coarse, 0))
            for p in (2 * k - 1, 2 * k):
                e = smooth(q, p, wx, wy, wz, inv, 1) + coarse
                if it < ITERS - 1:
                    err[p] = err[p] + e if it else e
                else:
                    out(p, field[p] + (err[p] + e if it else e))
            return carry

        lax.fori_loop(*reach(halo), corrections, 0, unroll=True)


def layout(reflect, depth):
    return (1, depth + HALO + 2) if reflect else (1 + HALO, depth + 2 * HALO + 2)


def each_plane(reflect, depth, place):
    odd_x = is_odd("gx")
    own_at, _ = layout(reflect, depth)

    def own_plane(p, carry):
        to = jnp.where(odd_x == 1, depth - 1 - p, p) if reflect else p
        place(None, p, own_at + to)
        return carry

    lax.fori_loop(0, depth, own_plane, 0, unroll=True)

    def near_plane(p, carry):
        if reflect:
            place(0, jnp.where(odd_x == 1, depth - 1 - p, p), own_at + depth + p)
            return carry
        for i in range(2):
            above = odd_x == i
            at = jnp.where(above, p, depth - HALO + p)
            place(i, at, jnp.where(above, own_at + depth + p, 1 + p))
        return carry

    lax.fori_loop(0, HALO, near_plane, 0, unroll=True)


def out_plane(reflect, depth, p):
    own_at, _ = layout(reflect, depth)
    at = p - own_at
    return jnp.where(is_odd("gx") == 1, depth - 1 - at, at) if reflect else at


def interior(reflect, n_x, *refs):
    own, rim = refs[0], refs[1]
    near, near_rim = refs[2 : 2 + n_x], refs[2 + n_x : 2 + 2 * n_x]
    result, ends = refs[2 + 2 * n_x : 4 + 2 * n_x]
    cells = refs[4 + 2 * n_x :]
    _, depth, inner, width = own.shape
    rows = inner + 2 * HALO
    lane = lax.broadcasted_iota(jnp.int32, (rows, LANES), 1)

    def place(i, p_from, p_to):
        block, halo = (own, rim) if i is None else (near[i], near_rim[i])
        for a in range(3):
            tile = cells[a]
            tile[p_to, 0:HALO, :] = halo[0, a, p_from]
            tile[p_to, HALO : HALO + inner, :] = block[a, p_from]
            tile[p_to, HALO + inner : rows, :] = halo[1, a, p_from]
            head = pltpu.roll(tile[p_to, :, 0:LANES], LANES // 2, 1)
            tail = tile[p_to, :, width - LANES : width]
            end = jnp.where((lane >= LANES // 2) & (lane < LANES // 2 + 2 * HALO), head, 0.0)
            ends[a, p_to] = jnp.where(lane >= LANES - 2 * HALO, tail, end)

    own_at, total = layout(reflect, depth)
    for a in range(3):
        for p in (0, total - 1):
            cells[a][p] = jnp.zeros((rows, width), jnp.float32)
            ends[a, p] = jnp.zeros((rows, LANES), jnp.float32)
    each_plane(reflect, depth, place)

    def out(p, v):
        result[out_plane(reflect, depth, p)] = v[HALO : rows - HALO, :]

    solve(cells, own_at, depth, out)


def edges(reflect, n_x, *refs):
    ends, inside, got_a, got_b = refs[:4]
    near_got = refs[4 : 4 + n_x]
    result = refs[4 + n_x]
    cells = refs[5 + n_x :]
    depth, inner, width = inside.shape
    rows = inner + 2 * HALO
    odd_z = is_odd("grp")
    lane = lax.broadcasted_iota(jnp.int32, (8, LANES), 1)
    in_right = lane < HALO
    in_left = (lane >= LANES // 2 - HALO) & (lane < LANES // 2)

    def place(i, p_from, p_to):
        for t in range(got_a.shape[0]):
            if i is None:
                va, vb = got_a[t, p_from], got_b[t, p_from]
            else:
                va, vb = near_got[i][0, t, p_from], near_got[i][1, t, p_from]
            upper = jnp.where(odd_z == 1, vb, va)
            lower = jnp.where(odd_z == 1, va, vb)
            for a, g, slot in slots(rows):
                if slot // 16 == t:
                    at = 8 * (slot % 16)
                    right = pltpu.roll(upper, (LANES - at) % LANES, 1)
                    left = pltpu.roll(lower, (LANES + LANES // 2 - HALO - at) % LANES, 1)
                    tile = ends[a, p_to, 8 * g : 8 * g + 8, :]
                    tile = jnp.where(in_left, left, tile)
                    cells[a][p_to, 8 * g : 8 * g + 8, :] = jnp.where(in_right, right, tile)

    own_at, total = layout(reflect, depth)
    for a in range(3):
        for p in (0, total - 1):
            cells[a][p] = ends[a, p]
    each_plane(reflect, depth, place)
    result[...] = inside[...]
    wide = lax.broadcasted_iota(jnp.int32, (inner, LANES), 1)

    def out(p, v):
        at = out_plane(reflect, depth, p)
        v = v[HALO : rows - HALO, :]
        head = pltpu.roll(v, LANES // 2, 1)
        result[at, :, 0:LANES] = jnp.where(wide < HALO, head, result[at, :, 0:LANES])
        tail = result[at, :, width - LANES : width]
        result[at, :, width - LANES : width] = jnp.where(wide >= LANES - HALO, v, tail)

    solve(cells, own_at, depth, out)


def shards(sizes, source_term, conductivity, initial_field):
    depth, inner, width = source_term.shape
    rows = inner + 2 * HALO
    f32 = jnp.float32
    params = pltpu.CompilerParams(vmem_limit_bytes=48 * 1024 * 1024)
    args = (source_term, conductivity, initial_field)

    def exchange(values, axis):
        found = [lax.ppermute(v, axis, pairs) for v, pairs in zip(values, swaps(axis, sizes[axis]))]
        return found + [jnp.zeros_like(v) for v in values[len(found) :]]

    def work(lanes):
        total = layout(reflect, depth)[1]
        fine = pltpu.VMEM((total, rows, lanes), f32)
        coarse = pltpu.VMEM((total // 2 + 1, rows, lanes), f32)
        return [fine] * 7 + [coarse] * 5 + [fine] * 2 + [coarse] + [fine]

    reflect = sizes["gx"] == 2
    n_x = 1 if reflect else 2
    face = jax.ShapeDtypeStruct((3, depth, HALO, width), f32)
    own = jnp.stack(args)
    msgs = pl.pallas_call(
        pack_rows, out_shape=(face, face), in_specs=[VMEM], out_specs=(VMEM, VMEM),
        compiler_params=params, name="pack_rows",
    )(own)
    got = exchange(msgs, "gy")
    near = exchange([own] * n_x, "gx")

    n_tiles = -(-3 * (rows // 8) // 16)
    strip = jax.ShapeDtypeStruct((n_tiles, depth, 8, LANES), f32)
    rim, *cols = pl.pallas_call(
        pack_columns,
        out_shape=(jax.ShapeDtypeStruct((2, 3, depth, HALO, width), f32), strip, strip),
        in_specs=[VMEM] * 3, out_specs=(VMEM,) * 3,
        compiler_params=params, name="pack_columns",
    )(own, *got)
    got = exchange(cols, "grp")
    near_rim = exchange([rim] * n_x, "gx")

    block = jax.ShapeDtypeStruct(source_term.shape, f32)
    total = layout(reflect, depth)[1]
    inside, ends = pl.pallas_call(
        functools.partial(interior, reflect, n_x),
        out_shape=(block, jax.ShapeDtypeStruct((3, total, rows, LANES), f32)),
        in_specs=[VMEM] * (2 + 2 * n_x), out_specs=(VMEM, VMEM), scratch_shapes=work(width),
        compiler_params=params, name="interior",
        cost_estimate=pl.CostEstimate(flops=20_000_000, bytes_accessed=20_000_000, transcendentals=0),
    )(own, rim, *near, *near_rim)
    inside, ends, got = lax.optimization_barrier((inside, ends, got))
    near_got = exchange([jnp.stack(got)] * n_x, "gx")
    return pl.pallas_call(
        functools.partial(edges, reflect, n_x),
        out_shape=block,
        in_specs=[VMEM] * (4 + n_x), out_specs=VMEM, scratch_shapes=work(LANES),
        compiler_params=params, name="edges",
    )(ends, inside, *got, *near_got)


def solution(mesh):
    spec = P("gx", "gy", "grp")
    return jax.shard_map(
        functools.partial(shards, dict(mesh.shape)),
        mesh=mesh,
        in_specs=(spec,) * 3,
        out_specs=spec,
        check_vma=False,
    )
```

```python
import functools

import jax
import jax.numpy as jnp
from jax import lax
from jax.experimental import pallas as pl
from jax.experimental.pallas import tpu as pltpu
from jax.sharding import PartitionSpec as P

ITERS = 2
HALO = 4 * ITERS
LANES = 128
KEEP = 48.0 / 41.0
SPREAD = 32.0 / 41.0
VMEM = pl.BlockSpec(memory_space=pltpu.VMEM)


def ahead(v, axis, n=1):
    return pltpu.roll(v, v.shape[axis] - n, axis)


def behind(v, axis, n=1):
    return pltpu.roll(v, n, axis)


def swaps(axis, sizes):
    count, fill = sizes[axis], sizes["gx"]
    over = [name for name in sizes if name in (axis, "gx")]
    filled = axis != "gx" and fill % 2 == 0

    def at(i, k):
        return i * fill + k if over[0] == axis else k * count + i

    rounds = []
    for start in (0, 1):
        pairs = [(i, i + 1) for i in range(start, count - 1, 2)]
        left = set(range(count)) - {i for pair in pairs for i in pair}
        if not pairs:
            continue
        if filled:
            pairs = [(at(i, k), at(j, k)) for i, j in pairs for k in range(fill)]
            pairs += [(at(i, k), at(i, k + 1)) for i in sorted(left) for k in range(0, fill, 2)]
        rounds.append(pairs + [(j, i) for i, j in pairs])
    return (tuple(over) if filled else axis), rounds


def is_odd(axis):
    return lax.rem(lax.axis_index(axis), 2)


def beyond(axis):
    at = lax.axis_index(axis)
    return at == 0, at == lax.axis_size(axis) - 1


def is_odd(axis):
    return lax.rem(lax.axis_index(axis), 2)


def pack_rows(own, first, second):
    odd = is_odd("gy")
    last = own.shape[2] - HALO
    first[...] = own[:, :, pl.ds(pl.multiple_of((1 - odd) * last, 8), HALO), :]
    second[...] = own[:, :, pl.ds(pl.multiple_of(odd * last, 8), HALO), :]


def slots(rows):
    return [(a, g, a * (rows // 8) + g) for a in range(3) for g in range(rows // 8)]


def pack_columns(own, got_a, got_b, rim, first, second):
    odd_y = is_odd("gy")
    odd_z = is_odd("grp")
    _, depth, inner, width = own.shape
    groups = inner // 8 + 2
    first_y, last_y = beyond("gy")
    lane = lax.broadcasted_iota(jnp.int32, (8, LANES), 1)

    def plane(p, carry):
        heads = [jnp.zeros((8, LANES), jnp.float32) for _ in range(first.shape[0])]
        tails = list(heads)
        for a, g, slot in slots(8 * groups):
            if g == 0 or g == groups - 1:
                from_a, from_b = got_a[a, p], got_b[a, p]
                low = g == 0
                strip = jnp.where(odd_y == (1 if low else 0), from_a, from_b)
                strip = jnp.where(first_y if low else last_y, 0.0, strip)
                rim[0 if g == 0 else 1, a, p] = strip
                head, tail = strip[:, 0:LANES], strip[:, width - LANES : width]
            else:
                head = own[a, p, 8 * g - 8 : 8 * g, 0:LANES]
                tail = own[a, p, 8 * g - 8 : 8 * g, width - LANES : width]
            at = 8 * (slot % 16)
            mine = (lane >= at) & (lane < at + HALO)
            head = pltpu.roll(head, at, 1)
            tail = pltpu.roll(tail, (at + HALO) % LANES, 1)
            heads[slot // 16] = jnp.where(mine, head, heads[slot // 16])
            tails[slot // 16] = jnp.where(mine, tail, tails[slot // 16])
        for t, (head, tail) in enumerate(zip(heads, tails)):
            first[t, p] = jnp.where(odd_z == 1, head, tail)
            second[t, p] = jnp.where(odd_z == 1, tail, head)
        return carry

    lax.fori_loop(0, depth, plane, 0)


def solve(cells, own_at, own, out):
    (src, cond, field, wx, wy, wz, inv, sum8, cwx, cwy, cwz, cinv, res, q, cq, err) = cells
    total = cond.shape[0]
    rows, lanes = cond.shape[1:]

    def reach(halo):
        low = max(1, own_at - halo)
        high = min(total, own_at + own + halo)
        return (low + 1) // 2, (high + 1) // 2

    zero = jnp.zeros((rows, lanes), jnp.float32)
    for ref in (q, cq, err, sum8):
        ref[0] = zero

    def gather8(k, carry):
        t = cond[2 * k - 1] + cond[2 * k]
        t = t + ahead(t, 0)
        sum8[k] = t + ahead(t, 1)
        return carry

    lax.fori_loop(*reach(HALO), gather8, 0, unroll=True)

    def weights(c, below, above, step):
        x = c + above
        y = c + ahead(c, 0, step)
        z = c + ahead(c, 1, step)
        k = (c + below + x) + (y + behind(y, 0, step)) + (z + behind(z, 1, step))
        return x, y, z, jnp.where(c > 0.0, 1.0 / k, 0.0)

    def setup(k, carry):
        for p in (2 * k - 1, 2 * k):
            wx[p], wy[p], wz[p], inv[p] = weights(cond[p], cond[p - 1], cond[p + 1], 1)
        cwx[k], cwy[k], cwz[k], cinv[k] = weights(sum8[k], sum8[k - 1], sum8[k + 1], 2)
        return carry

    low, high = reach(HALO - 2)
    wx[2 * low - 2] = cond[2 * low - 2] + cond[2 * low - 1]
    cwx[low - 1] = sum8[low - 1] + sum8[low]
    lax.fori_loop(low, high, setup, 0, unroll=True)

    row = lax.broadcasted_iota(jnp.int32, (rows, lanes), 0)
    lane = lax.broadcasted_iota(jnp.int32, (rows, lanes), 1)
    even_row = lax.rem(row, 2) == 0
    even_lane = lax.rem(lane, 2) == 0

    def image(v, p):
        here = v[p]
        across = wx[p - 1] * (here - v[p - 1]) - wx[p] * (v[p + 1] - here)
        fy = wy[p] * (ahead(here, 0) - here)
        fz = wz[p] * (ahead(here, 1) - here)
        return across + (behind(fy, 0) - fy) + (behind(fz, 1) - fz)

    def spread(v, p, x, y, z, step):
        here = v[p]
        n = x[p - 1] * v[p - 1] + x[p] * v[p + 1]
        n = n + (y[p] * ahead(here, 0, step) + behind(y[p] * here, 0, step))
        return n + (z[p] * ahead(here, 1, step) + behind(z[p] * here, 1, step))

    def smooth(v, p, x, y, z, diag, step):
        return KEEP * v[p] + SPREAD * (diag[p] * spread(v, p, x, y, z, step))

    for it in range(ITERS):
        halo = 4 * (ITERS - 1 - it)

        def residuals(k, carry, it=it):
            both = None
            for p in (2 * k - 1, 2 * k):
                if it == 0:
                    r = 2.0 * src[p] - image(field, p)
                else:
                    r = res[p] - image(err, p)
                res[p] = r
                q[p] = r * inv[p]
                both = r if both is None else both + r
            both = both + ahead(both, 0)
            both = both + ahead(both, 1)
            cq[k] = (4.0 * both) * cinv[k]
            return carry

        lax.fori_loop(*reach(halo + 2), residuals, 0, unroll=True)

        def corrections(k, carry, it=it):
            coarse = smooth(cq, k, cwx, cwy, cwz, cinv, 2)
            coarse = jnp.where(even_lane, coarse, behind(coarse, 1))
            coarse = jnp.where(even_row, coarse, behind(coarse, 0))
            for p in (2 * k - 1, 2 * k):
                e = smooth(q, p, wx, wy, wz, inv, 1) + coarse
                if it < ITERS - 1:
                    err[p] = err[p] + e if it else e
                else:
                    out(p, field[p] + (err[p] + e if it else e))
            return carry

        lax.fori_loop(*reach(halo), corrections, 0, unroll=True)


def layout(reflect, depth):
    return (1, depth + HALO + 2) if reflect else (1 + HALO, depth + 2 * HALO + 2)


def each_plane(reflect, depth, place):
    odd_x = is_odd("gx")
    own_at, _ = layout(reflect, depth)

    def own_plane(p, carry):
        to = jnp.where(odd_x == 1, depth - 1 - p, p) if reflect else p
        place(None, p, own_at + to)
        return carry

    lax.fori_loop(0, depth, own_plane, 0, unroll=True)

    def near_plane(p, carry):
        if reflect:
            place(0, jnp.where(odd_x == 1, depth - 1 - p, p), own_at + depth + p)
            return carry
        for i in range(2):
            above = odd_x == i
            at = jnp.where(above, p, depth - HALO + p)
            place(i, at, jnp.where(above, own_at + depth + p, 1 + p))
        return carry

    lax.fori_loop(0, HALO, near_plane, 0, unroll=True)


def out_plane(reflect, depth, p):
    own_at, _ = layout(reflect, depth)
    at = p - own_at
    return jnp.where(is_odd("gx") == 1, depth - 1 - at, at) if reflect else at


def interior(reflect, n_x, *refs):
    own, rim = refs[0], refs[1]
    near, near_rim = refs[2 : 2 + n_x], refs[2 + n_x : 2 + 2 * n_x]
    result, ends = refs[2 + 2 * n_x : 4 + 2 * n_x]
    cells = refs[4 + 2 * n_x :]
    _, depth, inner, width = own.shape
    rows = inner + 2 * HALO
    lane = lax.broadcasted_iota(jnp.int32, (rows, LANES), 1)

    def place(i, p_from, p_to):
        block, halo = (own, rim) if i is None else (near[i], near_rim[i])
        for a in range(3):
            tile = cells[a]
            tile[p_to, 0:HALO, :] = halo[0, a, p_from]
            tile[p_to, HALO : HALO + inner, :] = block[a, p_from]
            tile[p_to, HALO + inner : rows, :] = halo[1, a, p_from]
            head = pltpu.roll(tile[p_to, :, 0:LANES], LANES // 2, 1)
            tail = tile[p_to, :, width - LANES : width]
            end = jnp.where((lane >= LANES // 2) & (lane < LANES // 2 + 2 * HALO), head, 0.0)
            ends[a, p_to] = jnp.where(lane >= LANES - 2 * HALO, tail, end)

    own_at, total = layout(reflect, depth)
    for a in range(3):
        for p in (0, total - 1):
            cells[a][p] = jnp.zeros((rows, width), jnp.float32)
            ends[a, p] = jnp.zeros((rows, LANES), jnp.float32)
    each_plane(reflect, depth, place)

    def out(p, v):
        result[out_plane(reflect, depth, p)] = v[HALO : rows - HALO, :]

    solve(cells, own_at, depth, out)


def edges(reflect, n_x, *refs):
    ends, inside, got_a, got_b = refs[:4]
    near_got = refs[4 : 4 + n_x]
    result = refs[4 + n_x]
    cells = refs[5 + n_x :]
    depth, inner, width = inside.shape
    rows = inner + 2 * HALO
    odd_z = is_odd("grp")
    first_z, last_z = beyond("grp")
    lane = lax.broadcasted_iota(jnp.int32, (8, LANES), 1)
    in_right = lane < HALO
    in_left = (lane >= LANES // 2 - HALO) & (lane < LANES // 2)

    def place(i, p_from, p_to):
        for t in range(got_a.shape[0]):
            if i is None:
                va, vb = got_a[t, p_from], got_b[t, p_from]
            else:
                va, vb = near_got[i][0, t, p_from], near_got[i][1, t, p_from]
            upper = jnp.where(last_z, 0.0, jnp.where(odd_z == 1, vb, va))
            lower = jnp.where(first_z, 0.0, jnp.where(odd_z == 1, va, vb))
            for a, g, slot in slots(rows):
                if slot // 16 == t:
                    at = 8 * (slot % 16)
                    right = pltpu.roll(upper, (LANES - at) % LANES, 1)
                    left = pltpu.roll(lower, (LANES + LANES // 2 - HALO - at) % LANES, 1)
                    tile = ends[a, p_to, 8 * g : 8 * g + 8, :]
                    tile = jnp.where(in_left, left, tile)
                    cells[a][p_to, 8 * g : 8 * g + 8, :] = jnp.where(in_right, right, tile)

    own_at, total = layout(reflect, depth)
    for a in range(3):
        for p in (0, total - 1):
            cells[a][p] = ends[a, p]
    each_plane(reflect, depth, place)
    result[...] = inside[...]
    wide = lax.broadcasted_iota(jnp.int32, (inner, LANES), 1)

    def out(p, v):
        at = out_plane(reflect, depth, p)
        v = v[HALO : rows - HALO, :]
        head = pltpu.roll(v, LANES // 2, 1)
        result[at, :, 0:LANES] = jnp.where(wide < HALO, head, result[at, :, 0:LANES])
        tail = result[at, :, width - LANES : width]
        result[at, :, width - LANES : width] = jnp.where(wide >= LANES - HALO, v, tail)

    solve(cells, own_at, depth, out)


def shards(sizes, source_term, conductivity, initial_field):
    depth, inner, width = source_term.shape
    rows = inner + 2 * HALO
    f32 = jnp.float32
    params = pltpu.CompilerParams(vmem_limit_bytes=48 * 1024 * 1024)
    args = (source_term, conductivity, initial_field)

    def exchange(values, axis):
        over, rounds = swaps(axis, sizes)
        found = [lax.ppermute(v, over, pairs) for v, pairs in reversed(list(zip(values, rounds)))]
        return found[::-1] + [jnp.zeros_like(v) for v in values[len(found) :]]

    def work(lanes):
        total = layout(reflect, depth)[1]
        fine = pltpu.VMEM((total, rows, lanes), f32)
        coarse = pltpu.VMEM((total // 2 + 1, rows, lanes), f32)
        return [fine] * 7 + [coarse] * 5 + [fine] * 2 + [coarse] + [fine]

    reflect = sizes["gx"] == 2
    n_x = 1 if reflect else 2
    face = jax.ShapeDtypeStruct((3, depth, HALO, width), f32)
    own = jnp.stack(args)
    msgs = pl.pallas_call(
        pack_rows, out_shape=(face, face), in_specs=[VMEM], out_specs=(VMEM, VMEM),
        compiler_params=params, name="pack_rows",
    )(own)
    got = exchange(msgs, "gy")
    near = exchange([own] * n_x, "gx")

    n_tiles = -(-3 * (rows // 8) // 16)
    strip = jax.ShapeDtypeStruct((n_tiles, depth, 8, LANES), f32)
    rim, *cols = pl.pallas_call(
        pack_columns,
        out_shape=(jax.ShapeDtypeStruct((2, 3, depth, HALO, width), f32), strip, strip),
        in_specs=[VMEM] * 3, out_specs=(VMEM,) * 3,
        compiler_params=params, name="pack_columns",
    )(own, *got)
    got = exchange(cols, "grp")
    near_rim = exchange([rim] * n_x, "gx")

    block = jax.ShapeDtypeStruct(source_term.shape, f32)
    total = layout(reflect, depth)[1]
    inside, ends = pl.pallas_call(
        functools.partial(interior, reflect, n_x),
        out_shape=(block, jax.ShapeDtypeStruct((3, total, rows, LANES), f32)),
        in_specs=[VMEM] * (2 + 2 * n_x), out_specs=(VMEM, VMEM), scratch_shapes=work(width),
        compiler_params=params, name="interior",
        cost_estimate=pl.CostEstimate(flops=20_000_000, bytes_accessed=20_000_000, transcendentals=0),
    )(own, rim, *near, *near_rim)
    inside, ends, got = lax.optimization_barrier((inside, ends, got))
    near_got = exchange([jnp.stack(got)] * n_x, "gx")
    return pl.pallas_call(
        functools.partial(edges, reflect, n_x),
        out_shape=block,
        in_specs=[VMEM] * (4 + n_x), out_specs=VMEM, scratch_shapes=work(LANES),
        compiler_params=params, name="edges",
    )(ends, inside, *got, *near_got)


def solution(mesh):
    spec = P("gx", "gy", "grp")
    return jax.shard_map(
        functools.partial(shards, dict(mesh.shape)),
        mesh=mesh,
        in_specs=(spec,) * 3,
        out_specs=spec,
        check_vma=False,
    )
```

```python
import functools

import jax
import jax.numpy as jnp
from jax import lax
from jax.experimental import pallas as pl
from jax.experimental.pallas import tpu as pltpu
from jax.sharding import PartitionSpec as P

ITERS = 2
HALO = 4 * ITERS
LANES = 128
KEEP = 48.0 / 41.0
SPREAD = 32.0 / 41.0
VMEM = pl.BlockSpec(memory_space=pltpu.VMEM)


def ahead(v, axis, n=1):
    return pltpu.roll(v, v.shape[axis] - n, axis)


def behind(v, axis, n=1):
    return pltpu.roll(v, n, axis)


def swaps(axis, sizes):
    count, fill = sizes[axis], sizes["gx"]
    over = [name for name in sizes if name in (axis, "gx")]
    filled = axis != "gx" and fill % 2 == 0

    def at(i, k):
        return i * fill + k if over[0] == axis else k * count + i

    rounds = []
    for start in (0, 1):
        pairs = [(i, i + 1) for i in range(start, count - 1, 2)]
        left = set(range(count)) - {i for pair in pairs for i in pair}
        if not pairs:
            continue
        if filled:
            pairs = [(at(i, k), at(j, k)) for i, j in pairs for k in range(fill)]
            pairs += [(at(i, k), at(i, k + 1)) for i in sorted(left) for k in range(0, fill, 2)]
        rounds.append(pairs + [(j, i) for i, j in pairs])
    return (tuple(over) if filled else axis), rounds


def is_odd(axis):
    return lax.rem(lax.axis_index(axis), 2)


def beyond(axis):
    at = lax.axis_index(axis)
    return at == 0, at == lax.axis_size(axis) - 1


def is_odd(axis):
    return lax.rem(lax.axis_index(axis), 2)


def pack_rows(own, first, second):
    odd = is_odd("gy")
    last = own.shape[2] - HALO
    first[...] = own[:, :, pl.ds(pl.multiple_of((1 - odd) * last, 8), HALO), :]
    second[...] = own[:, :, pl.ds(pl.multiple_of(odd * last, 8), HALO), :]


def slots(rows):
    return [(a, g, a * (rows // 8) + g) for a in range(3) for g in range(rows // 8)]


def pack_columns(own, got_a, got_b, rim, first, second):
    odd_y = is_odd("gy")
    odd_z = is_odd("grp")
    _, depth, inner, width = own.shape
    groups = inner // 8 + 2
    first_y, last_y = beyond("gy")
    lane = lax.broadcasted_iota(jnp.int32, (8, LANES), 1)

    def plane(p, carry):
        heads = [jnp.zeros((8, LANES), jnp.float32) for _ in range(first.shape[0])]
        tails = list(heads)
        for a, g, slot in slots(8 * groups):
            if g == 0 or g == groups - 1:
                from_a, from_b = got_a[a, p], got_b[a, p]
                low = g == 0
                strip = jnp.where(odd_y == (1 if low else 0), from_a, from_b)
                strip = jnp.where(first_y if low else last_y, 0.0, strip)
                rim[0 if g == 0 else 1, a, p] = strip
                head, tail = strip[:, 0:LANES], strip[:, width - LANES : width]
            else:
                head = own[a, p, 8 * g - 8 : 8 * g, 0:LANES]
                tail = own[a, p, 8 * g - 8 : 8 * g, width - LANES : width]
            at = 8 * (slot % 16)
            mine = (lane >= at) & (lane < at + HALO)
            head = pltpu.roll(head, at, 1)
            tail = pltpu.roll(tail, (at + HALO) % LANES, 1)
            heads[slot // 16] = jnp.where(mine, head, heads[slot // 16])
            tails[slot // 16] = jnp.where(mine, tail, tails[slot // 16])
        for t, (head, tail) in enumerate(zip(heads, tails)):
            first[t, p] = jnp.where(odd_z == 1, head, tail)
            second[t, p] = jnp.where(odd_z == 1, tail, head)
        return carry

    lax.fori_loop(0, depth, plane, 0)


def solve(cells, own_at, own, out):
    (src, cond, field, wx, wy, wz, vy, vz, diag, inv, sum8, cwx, cwy, cwz, cvy, cvz, cinv, res, q, cq, err) = cells
    total = cond.shape[0]
    rows, lanes = cond.shape[1:]

    def reach(halo):
        low = max(1, own_at - halo)
        high = min(total, own_at + own + halo)
        return (low + 1) // 2, (high + 1) // 2

    def sweep(halo, body):
        low, high = reach(halo)
        lax.fori_loop(low, high, lambda k, carry: body(k) or carry, 0, unroll=True)

    zero = jnp.zeros((rows, lanes), jnp.float32)
    for ref in (q, cq, err, sum8):
        ref[0] = zero

    def gather8(k):
        t = cond[2 * k - 1] + cond[2 * k]
        t = t + ahead(t, 0)
        sum8[k] = t + ahead(t, 1)

    sweep(HALO, gather8)

    def weights(c, below, above, step):
        x = c + above
        y, z = c + ahead(c, 0, step), c + ahead(c, 1, step)
        yb, zb = c + behind(c, 0, step), c + behind(c, 1, step)
        k = (c + below + x) + (y + yb) + (z + zb)
        return x, y, z, yb, zb, k, jnp.where(c > 0.0, 1.0 / k, 0.0)

    def setup(k):
        for p in (2 * k - 1, 2 * k):
            wx[p], wy[p], wz[p], vy[p], vz[p], diag[p], inv[p] = weights(cond[p], cond[p - 1], cond[p + 1], 1)
        cwx[k], cwy[k], cwz[k], cvy[k], cvz[k], _, cinv[k] = weights(sum8[k], sum8[k - 1], sum8[k + 1], 2)

    low, _ = reach(HALO - 2)
    wx[2 * low - 2] = cond[2 * low - 2] + cond[2 * low - 1]
    cwx[low - 1] = sum8[low - 1] + sum8[low]
    sweep(HALO - 2, setup)

    row = lax.broadcasted_iota(jnp.int32, (rows, lanes), 0)
    lane = lax.broadcasted_iota(jnp.int32, (rows, lanes), 1)
    even_row = lax.rem(row, 2) == 0
    even_lane = lax.rem(lane, 2) == 0

    def spread(v, p, x, y, z, yb, zb, step):
        here = v[p]
        n = x[p - 1] * v[p - 1] + x[p] * v[p + 1]
        n = n + (y[p] * ahead(here, 0, step) + yb[p] * behind(here, 0, step))
        return n + (z[p] * ahead(here, 1, step) + zb[p] * behind(here, 1, step))

    def image(v, p):
        return diag[p] * v[p] - spread(v, p, wx, wy, wz, vy, vz, 1)

    for it in range(ITERS):
        halo = 4 * (ITERS - 1 - it)

        def residuals(k, it=it):
            both = None
            for p in (2 * k - 1, 2 * k):
                if it == 0:
                    r = 2.0 * src[p] - image(field, p)
                else:
                    r = res[p] - image(err, p)
                if it < ITERS - 1:
                    res[p] = r
                q[p] = r * inv[p]
                both = r if both is None else both + r
            both = both + ahead(both, 0)
            both = both + ahead(both, 1)
            cq[k] = (4.0 * both) * cinv[k]

        sweep(halo + 2, residuals)

        def corrections(k, it=it):
            coarse = KEEP * cq[k] + SPREAD * (cinv[k] * spread(cq, k, cwx, cwy, cwz, cvy, cvz, 2))
            coarse = jnp.where(even_lane, coarse, behind(coarse, 1))
            coarse = jnp.where(even_row, coarse, behind(coarse, 0))
            for p in (2 * k - 1, 2 * k):
                e = KEEP * q[p] + SPREAD * (inv[p] * spread(q, p, wx, wy, wz, vy, vz, 1))
                e = e + coarse
                if it < ITERS - 1:
                    err[p] = err[p] + e if it else e
                else:
                    out(p, field[p] + (err[p] + e if it else e))

        sweep(halo, corrections)


def layout(reflect, depth):
    return (1, depth + HALO + 2) if reflect else (1 + HALO, depth + 2 * HALO + 2)


def each_plane(reflect, depth, place):
    odd_x = is_odd("gx")
    own_at, _ = layout(reflect, depth)

    def own_plane(p, carry):
        to = jnp.where(odd_x == 1, depth - 1 - p, p) if reflect else p
        place(None, p, own_at + to)
        return carry

    lax.fori_loop(0, depth, own_plane, 0, unroll=True)

    def near_plane(p, carry):
        if reflect:
            place(0, jnp.where(odd_x == 1, depth - 1 - p, p), own_at + depth + p)
            return carry
        for i in range(2):
            above = odd_x == i
            at = jnp.where(above, p, depth - HALO + p)
            place(i, at, jnp.where(above, own_at + depth + p, 1 + p))
        return carry

    lax.fori_loop(0, HALO, near_plane, 0, unroll=True)


def out_plane(reflect, depth, p):
    own_at, _ = layout(reflect, depth)
    at = p - own_at
    return jnp.where(is_odd("gx") == 1, depth - 1 - at, at) if reflect else at


def interior(reflect, n_x, *refs):
    own, rim = refs[0], refs[1]
    near, near_rim = refs[2 : 2 + n_x], refs[2 + n_x : 2 + 2 * n_x]
    result, ends = refs[2 + 2 * n_x : 4 + 2 * n_x]
    cells = refs[4 + 2 * n_x :]
    _, depth, inner, width = own.shape
    rows = inner + 2 * HALO
    lane = lax.broadcasted_iota(jnp.int32, (rows, LANES), 1)

    def place(i, p_from, p_to):
        block, halo = (own, rim) if i is None else (near[i], near_rim[i])
        for a in range(3):
            tile = cells[a]
            tile[p_to, 0:HALO, :] = halo[0, a, p_from]
            tile[p_to, HALO : HALO + inner, :] = block[a, p_from]
            tile[p_to, HALO + inner : rows, :] = halo[1, a, p_from]
            head = pltpu.roll(tile[p_to, :, 0:LANES], LANES // 2, 1)
            tail = tile[p_to, :, width - LANES : width]
            end = jnp.where((lane >= LANES // 2) & (lane < LANES // 2 + 2 * HALO), head, 0.0)
            ends[a, p_to] = jnp.where(lane >= LANES - 2 * HALO, tail, end)

    own_at, total = layout(reflect, depth)
    for a in range(3):
        for p in (0, total - 1):
            cells[a][p] = jnp.zeros((rows, width), jnp.float32)
            ends[a, p] = jnp.zeros((rows, LANES), jnp.float32)
    each_plane(reflect, depth, place)

    def out(p, v):
        result[out_plane(reflect, depth, p)] = v[HALO : rows - HALO, :]

    solve(cells, own_at, depth, out)


def edges(reflect, n_x, *refs):
    ends, inside, got_a, got_b = refs[:4]
    near_got = refs[4 : 4 + n_x]
    result = refs[4 + n_x]
    cells = refs[5 + n_x :]
    depth, inner, width = inside.shape
    rows = inner + 2 * HALO
    odd_z = is_odd("grp")
    first_z, last_z = beyond("grp")
    lane = lax.broadcasted_iota(jnp.int32, (8, LANES), 1)
    in_right = lane < HALO
    in_left = (lane >= LANES // 2 - HALO) & (lane < LANES // 2)

    def place(i, p_from, p_to):
        for t in range(got_a.shape[0]):
            if i is None:
                va, vb = got_a[t, p_from], got_b[t, p_from]
            else:
                va, vb = near_got[i][0, t, p_from], near_got[i][1, t, p_from]
            upper = jnp.where(last_z, 0.0, jnp.where(odd_z == 1, vb, va))
            lower = jnp.where(first_z, 0.0, jnp.where(odd_z == 1, va, vb))
            for a, g, slot in slots(rows):
                if slot // 16 == t:
                    at = 8 * (slot % 16)
                    right = pltpu.roll(upper, (LANES - at) % LANES, 1)
                    left = pltpu.roll(lower, (LANES + LANES // 2 - HALO - at) % LANES, 1)
                    tile = ends[a, p_to, 8 * g : 8 * g + 8, :]
                    tile = jnp.where(in_left, left, tile)
                    cells[a][p_to, 8 * g : 8 * g + 8, :] = jnp.where(in_right, right, tile)

    own_at, total = layout(reflect, depth)
    for a in range(3):
        for p in (0, total - 1):
            cells[a][p] = ends[a, p]
    each_plane(reflect, depth, place)
    result[...] = inside[...]
    wide = lax.broadcasted_iota(jnp.int32, (inner, LANES), 1)

    def out(p, v):
        at = out_plane(reflect, depth, p)
        v = v[HALO : rows - HALO, :]
        head = pltpu.roll(v, LANES // 2, 1)
        result[at, :, 0:LANES] = jnp.where(wide < HALO, head, result[at, :, 0:LANES])
        tail = result[at, :, width - LANES : width]
        result[at, :, width - LANES : width] = jnp.where(wide >= LANES - HALO, v, tail)

    solve(cells, own_at, depth, out)


def shards(sizes, source_term, conductivity, initial_field):
    depth, inner, width = source_term.shape
    rows = inner + 2 * HALO
    f32 = jnp.float32
    params = pltpu.CompilerParams(vmem_limit_bytes=48 * 1024 * 1024)
    args = (source_term, conductivity, initial_field)

    def exchange(values, axis):
        over, rounds = swaps(axis, sizes)
        found = [lax.ppermute(v, over, pairs) for v, pairs in reversed(list(zip(values, rounds)))]
        return found[::-1] + [jnp.zeros_like(v) for v in values[len(found) :]]

    def work(lanes):
        total = layout(reflect, depth)[1]
        fine = pltpu.VMEM((total, rows, lanes), f32)
        coarse = pltpu.VMEM((total // 2 + 1, rows, lanes), f32)
        return [fine] * 10 + [coarse] * 7 + [fine] * 2 + [coarse] + [fine]

    reflect = sizes["gx"] == 2
    n_x = 1 if reflect else 2
    face = jax.ShapeDtypeStruct((3, depth, HALO, width), f32)
    own = jnp.stack(args)
    msgs = pl.pallas_call(
        pack_rows, out_shape=(face, face), in_specs=[VMEM], out_specs=(VMEM, VMEM),
        compiler_params=params, name="pack_rows",
    )(own)
    got = exchange(msgs, "gy")
    near = exchange([own] * n_x, "gx")

    n_tiles = -(-3 * (rows // 8) // 16)
    strip = jax.ShapeDtypeStruct((n_tiles, depth, 8, LANES), f32)
    rim, *cols = pl.pallas_call(
        pack_columns,
        out_shape=(jax.ShapeDtypeStruct((2, 3, depth, HALO, width), f32), strip, strip),
        in_specs=[VMEM] * 3, out_specs=(VMEM,) * 3,
        compiler_params=params, name="pack_columns",
    )(own, *got)
    got = exchange(cols, "grp")
    near_rim = exchange([rim] * n_x, "gx")

    block = jax.ShapeDtypeStruct(source_term.shape, f32)
    total = layout(reflect, depth)[1]
    inside, ends = pl.pallas_call(
        functools.partial(interior, reflect, n_x),
        out_shape=(block, jax.ShapeDtypeStruct((3, total, rows, LANES), f32)),
        in_specs=[VMEM] * (2 + 2 * n_x), out_specs=(VMEM, VMEM), scratch_shapes=work(width),
        compiler_params=params, name="interior",
        cost_estimate=pl.CostEstimate(flops=20_000_000, bytes_accessed=20_000_000, transcendentals=0),
    )(own, rim, *near, *near_rim)
    inside, ends, got = lax.optimization_barrier((inside, ends, got))
    near_got = exchange([jnp.stack(got)] * n_x, "gx")
    return pl.pallas_call(
        functools.partial(edges, reflect, n_x),
        out_shape=block,
        in_specs=[VMEM] * (4 + n_x), out_specs=VMEM, scratch_shapes=work(LANES),
        compiler_params=params, name="edges",
    )(ends, inside, *got, *near_got)


def solution(mesh):
    spec = P("gx", "gy", "grp")
    return jax.shard_map(
        functools.partial(shards, dict(mesh.shape)),
        mesh=mesh,
        in_specs=(spec,) * 3,
        out_specs=spec,
        check_vma=False,
    )
```

```python
import functools

import jax
import jax.numpy as jnp
from jax import lax
from jax.experimental import pallas as pl
from jax.experimental.pallas import tpu as pltpu
from jax.sharding import PartitionSpec as P

ITERS = 2
HALO = 4 * ITERS
LANES = 128
KEEP = 48.0 / 41.0
SPREAD = 32.0 / 41.0
VMEM = pl.BlockSpec(memory_space=pltpu.VMEM)


def ahead(v, axis, n=1):
    return pltpu.roll(v, v.shape[axis] - n, axis)


def behind(v, axis, n=1):
    return pltpu.roll(v, n, axis)


def swaps(axis, sizes):
    count, fill = sizes[axis], sizes["gx"]
    over = [name for name in sizes if name in (axis, "gx")]
    filled = axis != "gx" and fill % 2 == 0

    def at(i, k):
        return i * fill + k if over[0] == axis else k * count + i

    rounds = []
    for start in (0, 1):
        pairs = [(i, i + 1) for i in range(start, count - 1, 2)]
        left = set(range(count)) - {i for pair in pairs for i in pair}
        if not pairs:
            continue
        if filled:
            pairs = [(at(i, k), at(j, k)) for i, j in pairs for k in range(fill)]
            pairs += [(at(i, k), at(i, k + 1)) for i in sorted(left) for k in range(0, fill, 2)]
        rounds.append(pairs + [(j, i) for i, j in pairs])
    return (tuple(over) if filled else axis), rounds


def is_odd(axis):
    return lax.rem(lax.axis_index(axis), 2)


def beyond(axis):
    at = lax.axis_index(axis)
    return at == 0, at == lax.axis_size(axis) - 1


def is_odd(axis):
    return lax.rem(lax.axis_index(axis), 2)


def pack_rows(own, first, second):
    odd = is_odd("gy")
    last = own.shape[2] - HALO
    first[...] = own[:, :, pl.ds(pl.multiple_of((1 - odd) * last, 8), HALO), :]
    second[...] = own[:, :, pl.ds(pl.multiple_of(odd * last, 8), HALO), :]


def slots(rows):
    return [(a, g, a * (rows // 8) + g) for a in range(3) for g in range(rows // 8)]


def pack_columns(own, got_a, got_b, strips, rim):
    odd_y, odd_z = is_odd("gy"), is_odd("grp")
    first_y, last_y = beyond("gy")
    _, depth, inner, width = own.shape
    groups = inner // 8 + 2
    lane = lax.broadcasted_iota(jnp.int32, (8, LANES), 1)
    for p in range(depth):
        for a in range(3):
            from_a, from_b = got_a[a, p], got_b[a, p]
            rim[0, a, p] = jnp.where(first_y, 0.0, jnp.where(odd_y == 1, from_a, from_b))
            rim[1, a, p] = jnp.where(last_y, 0.0, jnp.where(odd_y == 1, from_b, from_a))
        heads = [jnp.zeros((8, LANES), jnp.float32) for _ in range(strips.shape[1])]
        tails = list(heads)
        for a, g, slot in slots(8 * groups):
            t, at = slot // 16, 8 * (slot % 16)
            if g == 0 or g == groups - 1:
                rows = rim[min(g, 1), a, p]
            else:
                rows = own[a, p, 8 * g - 8 : 8 * g, :]
            head = pltpu.roll(rows[:, 0:LANES], at, 1)
            tail = pltpu.roll(rows[:, width - LANES : width], (at + LANES // 2) % LANES, 1)
            far = (at + LANES // 2 - HALO) % LANES
            heads[t] = jnp.where((lane >= at) & (lane < at + HALO), head, heads[t])
            tails[t] = jnp.where((lane >= far) & (lane < far + HALO), tail, tails[t])
        for t, (head, tail) in enumerate(zip(heads, tails)):
            strips[0, t, p] = jnp.where(odd_z == 1, head, tail)
            strips[1, t, p] = jnp.where(odd_z == 1, tail, head)


def shifts(parts, step):
    if parts == 1:
        return (lambda v: [ahead(v[0], 1, step)]), (lambda v: [behind(v[0], 1, step)])
    return (lambda v: [v[1], ahead(v[0], 1)]), (lambda v: [behind(v[1], 1), v[0]])


def each(op, *lists):
    return [op(*values) for values in zip(*lists)]


def add(*lists):
    return each(lambda *values: functools.reduce(lambda x, y: x + y, values), *lists)


def times(x, y):
    return each(lambda v, w: v * w, x, y)


def solve(cells, own_at, own, out):
    (src, cond, field, wx, wy, wz, vy, vz, diag, inv, sum8, cwx, cwy, cwz, cvy, cvz, cinv, res, q, cq, err) = cells
    total, parts, rows, lanes = cond.shape

    def load(ref, p):
        return [ref[p, i] for i in range(ref.shape[1])]

    def store(ref, p, values):
        for i, v in enumerate(values):
            ref[p, i] = v

    def reach(halo):
        low = max(1, own_at - halo)
        high = min(total, own_at + own + halo)
        return range((low + 1) // 2, (high + 1) // 2)

    fine = (1, *shifts(parts, 1))
    coarse = (2, *shifts(1, 3 - parts))
    zero = jnp.zeros((rows, lanes), jnp.float32)
    for ref in (q, cq, err, sum8):
        store(ref, 0, [zero] * ref.shape[1])

    def gather(v):
        t = v[0] + v[1] if parts == 2 else v[0] + ahead(v[0], 1)
        return [t + ahead(t, 0)]

    for k in reach(HALO):
        store(sum8, k, gather(add(load(cond, 2 * k - 1), load(cond, 2 * k))))

    def weights(ref, p, level):
        step, ahead_z, behind_z = level
        c = load(ref, p)
        x = add(c, load(ref, p + 1))
        y, yb = ([v + shift(v, 0, step) for v in c] for shift in (ahead, behind))
        z, zb = add(c, ahead_z(c)), add(c, behind_z(c))
        k = add(add(c, load(ref, p - 1), x), add(y, yb), add(z, zb))
        return x, y, z, yb, zb, k, each(lambda v, w: jnp.where(v > 0.0, 1.0 / w, 0.0), c, k)

    low = reach(HALO - 2).start
    store(wx, 2 * low - 2, add(load(cond, 2 * low - 2), load(cond, 2 * low - 1)))
    store(cwx, low - 1, add(load(sum8, low - 1), load(sum8, low)))
    for k in reach(HALO - 2):
        for p in (2 * k - 1, 2 * k):
            for ref, v in zip((wx, wy, wz, vy, vz, diag, inv), weights(cond, p, fine)):
                store(ref, p, v)
        for ref, v in zip((cwx, cwy, cwz, cvy, cvz, None, cinv), weights(sum8, k, coarse)):
            if ref is not None:
                store(ref, k, v)

    even_row = lax.rem(lax.broadcasted_iota(jnp.int32, (rows, lanes), 0), 2) == 0
    even_lane = lax.rem(lax.broadcasted_iota(jnp.int32, (rows, lanes), 1), 2) == 0

    def spread(v, p, refs, level):
        x, y, z, yb, zb = refs
        step, ahead_z, behind_z = level
        here = load(v, p)
        n = add(times(load(x, p - 1), load(v, p - 1)), times(load(x, p), load(v, p + 1)))
        n = add(n, times(load(y, p), [ahead(u, 0, step) for u in here]))
        n = add(n, times(load(yb, p), [behind(u, 0, step) for u in here]))
        return add(n, add(times(load(z, p), ahead_z(here)), times(load(zb, p), behind_z(here))))

    def smooth(v, p, refs, scale, level):
        n = times(load(scale, p), spread(v, p, refs, level))
        return each(lambda u, w: KEEP * u + SPREAD * w, load(v, p), n)

    around, coarse_around = (wx, wy, wz, vy, vz), (cwx, cwy, cwz, cvy, cvz)

    for it in range(ITERS):
        halo = 4 * (ITERS - 1 - it)
        for k in reach(halo + 2):
            found = []
            for p in (2 * k - 1, 2 * k):
                v = field if it == 0 else err
                start = [2.0 * u for u in load(src, p)] if it == 0 else load(res, p)
                n = spread(v, p, around, fine)
                r = each(lambda u, d, w, m: u - (d * w - m), start, load(diag, p), load(v, p), n)
                if it < ITERS - 1:
                    store(res, p, r)
                store(q, p, times(r, load(inv, p)))
                found.append(r)
            store(cq, k, times([4.0 * gather(add(*found))[0]], load(cinv, k)))

        for k in reach(halo):
            (c,) = smooth(cq, k, coarse_around, cinv, coarse)
            if parts == 1:
                c = jnp.where(even_lane, c, behind(c, 1))
            c = jnp.where(even_row, c, behind(c, 0))
            for p in (2 * k - 1, 2 * k):
                e = [u + c for u in smooth(q, p, around, inv, fine)]
                if it:
                    e = add(load(err, p), e)
                if it < ITERS - 1:
                    store(err, p, e)
                else:
                    out(p, add(load(field, p), e))


def layout(reflect, depth):
    return (1, depth + HALO + 2) if reflect else (1 + HALO, depth + 2 * HALO + 2)


def each_plane(reflect, depth, place):
    odd_x = is_odd("gx")
    own_at, _ = layout(reflect, depth)

    def own_plane(p, carry):
        to = jnp.where(odd_x == 1, depth - 1 - p, p) if reflect else p
        place(None, p, own_at + to)
        return carry

    lax.fori_loop(0, depth, own_plane, 0, unroll=True)

    def near_plane(p, carry):
        if reflect:
            place(0, jnp.where(odd_x == 1, depth - 1 - p, p), own_at + depth + p)
            return carry
        for i in range(2):
            above = odd_x == i
            at = jnp.where(above, p, depth - HALO + p)
            place(i, at, jnp.where(above, own_at + depth + p, 1 + p))
        return carry

    lax.fori_loop(0, HALO, near_plane, 0, unroll=True)


def out_plane(reflect, depth, p):
    own_at, _ = layout(reflect, depth)
    at = p - own_at
    return jnp.where(is_odd("gx") == 1, depth - 1 - at, at) if reflect else at


def parting(width, lanes):
    column = lax.broadcasted_iota(jnp.int32, (width, 2 * lanes), 0)
    lane = lax.broadcasted_iota(jnp.int32, (width, 2 * lanes), 1)
    wanted = jnp.where(lane < lanes, 2 * lane, 2 * (lane - lanes) + 1)
    return jnp.where((column == wanted) & (wanted < width), 1.0, 0.0)


def rearranged(v, matrix):
    bf16, f32 = jnp.bfloat16, jnp.float32
    matrix = matrix.astype(bf16)
    result = None
    for _ in range(3):
        part = v.astype(bf16)
        v = v - part.astype(f32)
        moved = jnp.dot(part, matrix, preferred_element_type=f32)
        result = moved if result is None else result + moved
    return result


def interior(reflect, n_x, *refs):
    own, rim = refs[0], refs[1]
    near, near_rim = refs[2 : 2 + n_x], refs[2 + n_x : 2 + 2 * n_x]
    result, ends = refs[2 + 2 * n_x : 4 + 2 * n_x]
    whole, halves, *cells = refs[4 + 2 * n_x :]
    _, depth, inner, width = own.shape
    rows = inner + 2 * HALO
    lanes = cells[0].shape[3]
    lane = lax.broadcasted_iota(jnp.int32, (rows, LANES), 1)

    def place(i, p_from, p_to):
        block, halo = (own, rim) if i is None else (near[i], near_rim[i])
        for a in range(3):
            tile = whole.at[a, p_to]
            tile[0:HALO, :] = halo[0, a, p_from]
            tile[HALO : HALO + inner, :] = block[a, p_from]
            tile[HALO + inner : rows, :] = halo[1, a, p_from]
            head = pltpu.roll(tile[:, 0:LANES], LANES // 2, 1)
            tail = tile[:, width - LANES : width]
            end = jnp.where((lane >= LANES // 2) & (lane < LANES // 2 + 2 * HALO), head, 0.0)
            ends[a, p_to] = jnp.where(lane >= LANES - 2 * HALO, tail, end)

    own_at, total = layout(reflect, depth)
    for a in range(3):
        for p in (0, total - 1):
            whole[a, p] = jnp.zeros((rows, width), jnp.float32)
            ends[a, p] = jnp.zeros((rows, LANES), jnp.float32)
    each_plane(reflect, depth, place)
    apart = parting(width, lanes)
    for a in range(3):
        parts = rearranged(whole[a].reshape(total * rows, width), apart)
        for i in range(2):
            cells[a][:, i] = parts[:, i * lanes : (i + 1) * lanes].reshape(total, rows, lanes)

    def out(p, v):
        for i in range(2):
            halves[p - own_at, :, i * lanes : (i + 1) * lanes] = v[i][HALO : rows - HALO, :]

    solve(cells, own_at, depth, out)
    together = rearranged(halves[...].reshape(depth * inner, 2 * lanes), apart.T)
    together = together.reshape(depth, inner, width)
    for p in range(depth):
        result[out_plane(reflect, depth, own_at + p)] = together[p]


def edges(reflect, ends, inside, got_a, got_b, result, *cells):
    depth, inner, width = inside.shape
    rows = inner + 2 * HALO
    odd_z = is_odd("grp")
    first_z, last_z = beyond("grp")
    lane = lax.broadcasted_iota(jnp.int32, (8, LANES), 1)
    in_halo = (lane < HALO) | ((lane >= LANES // 2 - HALO) & (lane < LANES // 2))
    own_at, total = layout(reflect, depth)
    for p in (0, total - 1):
        for a in range(3):
            cells[a][p, 0] = ends[a, p]

    def place(i, p_from, p_to):
        at_plane = p_from if i is None else (i + 1) * depth + p_from
        for t in range(got_a.shape[0]):
            va, vb = got_a[t, at_plane], got_b[t, at_plane]
            upper = jnp.where(last_z, 0.0, jnp.where(odd_z == 1, vb, va))
            lower = jnp.where(first_z, 0.0, jnp.where(odd_z == 1, va, vb))
            for a, g, slot in slots(rows):
                if slot // 16 == t:
                    at = 8 * (slot % 16)
                    both = jnp.where((lane >= at) & (lane < at + HALO), upper, lower)
                    both = pltpu.roll(both, (LANES - at) % LANES, 1)
                    part = slice(8 * g, 8 * g + 8)
                    cells[a][p_to, 0, part, :] = jnp.where(in_halo, both, ends[a, p_to, part, :])

    each_plane(reflect, depth, place)
    result[...] = inside[...]
    wide = lax.broadcasted_iota(jnp.int32, (inner, LANES), 1)

    def out(p, v):
        at = out_plane(reflect, depth, p)
        v = v[0][HALO : rows - HALO, :]
        head = pltpu.roll(v, LANES // 2, 1)
        result[at, :, 0:LANES] = jnp.where(wide < HALO, head, result[at, :, 0:LANES])
        tail = result[at, :, width - LANES : width]
        result[at, :, width - LANES : width] = jnp.where(wide >= LANES - HALO, v, tail)

    solve(cells, own_at, depth, out)


def shards(sizes, source_term, conductivity, initial_field):
    depth, inner, width = source_term.shape
    rows = inner + 2 * HALO
    f32 = jnp.float32
    params = pltpu.CompilerParams(vmem_limit_bytes=48 * 1024 * 1024)
    args = (source_term, conductivity, initial_field)

    def exchange(values, axis):
        over, rounds = swaps(axis, sizes)
        found = [lax.ppermute(v, over, pairs) for v, pairs in reversed(list(zip(values, rounds)))]
        return found[::-1] + [jnp.zeros_like(v) for v in values[len(found) :]]

    def work(parts, lanes):
        total = layout(reflect, depth)[1]
        fine = pltpu.VMEM((total, parts, rows, lanes), f32)
        coarse = pltpu.VMEM((total // 2 + 1, 1, rows, lanes), f32)
        return [fine] * 10 + [coarse] * 7 + [fine] * 2 + [coarse] + [fine]

    reflect = sizes["gx"] == 2
    n_x = 1 if reflect else 2
    face = jax.ShapeDtypeStruct((3, depth, HALO, width), f32)
    own = jnp.stack(args)
    msgs = pl.pallas_call(
        pack_rows, out_shape=(face, face), in_specs=[VMEM], out_specs=(VMEM, VMEM),
        compiler_params=params, name="pack_rows",
    )(own)
    got = exchange(msgs, "gy")
    near = exchange([own] * n_x, "gx")
    n_tiles = -(-3 * (rows // 8) // 16)
    strips, rim = pl.pallas_call(
        pack_columns,
        out_shape=(
            jax.ShapeDtypeStruct((2, n_tiles, depth, 8, LANES), f32),
            jax.ShapeDtypeStruct((2, 3, depth, HALO, width), f32),
        ),
        in_specs=[VMEM] * 3, out_specs=(VMEM, VMEM),
        compiler_params=params, name="pack_columns",
    )(own, *got)
    strips = jnp.concatenate([strips] + exchange([strips] * n_x, "gx"), axis=2)
    strips, rim = lax.optimization_barrier((strips, rim))
    near_rim = exchange([rim] * n_x, "gx")
    strips = exchange([strips[0], strips[1]], "grp")

    block = jax.ShapeDtypeStruct(source_term.shape, f32)
    total = layout(reflect, depth)[1]
    lanes = -(-width // (2 * LANES)) * LANES
    apart = [pltpu.VMEM((3, total, rows, width), f32), pltpu.VMEM((depth, inner, 2 * lanes), f32)]
    inside, ends = pl.pallas_call(
        functools.partial(interior, reflect, n_x),
        out_shape=(block, jax.ShapeDtypeStruct((3, total, rows, LANES), f32)),
        in_specs=[VMEM] * (2 + 2 * n_x), out_specs=(VMEM, VMEM), scratch_shapes=apart + work(2, lanes),
        compiler_params=params, name="interior",
        cost_estimate=pl.CostEstimate(flops=20_000_000, bytes_accessed=20_000_000, transcendentals=0),
    )(own, rim, *near, *near_rim)
    inside, ends, *strips = lax.optimization_barrier((inside, ends, *strips[::-1]))
    strips = strips[::-1]
    return pl.pallas_call(
        functools.partial(edges, reflect),
        out_shape=block,
        in_specs=[VMEM] * 4, out_specs=VMEM, scratch_shapes=work(1, LANES),
        compiler_params=params, name="edges",
    )(ends, inside, *strips)


def solution(mesh):
    spec = P("gx", "gy", "grp")
    return jax.shard_map(
        functools.partial(shards, dict(mesh.shape)),
        mesh=mesh,
        in_specs=(spec,) * 3,
        out_specs=spec,
        check_vma=False,
    )
```

```python
import functools

import jax
import jax.numpy as jnp
from jax import lax
from jax.experimental import pallas as pl
from jax.experimental.pallas import tpu as pltpu
from jax.sharding import PartitionSpec as P

ITERS = 2
HALO = 4 * ITERS
LANES = 128
KEEP = 48.0 / 41.0
SPREAD = 32.0 / 41.0
VMEM = pl.BlockSpec(memory_space=pltpu.VMEM)


def ahead(v, axis, n=1):
    return pltpu.roll(v, v.shape[axis] - n, axis)


def behind(v, axis, n=1):
    return pltpu.roll(v, n, axis)


def swaps(axis, sizes):
    count, fill = sizes[axis], sizes["gx"]
    over = [name for name in sizes if name in (axis, "gx")]
    filled = axis != "gx" and fill % 2 == 0

    def at(i, k):
        return i * fill + k if over[0] == axis else k * count + i

    rounds = []
    for start in (0, 1):
        pairs = [(i, i + 1) for i in range(start, count - 1, 2)]
        left = set(range(count)) - {i for pair in pairs for i in pair}
        if not pairs:
            continue
        if filled:
            pairs = [(at(i, k), at(j, k)) for i, j in pairs for k in range(fill)]
            pairs += [(at(i, k), at(i, k + 1)) for i in sorted(left) for k in range(0, fill, 2)]
        rounds.append(pairs + [(j, i) for i, j in pairs])
    return (tuple(over) if filled else axis), rounds


def is_odd(axis):
    return lax.rem(lax.axis_index(axis), 2)


def beyond(axis):
    at = lax.axis_index(axis)
    return at == 0, at == lax.axis_size(axis) - 1


def is_odd(axis):
    return lax.rem(lax.axis_index(axis), 2)


def fetch(copies, sems):
    copies = [pltpu.make_async_copy(src, dst, sems.at[i]) for i, (src, dst) in enumerate(copies)]
    for copy in copies:
        copy.start()
    for copy in copies:
        copy.wait()


def pack_rows(s, c, f, first, second, sems):
    odd = is_odd("gy")
    last = s.shape[1] - HALO
    rows = [pl.ds(pl.multiple_of(at * last, 8), HALO) for at in (1 - odd, odd)]
    fetch(
        [(ref.at[:, part, :], dst.at[a]) for part, dst in zip(rows, (first, second)) for a, ref in enumerate((s, c, f))],
        sems,
    )


def pack_block(s, c, f, own, sems):
    fetch([(ref, own.at[a]) for a, ref in enumerate((s, c, f))], sems)


def head_lane(a, g):
    return 16 * a + LANES // 2 * (g % 2) + 8 * (g // 2)


def tail_lane(a, g):
    return 16 * a + LANES // 2 * (g % 2) + 8 * (1 - g // 2)


def pack_columns(own, got_a, got_b, strips, rim):
    odd_y, odd_z = is_odd("gy"), is_odd("grp")
    first_y, last_y = beyond("gy")
    _, depth, inner, width = own.shape
    groups = inner // 8 + 2
    lane = lax.broadcasted_iota(jnp.int32, (8, LANES), 1)
    for p in range(depth):
        for a in range(3):
            from_a, from_b = got_a[a, p], got_b[a, p]
            rim[0, a, p] = jnp.where(first_y, 0.0, jnp.where(odd_y == 1, from_a, from_b))
            rim[1, a, p] = jnp.where(last_y, 0.0, jnp.where(odd_y == 1, from_b, from_a))
        head = tail = jnp.zeros((8, LANES), jnp.float32)
        for a in range(3):
            for g in range(groups):
                if g == 0 or g == groups - 1:
                    rows = rim[min(g, 1), a, p]
                else:
                    rows = own[a, p, 8 * g - 8 : 8 * g, :]
                to = head_lane(a, g)
                moved = pltpu.roll(rows[:, 0:LANES], to, 1)
                head = jnp.where((lane >= to) & (lane < to + HALO), moved, head)
                to = tail_lane(a, g)
                moved = pltpu.roll(rows[:, width - LANES : width], (to + HALO) % LANES, 1)
                tail = jnp.where((lane >= to) & (lane < to + HALO), moved, tail)
        strips[0, p] = jnp.where(odd_z == 1, head, tail)
        strips[1, p] = jnp.where(odd_z == 1, tail, head)


def shifts(parts, step):
    if parts == 1:
        return (lambda v: [ahead(v[0], 1, step)]), (lambda v: [behind(v[0], 1, step)])
    return (lambda v: [v[1], ahead(v[0], 1)]), (lambda v: [behind(v[1], 1), v[0]])


def each(op, *lists):
    return [op(*values) for values in zip(*lists)]


def add(*lists):
    return each(lambda *values: functools.reduce(lambda x, y: x + y, values), *lists)


def times(x, y):
    return each(lambda v, w: v * w, x, y)


def solve(cells, own_at, own, out):
    (src, cond, field, wx, wy, wz, vy, vz, diag, inv, sum8, cwx, cwy, cwz, cvy, cvz, cinv, res, q, cq, err) = cells
    total, parts, rows, lanes = cond.shape

    def load(ref, p):
        return [ref[p, i] for i in range(ref.shape[1])]

    def store(ref, p, values):
        for i, v in enumerate(values):
            ref[p, i] = v

    def reach(halo):
        low = max(1, own_at - halo)
        high = min(total, own_at + own + halo)
        return range((low + 1) // 2, (high + 1) // 2)

    fine = (1, *shifts(parts, 1))
    coarse = (2, *shifts(1, 3 - parts))
    zero = jnp.zeros((rows, lanes), jnp.float32)
    for ref in (q, cq, err, sum8):
        store(ref, 0, [zero] * ref.shape[1])

    even_row = lax.rem(lax.broadcasted_iota(jnp.int32, (rows, lanes), 0), 2) == 0
    even_lane = lax.rem(lax.broadcasted_iota(jnp.int32, (rows, lanes), 1), 2) == 0

    def gather(v):
        other = v[1] if parts == 2 else jnp.where(even_lane, ahead(v[0], 1), behind(v[0], 1))
        t = v[0] + other
        return [t + ahead(t, 0)]

    for k in reach(HALO):
        store(sum8, k, gather(add(load(cond, 2 * k - 1), load(cond, 2 * k))))

    def weights(ref, p, level):
        step, ahead_z, behind_z = level
        c = load(ref, p)
        x = add(c, load(ref, p + 1))
        y, yb = ([v + shift(v, 0, step) for v in c] for shift in (ahead, behind))
        z, zb = add(c, ahead_z(c)), add(c, behind_z(c))
        k = add(add(c, load(ref, p - 1), x), add(y, yb), add(z, zb))
        return x, y, z, yb, zb, k, each(lambda v, w: jnp.where(v > 0.0, 1.0 / w, 0.0), c, k)

    low = reach(HALO - 2).start
    store(wx, 2 * low - 2, add(load(cond, 2 * low - 2), load(cond, 2 * low - 1)))
    store(cwx, low - 1, add(load(sum8, low - 1), load(sum8, low)))
    for k in reach(HALO - 2):
        for p in (2 * k - 1, 2 * k):
            for ref, v in zip((wx, wy, wz, vy, vz, diag, inv), weights(cond, p, fine)):
                store(ref, p, v)
        for ref, v in zip((cwx, cwy, cwz, cvy, cvz, None, cinv), weights(sum8, k, coarse)):
            if ref is not None:
                store(ref, k, v)

    def spread(v, p, refs, level):
        x, y, z, yb, zb = refs
        step, ahead_z, behind_z = level
        here = load(v, p)
        n = add(times(load(x, p - 1), load(v, p - 1)), times(load(x, p), load(v, p + 1)))
        n = add(n, times(load(y, p), [ahead(u, 0, step) for u in here]))
        n = add(n, times(load(yb, p), [behind(u, 0, step) for u in here]))
        return add(n, add(times(load(z, p), ahead_z(here)), times(load(zb, p), behind_z(here))))

    def smooth(v, p, refs, scale, level):
        n = times(load(scale, p), spread(v, p, refs, level))
        return each(lambda u, w: KEEP * u + SPREAD * w, load(v, p), n)

    around, coarse_around = (wx, wy, wz, vy, vz), (cwx, cwy, cwz, cvy, cvz)

    for it in range(ITERS):
        halo = 4 * (ITERS - 1 - it)
        for k in reach(halo + 2):
            found = []
            for p in (2 * k - 1, 2 * k):
                v = field if it == 0 else err
                start = [2.0 * u for u in load(src, p)] if it == 0 else load(res, p)
                n = spread(v, p, around, fine)
                r = each(lambda u, d, w, m: u - (d * w - m), start, load(diag, p), load(v, p), n)
                if it < ITERS - 1:
                    store(res, p, r)
                store(q, p, times(r, load(inv, p)))
                found.append(r)
            store(cq, k, times([4.0 * gather(add(*found))[0]], load(cinv, k)))

        for k in reach(halo):
            (c,) = smooth(cq, k, coarse_around, cinv, coarse)
            c = jnp.where(even_row, c, behind(c, 0))
            for p in (2 * k - 1, 2 * k):
                e = [u + c for u in smooth(q, p, around, inv, fine)]
                if it:
                    e = add(load(err, p), e)
                if it < ITERS - 1:
                    store(err, p, e)
                else:
                    out(p, add(load(field, p), e))


def layout(reflect, depth):
    return (1, depth + HALO + 2) if reflect else (1 + HALO, depth + 2 * HALO + 2)


def each_plane(reflect, depth, place):
    odd_x = is_odd("gx")
    own_at, _ = layout(reflect, depth)

    for p in range(depth):
        place(None, jnp.where(odd_x == 1, depth - 1 - p, p) if reflect else p, own_at + p)
    for p in range(HALO):
        if reflect:
            place(0, jnp.where(odd_x == 1, depth - 1 - p, p), own_at + depth + p)
            continue
        for i in range(2):
            above = odd_x == i
            at = jnp.where(above, p, depth - HALO + p)
            place(i, at, jnp.where(above, own_at + depth + p, 1 + p))


def out_plane(reflect, depth, p):
    own_at, _ = layout(reflect, depth)
    at = p - own_at
    return jnp.where(is_odd("gx") == 1, depth - 1 - at, at) if reflect else at


def parting(width, lanes):
    column = lax.broadcasted_iota(jnp.int32, (width, 2 * lanes), 0)
    lane = lax.broadcasted_iota(jnp.int32, (width, 2 * lanes), 1)
    wanted = jnp.where(lane < lanes, 2 * lane, 2 * (lane - lanes) + 1)
    return jnp.where((column == wanted) & (wanted < width), 1.0, 0.0)


def ending(width):
    column = lax.broadcasted_iota(jnp.int32, (width, 2 * LANES), 0)
    lane = lax.broadcasted_iota(jnp.int32, (width, 2 * LANES), 1)
    lane = jnp.where(lane < LANES, lane, lane - LANES - LANES // 2)
    last = (lane >= 8) & (lane < 24) & (column == lane + width - 24)
    first = (lane >= 40) & (lane < 56) & (column == lane - 40)
    return jnp.where(last | first, 1.0, 0.0)


def rearranged(v, matrix):
    bf16, f32 = jnp.bfloat16, jnp.float32
    matrix = matrix.astype(bf16)
    result = None
    for _ in range(3):
        part = v.astype(bf16)
        v = v - part.astype(f32)
        moved = jnp.dot(part, matrix, preferred_element_type=f32)
        result = moved if result is None else result + moved
    return result


def interior(reflect, n_x, *refs):
    own, rim = refs[0], refs[1]
    near, near_rim = refs[2 : 2 + n_x], refs[2 + n_x : 2 + 2 * n_x]
    result, ends = refs[2 + 2 * n_x : 4 + 2 * n_x]
    whole, halves, *cells = refs[4 + 2 * n_x :]
    _, depth, inner, width = own.shape
    rows = inner + 2 * HALO
    lanes = cells[0].shape[3]

    def place(i, p_from, p_to):
        block, halo = (own, rim) if i is None else (near[i], near_rim[i])
        for a in range(3):
            tile = whole.at[a, p_to]
            tile[0:HALO, :] = halo[0, a, p_from]
            tile[HALO : HALO + inner, :] = block[a, p_from]
            tile[HALO + inner : rows, :] = halo[1, a, p_from]

    own_at, total = layout(reflect, depth)
    for a in range(3):
        for p in (0, total - 1):
            whole[a, p] = jnp.zeros((rows, width), jnp.float32)
    each_plane(reflect, depth, place)
    apart = parting(width, lanes)
    target = jnp.concatenate([apart, ending(width)], 1)
    for a in range(3):
        parts = rearranged(whole[a].reshape(total * rows, width), target).reshape(total, rows, -1)
        for i in range(2):
            cells[a][:, i] = parts[:, :, i * lanes : (i + 1) * lanes]
        low = parts[:, 0 : rows - 8, 2 * lanes : 2 * lanes + LANES]
        ends[a] = low + parts[:, 8:rows, 2 * lanes + LANES :]

    def out(p, v):
        for i in range(2):
            halves[p - own_at, :, i * lanes : (i + 1) * lanes] = v[i][HALO : rows - HALO, :]

    solve(cells, own_at, depth, out)
    together = rearranged(halves[...].reshape(depth * inner, 2 * lanes), apart.T)
    together = together.reshape(depth, inner, width)
    for p in range(depth):
        result[out_plane(reflect, depth, own_at + p)] = together[p]


def edges(reflect, ends, inside, got_a, got_b, result, *cells):
    depth, inner, width = inside.shape
    groups = ends.shape[2] // 8
    odd_z = is_odd("grp")
    first_z, last_z = beyond("grp")
    lane = lax.broadcasted_iota(jnp.int32, (8, LANES), 1)
    half = LANES // 2
    own_at, total = layout(reflect, depth)
    for p in (0, total - 1):
        for a in range(3):
            cells[a][p, 0] = ends[a, p]

    def place(i, p_from, p_to):
        at_plane = p_from if i is None else (i + 1) * depth + p_from
        va, vb = got_a[at_plane], got_b[at_plane]
        right = jnp.where(last_z, 0.0, jnp.where(odd_z == 1, vb, va))
        left = jnp.where(first_z, 0.0, jnp.where(odd_z == 1, va, vb))
        side = lax.rem(lane, 16) < 8
        lower = jnp.where(side, right, left)
        upper = jnp.where(side, pltpu.roll(right, LANES - 8, 1), pltpu.roll(left, 8, 1))
        middle = jnp.where(lane < half, upper, lower)
        for a in range(3):
            for t, (groups_of, shift) in enumerate(((lower, 24), (middle, 24 + half), (upper, 24))):
                moved = pltpu.roll(groups_of, (shift - 16 * a) % LANES, 1)
                here = lax.rem(lane, half)
                part = slice(8 * t, 8 * t + 8)
                cells[a][p_to, 0, part, :] = jnp.where((here >= 24) & (here < 40), moved, ends[a, p_to, part, :])

    each_plane(reflect, depth, place)

    def out(p, v):
        at = out_plane(reflect, depth, p)
        v = v[0][8:16]
        for i in range(2):
            part = slice(8 * i, 8 * i + 8)
            head = pltpu.roll(v, (LANES - 40 - half * i) % LANES, 1)
            tail = pltpu.roll(v, (LANES - 24 - half * i) % LANES, 1)
            for c in range(0, width, LANES):
                tile = inside[at, part, c : c + LANES]
                if c == 0:
                    tile = jnp.where(lane < HALO, head, tile)
                if c == width - LANES:
                    tile = jnp.where(lane >= LANES - HALO, tail, tile)
                result[at, part, c : c + LANES] = tile

    solve(cells, own_at, depth, out)


def shards(sizes, source_term, conductivity, initial_field):
    depth, inner, width = source_term.shape
    assert inner == 16 and depth >= HALO and depth % 2 == 0 and width % LANES == 0
    rows = inner + 2 * HALO
    f32 = jnp.float32
    params = pltpu.CompilerParams(vmem_limit_bytes=48 * 1024 * 1024)
    args = (source_term, conductivity, initial_field)

    def exchange(values, axis):
        over, rounds = swaps(axis, sizes)
        found = [lax.ppermute(v, over, pairs) for v, pairs in reversed(list(zip(values, rounds)))]
        return found[::-1] + [jnp.zeros_like(v) for v in values[len(found) :]]

    def work(parts, rows, lanes):
        total = layout(reflect, depth)[1]
        fine = pltpu.VMEM((total, parts, rows, lanes), f32)
        coarse = pltpu.VMEM((total // 2 + 1, 1, rows, lanes), f32)
        return [fine] * 10 + [coarse] * 7 + [fine] * 2 + [coarse] + [fine]

    reflect = sizes["gx"] == 2
    n_x = 1 if reflect else 2
    face = jax.ShapeDtypeStruct((3, depth, HALO, width), f32)
    args = [pltpu.with_memory_space_constraint(v, pltpu.HBM) for v in args]
    hbm = [pl.BlockSpec(memory_space=pltpu.HBM)] * 3
    msgs = pl.pallas_call(
        pack_rows, out_shape=(face, face), in_specs=hbm, out_specs=(VMEM, VMEM),
        scratch_shapes=[pltpu.SemaphoreType.DMA((6,))], compiler_params=params, name="pack_rows",
    )(*args)
    own = pl.pallas_call(
        pack_block, out_shape=jax.ShapeDtypeStruct((3, depth, inner, width), f32), in_specs=hbm, out_specs=VMEM,
        scratch_shapes=[pltpu.SemaphoreType.DMA((3,))], compiler_params=params, name="pack_block",
        cost_estimate=pl.CostEstimate(flops=0, bytes_accessed=2_000_000, transcendentals=0),
    )(*args)
    got = exchange(msgs, "gy")
    near = exchange([own] * n_x, "gx")
    strips, rim = pl.pallas_call(
        pack_columns,
        out_shape=(
            jax.ShapeDtypeStruct((2, depth, 8, LANES), f32),
            jax.ShapeDtypeStruct((2, 3, depth, HALO, width), f32),
        ),
        in_specs=[VMEM] * 3, out_specs=(VMEM, VMEM),
        compiler_params=params, name="pack_columns",
    )(own, *got)
    strips = jnp.concatenate([strips] + exchange([strips] * n_x, "gx"), axis=1)
    strips, rim = lax.optimization_barrier((strips, rim))
    near_rim = exchange([rim] * n_x, "gx")
    strips = exchange([strips[0], strips[1]], "grp")

    block = jax.ShapeDtypeStruct(source_term.shape, f32)
    total = layout(reflect, depth)[1]
    lanes = -(-width // (2 * LANES)) * LANES
    apart = [pltpu.VMEM((3, total, rows, width), f32), pltpu.VMEM((depth, inner, 2 * lanes), f32)]
    inside, ends = pl.pallas_call(
        functools.partial(interior, reflect, n_x),
        out_shape=(block, jax.ShapeDtypeStruct((3, total, rows - 8, LANES), f32)),
        in_specs=[VMEM] * (2 + 2 * n_x), out_specs=(VMEM, VMEM), scratch_shapes=apart + work(2, rows, lanes),
        compiler_params=params, name="interior",
        cost_estimate=pl.CostEstimate(flops=20_000_000, bytes_accessed=20_000_000, transcendentals=0),
    )(own, rim, *near, *near_rim)
    inside, ends, *strips = lax.optimization_barrier((inside, ends, *strips[::-1]))
    strips = strips[::-1]
    return pl.pallas_call(
        functools.partial(edges, reflect),
        out_shape=block,
        in_specs=[VMEM] * 4, out_specs=VMEM, scratch_shapes=work(1, rows - 8, LANES),
        compiler_params=params, name="edges",
    )(ends, inside, *strips)


def solution(mesh):
    spec = P("gx", "gy", "grp")
    return jax.shard_map(
        functools.partial(shards, dict(mesh.shape)),
        mesh=mesh,
        in_specs=(spec,) * 3,
        out_specs=spec,
        check_vma=False,
    )
```

```python
import functools

import jax
import jax.numpy as jnp
from jax import lax
from jax.experimental import pallas as pl
from jax.experimental.pallas import tpu as pltpu
from jax.sharding import PartitionSpec as P

ITERS = 2
HALO = 4 * ITERS
LANES = 128
KEEP = 48.0 / 41.0
SPREAD = 32.0 / 41.0
VMEM = pl.BlockSpec(memory_space=pltpu.VMEM)


def ahead(v, axis, n=1):
    return pltpu.roll(v, v.shape[axis] - n, axis)


def behind(v, axis, n=1):
    return pltpu.roll(v, n, axis)


def swaps(axis, sizes):
    count, fill = sizes[axis], sizes["gx"]
    over = [name for name in sizes if name in (axis, "gx")]
    filled = axis != "gx" and fill % 2 == 0

    def at(i, k):
        return i * fill + k if over[0] == axis else k * count + i

    rounds = []
    for start in (0, 1):
        pairs = [(i, i + 1) for i in range(start, count - 1, 2)]
        left = set(range(count)) - {i for pair in pairs for i in pair}
        if not pairs:
            continue
        if filled:
            pairs = [(at(i, k), at(j, k)) for i, j in pairs for k in range(fill)]
            pairs += [(at(i, k), at(i, k + 1)) for i in sorted(left) for k in range(0, fill, 2)]
        rounds.append(pairs + [(j, i) for i, j in pairs])
    return (tuple(over) if filled else axis), rounds


def is_odd(axis):
    return lax.rem(lax.axis_index(axis), 2)


def beyond(axis):
    at = lax.axis_index(axis)
    return at == 0, at == lax.axis_size(axis) - 1


def is_odd(axis):
    return lax.rem(lax.axis_index(axis), 2)


def prepare(reflect, s, c, f, own, first, second, sems):
    copies = [pltpu.make_async_copy(ref, own.at[a], sems.at[a]) for a, ref in enumerate((s, c, f))]
    for copy in copies:
        copy.start()
    for copy in copies:
        copy.wait()
    _, depth, inner, width = own.shape
    row = lax.broadcasted_iota(jnp.int32, (inner, width), 0)
    column = lax.broadcasted_iota(jnp.int32, (inner, width), 1)
    outer = jnp.where(is_odd("gx") == 1, depth - 1, 0)
    for p in range(depth):
        cond, field = own[1, p], own[2, p]

        def flux(shift, axis):
            return (cond + shift(cond, axis)) * (field - shift(field, axis))

        total = jnp.where(row < inner - 1, flux(ahead, 0), 0.0) + jnp.where(row > 0, flux(behind, 0), 0.0)
        total += jnp.where(column < width - 1, flux(ahead, 1), 0.0) + jnp.where(column > 0, flux(behind, 1), 0.0)
        for other in (p - 1, p + 1):
            if 0 <= other < depth:
                total += (cond + own[1, other]) * (field - own[2, other])
        if reflect and p in (0, depth - 1):
            total += jnp.where(outer == p, cond * field, 0.0)
        own[0, p] = 2.0 * own[0, p] - total

    odd = is_odd("gy")
    row = lax.broadcasted_iota(jnp.int32, (HALO, width), 0)
    lane = lax.broadcasted_iota(jnp.int32, (HALO, LANES), 1)
    for message, high in ((first, odd == 0), (second, odd == 1)):
        rows = pl.ds(pl.multiple_of(jnp.where(high, inner - HALO, 0), 8), HALO)
        sides = jnp.zeros((HALO, LANES), jnp.float32)
        for p in range(depth):
            field = own[2, p, rows, :]
            below = jnp.where(row == HALO - 1, pltpu.roll(field, HALO - 1, 0), own[0, p, rows, :])
            above = jnp.where(row == 0, pltpu.roll(field, 1, 0), own[0, p, rows, :])
            message[p] = jnp.where(high, above, below)
            message[depth + p] = own[1, p, rows, :]
            sides = jnp.where(lane == p, pltpu.roll(field[:, 0:LANES], p, 1), sides)
            sides = jnp.where(lane == depth + p, pltpu.roll(field[:, width - LANES : width], depth + p + 1, 1), sides)
        if reflect:
            message[2 * depth] = own[2, depth - 1 - outer, rows, :]
        else:
            message[2 * depth] = own[2, 0, rows, :]
            message[2 * depth + 1] = own[2, depth - 1, rows, :]
        message[message.shape[0] - 1] = jnp.zeros((HALO, width), jnp.float32)
        message[message.shape[0] - 1, :, 0:LANES] = sides


def head_lane(a, g):
    return 16 * a + LANES // 2 * (g % 2) + 8 * (g // 2)


def tail_lane(a, g):
    return 16 * a + LANES // 2 * (g % 2) + 8 * (1 - g // 2)


def pack_columns(reflect, own, got_a, got_b, strips, rim):
    odd_y, odd_z = is_odd("gy"), is_odd("grp")
    first_y, last_y = beyond("gy")
    _, depth, inner, width = own.shape
    groups = inner // 8 + 2
    odd_x = is_odd("gx")
    lane = lax.broadcasted_iota(jnp.int32, (8, LANES), 1)
    row = lax.broadcasted_iota(jnp.int32, (8, width), 0)
    wide = lax.broadcasted_iota(jnp.int32, (8, width), 1)

    def spread_out(v):
        return jnp.concatenate([v] * (width // LANES), 1)

    for p in range(depth):
        for side, (low, outside) in enumerate(((True, first_y), (False, last_y))):

            def take(i):
                strip = jnp.where(odd_y == (1 if low else 0), got_a[i], got_b[i])
                return jnp.where(outside, 0.0, strip)

            g = take(p)
            sides = take(got_a.shape[0] - 1)[:, 0:LANES]
            field = jnp.where(wide == 0, spread_out(pltpu.roll(sides, (LANES - p) % LANES, 1)), 0.0)
            last = spread_out(pltpu.roll(sides, LANES - 1 - depth - p, 1))
            field = jnp.where(wide == width - 1, last, field)
            moved = pltpu.roll(g, HALO - 1 if low else 1, 0)
            field = jnp.where(row == (HALO - 1 if low else 0), moved, field)
            if reflect and p in (0, depth - 1):
                field = jnp.where(odd_x == (1 if p == 0 else 0), take(2 * depth), field)
            elif not reflect and p in (0, depth - 1):
                field = take(2 * depth + (0 if p == 0 else 1))
            rim[side, 0, p] = g
            rim[side, 1, p] = take(depth + p)
            rim[side, 2, p] = field
        head = tail = jnp.zeros((8, LANES), jnp.float32)
        for a in range(3):
            for g in range(groups):
                if g == 0 or g == groups - 1:
                    rows = rim[min(g, 1), a, p]
                else:
                    rows = own[a, p, 8 * g - 8 : 8 * g, :]
                to = head_lane(a, g)
                moved = pltpu.roll(rows[:, 0:LANES], to, 1)
                head = jnp.where((lane >= to) & (lane < to + HALO), moved, head)
                to = tail_lane(a, g)
                moved = pltpu.roll(rows[:, width - LANES : width], (to + HALO) % LANES, 1)
                tail = jnp.where((lane >= to) & (lane < to + HALO), moved, tail)
        strips[0, p] = jnp.where(odd_z == 1, head, tail)
        strips[1, p] = jnp.where(odd_z == 1, tail, head)


def shifts(parts, step):
    if parts == 1:
        return (lambda v: [ahead(v[0], 1, step)]), (lambda v: [behind(v[0], 1, step)])
    return (lambda v: [v[1], ahead(v[0], 1)]), (lambda v: [behind(v[1], 1), v[0]])


def each(op, *lists):
    return [op(*values) for values in zip(*lists)]


def add(*lists):
    return each(lambda *values: functools.reduce(lambda x, y: x + y, values), *lists)


def times(x, y):
    return each(lambda v, w: v * w, x, y)


def solve(cells, own_at, own, out, seams):
    (src, cond, field, wx, wy, wz, vy, vz, diag, inv, sum8, cwx, cwy, cwz, cvy, cvz, cinv, res, q, cq, err) = cells
    total, parts, rows, lanes = cond.shape

    def load(ref, p):
        return [ref[p, i] for i in range(ref.shape[1])]

    def store(ref, p, values):
        for i, v in enumerate(values):
            ref[p, i] = v

    def reach(halo):
        low = max(1, own_at - halo)
        high = min(total, own_at + own + halo)
        return range((low + 1) // 2, (high + 1) // 2)

    fine = (1, *shifts(parts, 1))
    coarse = (2, *shifts(1, 3 - parts))
    zero = jnp.zeros((rows, lanes), jnp.float32)
    for ref in (q, cq, err, sum8):
        store(ref, 0, [zero] * ref.shape[1])

    even_row = lax.rem(lax.broadcasted_iota(jnp.int32, (rows, lanes), 0), 2) == 0
    even_lane = lax.rem(lax.broadcasted_iota(jnp.int32, (rows, lanes), 1), 2) == 0

    def gather(v):
        other = v[1] if parts == 2 else jnp.where(even_lane, ahead(v[0], 1), behind(v[0], 1))
        t = v[0] + other
        return [t + ahead(t, 0)]

    for k in reach(HALO):
        store(sum8, k, gather(add(load(cond, 2 * k - 1), load(cond, 2 * k))))

    def weights(ref, p, level):
        step, ahead_z, behind_z = level
        c = load(ref, p)
        x = add(c, load(ref, p + 1))
        y, yb = ([v + shift(v, 0, step) for v in c] for shift in (ahead, behind))
        z, zb = add(c, ahead_z(c)), add(c, behind_z(c))
        k = add(add(c, load(ref, p - 1), x), add(y, yb), add(z, zb))
        return x, y, z, yb, zb, k, each(lambda v, w: jnp.where(v > 0.0, 1.0 / w, 0.0), c, k)

    low = reach(HALO - 2).start
    store(wx, 2 * low - 2, add(load(cond, 2 * low - 2), load(cond, 2 * low - 1)))
    store(cwx, low - 1, add(load(sum8, low - 1), load(sum8, low)))
    for k in reach(HALO - 2):
        for p in (2 * k - 1, 2 * k):
            for ref, v in zip((wx, wy, wz, vy, vz, diag, inv), weights(cond, p, fine)):
                store(ref, p, v)
        for ref, v in zip((cwx, cwy, cwz, cvy, cvz, None, cinv), weights(sum8, k, coarse)):
            if ref is not None:
                store(ref, k, v)

    def spread(v, p, refs, level):
        x, y, z, yb, zb = refs
        step, ahead_z, behind_z = level
        here = load(v, p)
        n = add(times(load(x, p - 1), load(v, p - 1)), times(load(x, p), load(v, p + 1)))
        n = add(n, times(load(y, p), [ahead(u, 0, step) for u in here]))
        n = add(n, times(load(yb, p), [behind(u, 0, step) for u in here]))
        return add(n, add(times(load(z, p), ahead_z(here)), times(load(zb, p), behind_z(here))))

    def smooth(v, p, refs, scale, level):
        n = times(load(scale, p), spread(v, p, refs, level))
        return each(lambda u, w: KEEP * u + SPREAD * w, load(v, p), n)

    def between(p):
        planes, along_y, along_z = seams
        here = load(field, p)
        r = load(src, p)

        def less(r, weights, there, where=None):
            flux = each(lambda w, u, v: w * (u - v), weights, here, there)
            return each(lambda x, y: x - (y if where is None else jnp.where(where, y, 0.0)), r, flux)

        if p in planes:
            r = less(r, load(wx, p), load(field, p + 1))
        if p - 1 in planes:
            r = less(r, load(wx, p - 1), load(field, p - 1))
        r = less(r, load(wy, p), [ahead(v, 0) for v in here], along_y[0])
        r = less(r, load(vy, p), [behind(v, 0) for v in here], along_y[1])
        if along_z is not None:
            r = less(r, load(wz, p), fine[1](here), along_z[0])
            r = less(r, load(vz, p), fine[2](here), along_z[1])
        return r

    around, coarse_around = (wx, wy, wz, vy, vz), (cwx, cwy, cwz, cvy, cvz)

    for it in range(ITERS):
        halo = 4 * (ITERS - 1 - it)
        for k in reach(halo + 2):
            found = []
            for p in (2 * k - 1, 2 * k):
                if it == 0:
                    r = between(p)
                else:
                    n = spread(err, p, around, fine)
                    r = each(lambda u, d, w, m: u - (d * w - m), load(res, p), load(diag, p), load(err, p), n)
                if it < ITERS - 1:
                    store(res, p, r)
                store(q, p, times(r, load(inv, p)))
                found.append(r)
            store(cq, k, times([4.0 * gather(add(*found))[0]], load(cinv, k)))

        for k in reach(halo):
            (c,) = smooth(cq, k, coarse_around, cinv, coarse)
            c = jnp.where(even_row, c, behind(c, 0))
            for p in (2 * k - 1, 2 * k):
                e = [u + c for u in smooth(q, p, around, inv, fine)]
                if it:
                    e = add(load(err, p), e)
                if it < ITERS - 1:
                    store(err, p, e)
                else:
                    out(p, add(load(field, p), e))


def layout(reflect, depth):
    return (1, depth + HALO + 2) if reflect else (1 + HALO, depth + 2 * HALO + 2)


def each_plane(reflect, depth, place):
    odd_x = is_odd("gx")
    own_at, _ = layout(reflect, depth)

    for p in range(depth):
        place(None, jnp.where(odd_x == 1, depth - 1 - p, p) if reflect else p, own_at + p)
    for p in range(HALO):
        if reflect:
            place(0, jnp.where(odd_x == 1, depth - 1 - p, p), own_at + depth + p)
            continue
        for i in range(2):
            above = odd_x == i
            at = jnp.where(above, p, depth - HALO + p)
            place(i, at, jnp.where(above, own_at + depth + p, 1 + p))


def x_seams(reflect, depth):
    own_at, _ = layout(reflect, depth)
    return (own_at + depth - 1,) if reflect else (own_at - 1, own_at + depth - 1)


def out_plane(reflect, depth, p):
    own_at, _ = layout(reflect, depth)
    at = p - own_at
    return jnp.where(is_odd("gx") == 1, depth - 1 - at, at) if reflect else at


def parting(width, lanes):
    column = lax.broadcasted_iota(jnp.int32, (width, 2 * lanes), 0)
    lane = lax.broadcasted_iota(jnp.int32, (width, 2 * lanes), 1)
    wanted = jnp.where(lane < lanes, 2 * lane, 2 * (lane - lanes) + 1)
    return jnp.where((column == wanted) & (wanted < width), 1.0, 0.0)


def ending(width):
    column = lax.broadcasted_iota(jnp.int32, (width, 2 * LANES), 0)
    lane = lax.broadcasted_iota(jnp.int32, (width, 2 * LANES), 1)
    lane = jnp.where(lane < LANES, lane, lane - LANES - LANES // 2)
    last = (lane >= 8) & (lane < 24) & (column == lane + width - 24)
    first = (lane >= 40) & (lane < 56) & (column == lane - 40)
    return jnp.where(last | first, 1.0, 0.0)


def rearranged(v, matrix):
    bf16, f32 = jnp.bfloat16, jnp.float32
    matrix = matrix.astype(bf16)
    result = None
    for _ in range(3):
        part = v.astype(bf16)
        v = v - part.astype(f32)
        moved = jnp.dot(part, matrix, preferred_element_type=f32)
        result = moved if result is None else result + moved
    return result


def interior(reflect, n_x, *refs):
    own, rim = refs[0], refs[1]
    near, near_rim = refs[2 : 2 + n_x], refs[2 + n_x : 2 + 2 * n_x]
    result, ends = refs[2 + 2 * n_x : 4 + 2 * n_x]
    whole, halves, *cells = refs[4 + 2 * n_x :]
    _, depth, inner, width = own.shape
    rows = inner + 2 * HALO
    lanes = cells[0].shape[3]

    def place(i, p_from, p_to):
        block, halo = (own, rim) if i is None else (near[i], near_rim[i])
        for a in range(3):
            tile = whole.at[a, p_to]
            tile[0:HALO, :] = halo[0, a, p_from]
            tile[HALO : HALO + inner, :] = block[a, p_from]
            tile[HALO + inner : rows, :] = halo[1, a, p_from]

    own_at, total = layout(reflect, depth)
    for a in range(3):
        for p in (0, total - 1):
            whole[a, p] = jnp.zeros((rows, width), jnp.float32)
    each_plane(reflect, depth, place)
    apart = parting(width, lanes)
    target = jnp.concatenate([apart, ending(width)], 1)
    for a in range(3):
        parts = rearranged(whole[a].reshape(total * rows, width), target).reshape(total, rows, -1)
        for i in range(2):
            cells[a][:, i] = parts[:, :, i * lanes : (i + 1) * lanes]
        low = parts[:, 0 : rows - 8, 2 * lanes : 2 * lanes + LANES]
        ends[a] = low + parts[:, 8:rows, 2 * lanes + LANES :]

    def out(p, v):
        for i in range(2):
            halves[p - own_at, :, i * lanes : (i + 1) * lanes] = v[i][HALO : rows - HALO, :]

    row = lax.broadcasted_iota(jnp.int32, (rows, lanes), 0)
    along_y = (row == HALO - 1) | (row == HALO + inner - 1), (row == HALO) | (row == HALO + inner)
    solve(cells, own_at, depth, out, (x_seams(reflect, depth), along_y, None))
    together = rearranged(halves[...].reshape(depth * inner, 2 * lanes), apart.T)
    together = together.reshape(depth, inner, width)
    for p in range(depth):
        result[out_plane(reflect, depth, own_at + p)] = together[p]


def edges(reflect, ends, inside, got_a, got_b, result, *cells):
    depth, inner, width = inside.shape
    groups = ends.shape[2] // 8
    odd_z = is_odd("grp")
    first_z, last_z = beyond("grp")
    lane = lax.broadcasted_iota(jnp.int32, (8, LANES), 1)
    half = LANES // 2
    own_at, total = layout(reflect, depth)
    for p in (0, total - 1):
        for a in range(3):
            cells[a][p, 0] = ends[a, p]

    def place(i, p_from, p_to):
        at_plane = p_from if i is None else (i + 1) * depth + p_from
        va, vb = got_a[at_plane], got_b[at_plane]
        right = jnp.where(last_z, 0.0, jnp.where(odd_z == 1, vb, va))
        left = jnp.where(first_z, 0.0, jnp.where(odd_z == 1, va, vb))
        side = lax.rem(lane, 16) < 8
        lower = jnp.where(side, right, left)
        upper = jnp.where(side, pltpu.roll(right, LANES - 8, 1), pltpu.roll(left, 8, 1))
        middle = jnp.where(lane < half, upper, lower)
        for a in range(3):
            for t, (groups_of, shift) in enumerate(((lower, 24), (middle, 24 + half), (upper, 24))):
                moved = pltpu.roll(groups_of, (shift - 16 * a) % LANES, 1)
                here = lax.rem(lane, half)
                part = slice(8 * t, 8 * t + 8)
                cells[a][p_to, 0, part, :] = jnp.where((here >= 24) & (here < 40), moved, ends[a, p_to, part, :])

    each_plane(reflect, depth, place)

    def out(p, v):
        at = out_plane(reflect, depth, p)
        v = v[0][8:16]
        for i in range(2):
            part = slice(8 * i, 8 * i + 8)
            head = pltpu.roll(v, (LANES - 40 - half * i) % LANES, 1)
            tail = pltpu.roll(v, (LANES - 24 - half * i) % LANES, 1)
            for c in range(0, width, LANES):
                tile = inside[at, part, c : c + LANES]
                if c == 0:
                    tile = jnp.where(lane < HALO, head, tile)
                if c == width - LANES:
                    tile = jnp.where(lane >= LANES - HALO, tail, tile)
                result[at, part, c : c + LANES] = tile

    row = lax.broadcasted_iota(jnp.int32, ends.shape[2:], 0)
    lane_in_half = lax.rem(lax.broadcasted_iota(jnp.int32, ends.shape[2:], 1), half)
    upper_half = lax.broadcasted_iota(jnp.int32, ends.shape[2:], 1) >= half
    face = jnp.where(upper_half, inner, HALO)
    along_z = tuple((lane_in_half == at) | (lane_in_half == at + 16) for at in (23, 24))
    solve(cells, own_at, depth, out, (x_seams(reflect, depth), (row == face - 1, row == face), along_z))


def shards(sizes, source_term, conductivity, initial_field):
    depth, inner, width = source_term.shape
    assert inner == 16 and depth >= HALO and depth % 2 == 0 and width % LANES == 0
    rows = inner + 2 * HALO
    f32 = jnp.float32
    params = pltpu.CompilerParams(vmem_limit_bytes=48 * 1024 * 1024)
    args = (source_term, conductivity, initial_field)

    def exchange(values, axis):
        over, rounds = swaps(axis, sizes)
        found = [lax.ppermute(v, over, pairs) for v, pairs in reversed(list(zip(values, rounds)))]
        return found[::-1] + [jnp.zeros_like(v) for v in values[len(found) :]]

    def work(parts, rows, lanes):
        total = layout(reflect, depth)[1]
        fine = pltpu.VMEM((total, parts, rows, lanes), f32)
        coarse = pltpu.VMEM((total // 2 + 1, 1, rows, lanes), f32)
        return [fine] * 10 + [coarse] * 7 + [fine] * 2 + [coarse] + [fine]

    reflect = sizes["gx"] == 2
    n_x = 1 if reflect else 2
    args = [pltpu.with_memory_space_constraint(v, pltpu.HBM) for v in args]
    face = jax.ShapeDtypeStruct((2 * depth + n_x + 1, HALO, width), f32)
    own, *msgs = pl.pallas_call(
        functools.partial(prepare, reflect),
        out_shape=(jax.ShapeDtypeStruct((3, depth, inner, width), f32), face, face),
        in_specs=[pl.BlockSpec(memory_space=pltpu.HBM)] * 3, out_specs=(VMEM,) * 3,
        scratch_shapes=[pltpu.SemaphoreType.DMA((3,))], compiler_params=params, name="prepare",
    )(*args)
    got = exchange(msgs, "gy")
    near = exchange([own] * n_x, "gx")
    strips, rim = pl.pallas_call(
        functools.partial(pack_columns, reflect),
        out_shape=(
            jax.ShapeDtypeStruct((2, depth, 8, LANES), f32),
            jax.ShapeDtypeStruct((2, 3, depth, HALO, width), f32),
        ),
        in_specs=[VMEM] * 3, out_specs=(VMEM, VMEM),
        compiler_params=params, name="pack_columns",
    )(own, *got)
    strips = jnp.concatenate([strips] + exchange([strips] * n_x, "gx"), axis=1)
    strips, rim = lax.optimization_barrier((strips, rim))
    near_rim = exchange([rim] * n_x, "gx")
    strips = exchange([strips[0], strips[1]], "grp")

    block = jax.ShapeDtypeStruct(source_term.shape, f32)
    total = layout(reflect, depth)[1]
    lanes = -(-width // (2 * LANES)) * LANES
    apart = [pltpu.VMEM((3, total, rows, width), f32), pltpu.VMEM((depth, inner, 2 * lanes), f32)]
    inside, ends = pl.pallas_call(
        functools.partial(interior, reflect, n_x),
        out_shape=(block, jax.ShapeDtypeStruct((3, total, rows - 8, LANES), f32)),
        in_specs=[VMEM] * (2 + 2 * n_x), out_specs=(VMEM, VMEM), scratch_shapes=apart + work(2, rows, lanes),
        compiler_params=params, name="interior",
        cost_estimate=pl.CostEstimate(flops=20_000_000, bytes_accessed=20_000_000, transcendentals=0),
    )(own, rim, *near, *near_rim)
    inside, ends, *strips = lax.optimization_barrier((inside, ends, *strips[::-1]))
    strips = strips[::-1]
    return pl.pallas_call(
        functools.partial(edges, reflect),
        out_shape=block,
        in_specs=[VMEM] * 4, out_specs=VMEM, scratch_shapes=work(1, rows - 8, LANES),
        compiler_params=params, name="edges",
    )(ends, inside, *strips)


def solution(mesh):
    spec = P("gx", "gy", "grp")
    return jax.shard_map(
        functools.partial(shards, dict(mesh.shape)),
        mesh=mesh,
        in_specs=(spec,) * 3,
        out_specs=spec,
        check_vma=False,
    )
```

```python
import functools

import jax
import jax.numpy as jnp
from jax import lax
from jax.experimental import pallas as pl
from jax.experimental.pallas import tpu as pltpu
from jax.sharding import PartitionSpec as P

ITERS = 2
HALO = 4 * ITERS
LANES = 128
KEEP = 48.0 / 41.0
SPREAD = 32.0 / 41.0
VMEM = pl.BlockSpec(memory_space=pltpu.VMEM)


def ahead(v, axis, n=1):
    return pltpu.roll(v, v.shape[axis] - n, axis)


def behind(v, axis, n=1):
    return pltpu.roll(v, n, axis)


def swaps(axis, sizes):
    count, fill = sizes[axis], sizes["gx"]
    over = [name for name in sizes if name in (axis, "gx")]
    filled = axis != "gx" and fill % 2 == 0

    def at(i, k):
        return i * fill + k if over[0] == axis else k * count + i

    rounds = []
    for start in (0, 1):
        pairs = [(i, i + 1) for i in range(start, count - 1, 2)]
        left = set(range(count)) - {i for pair in pairs for i in pair}
        if not pairs:
            continue
        if filled:
            pairs = [(at(i, k), at(j, k)) for i, j in pairs for k in range(fill)]
            pairs += [(at(i, k), at(i, k + 1)) for i in sorted(left) for k in range(0, fill, 2)]
        rounds.append(pairs + [(j, i) for i, j in pairs])
    return (tuple(over) if filled else axis), rounds


def is_odd(axis):
    return lax.rem(lax.axis_index(axis), 2)


def beyond(axis):
    at = lax.axis_index(axis)
    return at == 0, at == lax.axis_size(axis) - 1


def is_odd(axis):
    return lax.rem(lax.axis_index(axis), 2)


def far_row(high, distance):
    if isinstance(high, bool):
        return HALO - distance if high else distance - 1
    return jnp.where(high, HALO - distance, distance - 1)


def shifted_rows(high, v, n):
    if isinstance(high, bool):
        return pltpu.roll(v, HALO - n if high else n, 0)
    return jnp.where(high, pltpu.roll(v, HALO - n, 0), pltpu.roll(v, n, 0))


def inward(high, v):
    return shifted_rows(high, v, HALO - 1)


def prepare(reflect, s, c, f, own, first, second, sems):
    copies = [pltpu.make_async_copy(ref, own.at[a], sems.at[a]) for a, ref in enumerate((s, c, f))]
    for copy in copies:
        copy.start()
    for copy in copies:
        copy.wait()
    _, depth, inner, width = own.shape
    row = lax.broadcasted_iota(jnp.int32, (inner, width), 0)
    column = lax.broadcasted_iota(jnp.int32, (inner, width), 1)
    outer = jnp.where(is_odd("gx") == 1, depth - 1, 0)
    for p in range(depth):
        cond, field = own[1, p], own[2, p]

        def flux(shift, axis):
            return (cond + shift(cond, axis)) * (field - shift(field, axis))

        total = jnp.where(row < inner - 1, flux(ahead, 0), 0.0) + jnp.where(row > 0, flux(behind, 0), 0.0)
        total += jnp.where(column < width - 1, flux(ahead, 1), 0.0) + jnp.where(column > 0, flux(behind, 1), 0.0)
        for other in (p - 1, p + 1):
            if 0 <= other < depth:
                total += (cond + own[1, other]) * (field - own[2, other])
        if reflect and p in (0, depth - 1):
            total += jnp.where(outer == p, cond * field, 0.0)
        own[0, p] = 2.0 * own[0, p] - total

    odd = is_odd("gy")
    row = lax.broadcasted_iota(jnp.int32, (HALO, width), 0)
    lane = lax.broadcasted_iota(jnp.int32, (HALO, LANES), 1)
    for message, high in ((first, odd == 0), (second, odd == 1)):
        rows = pl.ds(pl.multiple_of(jnp.where(high, inner - HALO, 0), 8), HALO)
        at = functools.partial(far_row, high)
        sides = jnp.zeros((HALO, LANES), jnp.float32)
        for p in range(0, depth, 2):
            sums = own[1, p, rows, :] + own[1, p + 1, rows, :]
            sums = sums + inward(high, sums)
            rests = own[0, p, rows, :] + own[0, p + 1, rows, :]
            rests = shifted_rows(high, rests + inward(high, rests), 2)
            for i, seventh in enumerate((sums, rests)):
                field = own[2, p + i, rows, :]
                cond = jnp.where(row == at(7), seventh, own[1, p + i, rows, :])
                message[p + i] = jnp.where(row == at(8), inward(high, field), cond)
                head, tail = field[:, 0:LANES], field[:, width - LANES : width]
                sides = jnp.where(lane == p + i, pltpu.roll(head, p + i, 1), sides)
                sides = jnp.where(lane == depth + p + i, pltpu.roll(tail, depth + p + i + 1, 1), sides)
            near = jnp.where(high, HALO - 1 - row, row) < 4
            message[depth + p // 2] = jnp.where(near, own[0, p, rows, :], pltpu.roll(own[0, p + 1, rows, :], 4, 0))
        planes = depth + depth // 2
        if reflect:
            message[planes] = own[2, depth - 1 - outer, rows, :]
        else:
            message[planes] = own[2, 0, rows, :]
            message[planes + 1] = own[2, depth - 1, rows, :]
        message[message.shape[0] - 1] = jnp.zeros((HALO, width), jnp.float32)
        message[message.shape[0] - 1, :, 0:LANES] = sides


def head_lane(a, g):
    return 16 * a + LANES // 2 * (g % 2) + 8 * (g // 2)


def tail_lane(a, g):
    return 16 * a + LANES // 2 * (g % 2) + 8 * (1 - g // 2)


def pack_columns(reflect, own, got_a, got_b, strips, rim):
    odd_y, odd_z = is_odd("gy"), is_odd("grp")
    first_y, last_y = beyond("gy")
    _, depth, inner, width = own.shape
    groups = inner // 8 + 2
    odd_x = is_odd("gx")
    lane = lax.broadcasted_iota(jnp.int32, (8, LANES), 1)
    row = lax.broadcasted_iota(jnp.int32, (8, width), 0)
    wide = lax.broadcasted_iota(jnp.int32, (8, width), 1)

    def spread_out(v):
        return jnp.concatenate([v] * (width // LANES), 1)

    for p in range(depth):
        for side, (low, outside) in enumerate(((True, first_y), (False, last_y))):

            at = functools.partial(far_row, low)

            def take(i):
                strip = jnp.where(odd_y == (1 if low else 0), got_a[i], got_b[i])
                return jnp.where(outside, 0.0, strip)

            cond, mixed = take(p), take(depth + p // 2)
            g = mixed if p % 2 == 0 else pltpu.roll(mixed, 4, 0)
            g = jnp.where(row >= 4 if low else row < 4, g, 0.0)
            if p % 2:
                g = jnp.where(row == at(5), shifted_rows(low, cond, HALO - 2), g)
            sides = take(got_a.shape[0] - 1)[:, 0:LANES]
            field = jnp.where(wide == 0, spread_out(pltpu.roll(sides, (LANES - p) % LANES, 1)), 0.0)
            last = spread_out(pltpu.roll(sides, LANES - 1 - depth - p, 1))
            field = jnp.where(wide == width - 1, last, field)
            field = jnp.where(row == at(1), shifted_rows(low, cond, 1), field)
            planes = depth + depth // 2
            if reflect and p in (0, depth - 1):
                field = jnp.where(odd_x == (1 if p == 0 else 0), take(planes), field)
            elif not reflect and p in (0, depth - 1):
                field = take(planes + (0 if p == 0 else 1))
            cond = jnp.where(row == at(8), 0.0, cond)
            if p % 2:
                cond = jnp.where(row == at(7), 0.0, cond)
            rim[side, 0, p] = g
            rim[side, 1, p] = cond
            rim[side, 2, p] = field
        head = tail = jnp.zeros((8, LANES), jnp.float32)
        for a in range(3):
            for g in range(groups):
                if g == 0 or g == groups - 1:
                    rows = rim[min(g, 1), a, p]
                else:
                    rows = own[a, p, 8 * g - 8 : 8 * g, :]
                to = head_lane(a, g)
                moved = pltpu.roll(rows[:, 0:LANES], to, 1)
                head = jnp.where((lane >= to) & (lane < to + HALO), moved, head)
                to = tail_lane(a, g)
                moved = pltpu.roll(rows[:, width - LANES : width], (to + HALO) % LANES, 1)
                tail = jnp.where((lane >= to) & (lane < to + HALO), moved, tail)
        strips[0, p] = jnp.where(odd_z == 1, head, tail)
        strips[1, p] = jnp.where(odd_z == 1, tail, head)


def shifts(parts, step):
    if parts == 1:
        return (lambda v: [ahead(v[0], 1, step)]), (lambda v: [behind(v[0], 1, step)])
    return (lambda v: [v[1], ahead(v[0], 1)]), (lambda v: [behind(v[1], 1), v[0]])


def each(op, *lists):
    return [op(*values) for values in zip(*lists)]


def add(*lists):
    return each(lambda *values: functools.reduce(lambda x, y: x + y, values), *lists)


def times(x, y):
    return each(lambda v, w: v * w, x, y)


def solve(cells, own_at, own, out, seams):
    (src, cond, field, wx, wy, wz, vy, vz, diag, inv, sum8, cwx, cwy, cwz, cvy, cvz, cinv, res, q, cq, err) = cells
    total, parts, rows, lanes = cond.shape

    def load(ref, p):
        return [ref[p, i] for i in range(ref.shape[1])]

    def store(ref, p, values):
        for i, v in enumerate(values):
            ref[p, i] = v

    def reach(halo):
        low = max(1, own_at - halo)
        high = min(total, own_at + own + halo)
        return range((low + 1) // 2, (high + 1) // 2)

    fine = (1, *shifts(parts, 1))
    coarse = (2, *shifts(1, 3 - parts))
    zero = jnp.zeros((rows, lanes), jnp.float32)
    for ref in (q, cq, err, sum8):
        store(ref, 0, [zero] * ref.shape[1])

    even_row = lax.rem(lax.broadcasted_iota(jnp.int32, (rows, lanes), 0), 2) == 0
    even_lane = lax.rem(lax.broadcasted_iota(jnp.int32, (rows, lanes), 1), 2) == 0

    def gather(v):
        other = v[1] if parts == 2 else jnp.where(even_lane, ahead(v[0], 1), behind(v[0], 1))
        t = v[0] + other
        return [t + ahead(t, 0)]

    for k in reach(HALO):
        store(sum8, k, gather(add(load(cond, 2 * k - 1), load(cond, 2 * k))))

    def weights(ref, p, level):
        step, ahead_z, behind_z = level
        c = load(ref, p)
        x = add(c, load(ref, p + 1))
        y, yb = ([v + shift(v, 0, step) for v in c] for shift in (ahead, behind))
        z, zb = add(c, ahead_z(c)), add(c, behind_z(c))
        k = add(add(c, load(ref, p - 1), x), add(y, yb), add(z, zb))
        return x, y, z, yb, zb, k, each(lambda v, w: jnp.where(v > 0.0, 1.0 / w, 0.0), c, k)

    low = reach(HALO - 2).start
    store(wx, 2 * low - 2, add(load(cond, 2 * low - 2), load(cond, 2 * low - 1)))
    store(cwx, low - 1, add(load(sum8, low - 1), load(sum8, low)))
    for k in reach(HALO - 2):
        for p in (2 * k - 1, 2 * k):
            for ref, v in zip((wx, wy, wz, vy, vz, diag, inv), weights(cond, p, fine)):
                store(ref, p, v)
        for ref, v in zip((cwx, cwy, cwz, cvy, cvz, None, cinv), weights(sum8, k, coarse)):
            if ref is not None:
                store(ref, k, v)

    def spread(v, p, refs, level):
        x, y, z, yb, zb = refs
        step, ahead_z, behind_z = level
        here = load(v, p)
        n = add(times(load(x, p - 1), load(v, p - 1)), times(load(x, p), load(v, p + 1)))
        n = add(n, times(load(y, p), [ahead(u, 0, step) for u in here]))
        n = add(n, times(load(yb, p), [behind(u, 0, step) for u in here]))
        return add(n, add(times(load(z, p), ahead_z(here)), times(load(zb, p), behind_z(here))))

    def smooth(v, p, refs, scale, level):
        n = times(load(scale, p), spread(v, p, refs, level))
        return each(lambda u, w: KEEP * u + SPREAD * w, load(v, p), n)

    def between(p):
        planes, along_y, along_z = seams
        here = load(field, p)
        r = load(src, p)

        def less(r, weights, there, where=None):
            flux = each(lambda w, u, v: w * (u - v), weights, here, there)
            return each(lambda x, y: x - (y if where is None else jnp.where(where, y, 0.0)), r, flux)

        if p in planes:
            r = less(r, load(wx, p), load(field, p + 1))
        if p - 1 in planes:
            r = less(r, load(wx, p - 1), load(field, p - 1))
        r = less(r, load(wy, p), [ahead(v, 0) for v in here], along_y[0])
        r = less(r, load(vy, p), [behind(v, 0) for v in here], along_y[1])
        if along_z is not None:
            r = less(r, load(wz, p), fine[1](here), along_z[0])
            r = less(r, load(vz, p), fine[2](here), along_z[1])
        return r

    around, coarse_around = (wx, wy, wz, vy, vz), (cwx, cwy, cwz, cvy, cvz)

    for it in range(ITERS):
        halo = 4 * (ITERS - 1 - it)
        for k in reach(halo + 2):
            found = []
            for p in (2 * k - 1, 2 * k):
                if it == 0:
                    r = between(p)
                else:
                    n = spread(err, p, around, fine)
                    r = each(lambda u, d, w, m: u - (d * w - m), load(res, p), load(diag, p), load(err, p), n)
                if it < ITERS - 1:
                    store(res, p, r)
                store(q, p, times(r, load(inv, p)))
                found.append(r)
            store(cq, k, times([4.0 * gather(add(*found))[0]], load(cinv, k)))

        for k in reach(halo):
            (c,) = smooth(cq, k, coarse_around, cinv, coarse)
            c = jnp.where(even_row, c, behind(c, 0))
            for p in (2 * k - 1, 2 * k):
                e = [u + c for u in smooth(q, p, around, inv, fine)]
                if it:
                    e = add(load(err, p), e)
                if it < ITERS - 1:
                    store(err, p, e)
                else:
                    out(p, add(load(field, p), e))


def layout(reflect, depth):
    return (1, depth + HALO + 2) if reflect else (1 + HALO, depth + 2 * HALO + 2)


def each_plane(reflect, depth, place):
    odd_x = is_odd("gx")
    own_at, _ = layout(reflect, depth)

    for p in range(depth):
        place(None, jnp.where(odd_x == 1, depth - 1 - p, p) if reflect else p, own_at + p)
    for p in range(HALO):
        if reflect:
            place(0, jnp.where(odd_x == 1, depth - 1 - p, p), own_at + depth + p)
            continue
        for i in range(2):
            above = odd_x == i
            at = jnp.where(above, p, depth - HALO + p)
            place(i, at, jnp.where(above, own_at + depth + p, 1 + p))


def x_seams(reflect, depth):
    own_at, _ = layout(reflect, depth)
    return (own_at + depth - 1,) if reflect else (own_at - 1, own_at + depth - 1)


def out_plane(reflect, depth, p):
    own_at, _ = layout(reflect, depth)
    at = p - own_at
    return jnp.where(is_odd("gx") == 1, depth - 1 - at, at) if reflect else at


def parting(width, lanes):
    column = lax.broadcasted_iota(jnp.int32, (width, 2 * lanes), 0)
    lane = lax.broadcasted_iota(jnp.int32, (width, 2 * lanes), 1)
    wanted = jnp.where(lane < lanes, 2 * lane, 2 * (lane - lanes) + 1)
    return jnp.where((column == wanted) & (wanted < width), 1.0, 0.0)


def ending(width):
    column = lax.broadcasted_iota(jnp.int32, (width, 2 * LANES), 0)
    lane = lax.broadcasted_iota(jnp.int32, (width, 2 * LANES), 1)
    lane = jnp.where(lane < LANES, lane, lane - LANES - LANES // 2)
    last = (lane >= 8) & (lane < 24) & (column == lane + width - 24)
    first = (lane >= 40) & (lane < 56) & (column == lane - 40)
    return jnp.where(last | first, 1.0, 0.0)


def rearranged(v, matrix):
    bf16, f32 = jnp.bfloat16, jnp.float32
    matrix = matrix.astype(bf16)
    result = None
    for _ in range(3):
        part = v.astype(bf16)
        v = v - part.astype(f32)
        moved = jnp.dot(part, matrix, preferred_element_type=f32)
        result = moved if result is None else result + moved
    return result


def interior(reflect, n_x, *refs):
    own, rim = refs[0], refs[1]
    near, near_rim = refs[2 : 2 + n_x], refs[2 + n_x : 2 + 2 * n_x]
    result, ends = refs[2 + 2 * n_x : 4 + 2 * n_x]
    whole, halves, *cells = refs[4 + 2 * n_x :]
    _, depth, inner, width = own.shape
    rows = inner + 2 * HALO
    lanes = cells[0].shape[3]

    def place(i, p_from, p_to):
        block, halo = (own, rim) if i is None else (near[i], near_rim[i])
        for a in range(3):
            tile = whole.at[a, p_to]
            tile[0:HALO, :] = halo[0, a, p_from]
            tile[HALO : HALO + inner, :] = block[a, p_from]
            tile[HALO + inner : rows, :] = halo[1, a, p_from]

    own_at, total = layout(reflect, depth)
    for a in range(3):
        for p in (0, total - 1):
            whole[a, p] = jnp.zeros((rows, width), jnp.float32)
    each_plane(reflect, depth, place)
    apart = parting(width, lanes)
    target = jnp.concatenate([apart, ending(width)], 1)
    for a in range(3):
        parts = rearranged(whole[a].reshape(total * rows, width), target).reshape(total, rows, -1)
        for i in range(2):
            cells[a][:, i] = parts[:, :, i * lanes : (i + 1) * lanes]
        low = parts[:, 0 : rows - 8, 2 * lanes : 2 * lanes + LANES]
        ends[a] = low + parts[:, 8:rows, 2 * lanes + LANES :]

    def out(p, v):
        for i in range(2):
            halves[p - own_at, :, i * lanes : (i + 1) * lanes] = v[i][HALO : rows - HALO, :]

    row = lax.broadcasted_iota(jnp.int32, (rows, lanes), 0)
    along_y = (row == HALO - 1) | (row == HALO + inner - 1), (row == HALO) | (row == HALO + inner)
    solve(cells, own_at, depth, out, (x_seams(reflect, depth), along_y, None))
    together = rearranged(halves[...].reshape(depth * inner, 2 * lanes), apart.T)
    together = together.reshape(depth, inner, width)
    for p in range(depth):
        result[out_plane(reflect, depth, own_at + p)] = together[p]


def edges(reflect, ends, inside, got_a, got_b, result, *cells):
    depth, inner, width = inside.shape
    groups = ends.shape[2] // 8
    odd_z = is_odd("grp")
    first_z, last_z = beyond("grp")
    lane = lax.broadcasted_iota(jnp.int32, (8, LANES), 1)
    half = LANES // 2
    own_at, total = layout(reflect, depth)
    for p in (0, total - 1):
        for a in range(3):
            cells[a][p, 0] = ends[a, p]

    def place(i, p_from, p_to):
        at_plane = p_from if i is None else (i + 1) * depth + p_from
        va, vb = got_a[at_plane], got_b[at_plane]
        right = jnp.where(last_z, 0.0, jnp.where(odd_z == 1, vb, va))
        left = jnp.where(first_z, 0.0, jnp.where(odd_z == 1, va, vb))
        side = lax.rem(lane, 16) < 8
        lower = jnp.where(side, right, left)
        upper = jnp.where(side, pltpu.roll(right, LANES - 8, 1), pltpu.roll(left, 8, 1))
        middle = jnp.where(lane < half, upper, lower)
        for a in range(3):
            for t, (groups_of, shift) in enumerate(((lower, 24), (middle, 24 + half), (upper, 24))):
                moved = pltpu.roll(groups_of, (shift - 16 * a) % LANES, 1)
                here = lax.rem(lane, half)
                part = slice(8 * t, 8 * t + 8)
                cells[a][p_to, 0, part, :] = jnp.where((here >= 24) & (here < 40), moved, ends[a, p_to, part, :])

    each_plane(reflect, depth, place)

    def out(p, v):
        at = out_plane(reflect, depth, p)
        v = v[0][8:16]
        for i in range(2):
            part = slice(8 * i, 8 * i + 8)
            head = pltpu.roll(v, (LANES - 40 - half * i) % LANES, 1)
            tail = pltpu.roll(v, (LANES - 24 - half * i) % LANES, 1)
            for c in range(0, width, LANES):
                tile = inside[at, part, c : c + LANES]
                if c == 0:
                    tile = jnp.where(lane < HALO, head, tile)
                if c == width - LANES:
                    tile = jnp.where(lane >= LANES - HALO, tail, tile)
                result[at, part, c : c + LANES] = tile

    row = lax.broadcasted_iota(jnp.int32, ends.shape[2:], 0)
    lane_in_half = lax.rem(lax.broadcasted_iota(jnp.int32, ends.shape[2:], 1), half)
    upper_half = lax.broadcasted_iota(jnp.int32, ends.shape[2:], 1) >= half
    face = jnp.where(upper_half, inner, HALO)
    along_z = tuple((lane_in_half == at) | (lane_in_half == at + 16) for at in (23, 24))
    solve(cells, own_at, depth, out, (x_seams(reflect, depth), (row == face - 1, row == face), along_z))


def shards(sizes, source_term, conductivity, initial_field):
    depth, inner, width = source_term.shape
    assert inner == 16 and depth >= HALO and depth % 2 == 0 and width % LANES == 0
    rows = inner + 2 * HALO
    f32 = jnp.float32
    params = pltpu.CompilerParams(vmem_limit_bytes=48 * 1024 * 1024)
    args = (source_term, conductivity, initial_field)

    def exchange(values, axis):
        over, rounds = swaps(axis, sizes)
        found = [lax.ppermute(v, over, pairs) for v, pairs in reversed(list(zip(values, rounds)))]
        return found[::-1] + [jnp.zeros_like(v) for v in values[len(found) :]]

    def work(parts, rows, lanes):
        total = layout(reflect, depth)[1]
        fine = pltpu.VMEM((total, parts, rows, lanes), f32)
        coarse = pltpu.VMEM((total // 2 + 1, 1, rows, lanes), f32)
        return [fine] * 10 + [coarse] * 7 + [fine] * 2 + [coarse] + [fine]

    reflect = sizes["gx"] == 2
    n_x = 1 if reflect else 2
    args = [pltpu.with_memory_space_constraint(v, pltpu.HBM) for v in args]
    face = jax.ShapeDtypeStruct((depth + depth // 2 + n_x + 1, HALO, width), f32)
    own, *msgs = pl.pallas_call(
        functools.partial(prepare, reflect),
        out_shape=(jax.ShapeDtypeStruct((3, depth, inner, width), f32), face, face),
        in_specs=[pl.BlockSpec(memory_space=pltpu.HBM)] * 3, out_specs=(VMEM,) * 3,
        scratch_shapes=[pltpu.SemaphoreType.DMA((3,))], compiler_params=params, name="prepare",
    )(*args)
    got = exchange(msgs, "gy")
    near = exchange([own] * n_x, "gx")
    strips, rim = pl.pallas_call(
        functools.partial(pack_columns, reflect),
        out_shape=(
            jax.ShapeDtypeStruct((2, depth, 8, LANES), f32),
            jax.ShapeDtypeStruct((2, 3, depth, HALO, width), f32),
        ),
        in_specs=[VMEM] * 3, out_specs=(VMEM, VMEM),
        compiler_params=params, name="pack_columns",
    )(own, *got)
    strips = jnp.concatenate([strips] + exchange([strips] * n_x, "gx"), axis=1)
    strips, rim = lax.optimization_barrier((strips, rim))
    near_rim = exchange([rim] * n_x, "gx")
    strips = exchange([strips[0], strips[1]], "grp")

    block = jax.ShapeDtypeStruct(source_term.shape, f32)
    total = layout(reflect, depth)[1]
    lanes = -(-width // (2 * LANES)) * LANES
    apart = [pltpu.VMEM((3, total, rows, width), f32), pltpu.VMEM((depth, inner, 2 * lanes), f32)]
    inside, ends = pl.pallas_call(
        functools.partial(interior, reflect, n_x),
        out_shape=(block, jax.ShapeDtypeStruct((3, total, rows - 8, LANES), f32)),
        in_specs=[VMEM] * (2 + 2 * n_x), out_specs=(VMEM, VMEM), scratch_shapes=apart + work(2, rows, lanes),
        compiler_params=params, name="interior",
        cost_estimate=pl.CostEstimate(flops=20_000_000, bytes_accessed=20_000_000, transcendentals=0),
    )(own, rim, *near, *near_rim)
    inside, ends, *strips = lax.optimization_barrier((inside, ends, *strips[::-1]))
    strips = strips[::-1]
    return pl.pallas_call(
        functools.partial(edges, reflect),
        out_shape=block,
        in_specs=[VMEM] * 4, out_specs=VMEM, scratch_shapes=work(1, rows - 8, LANES),
        compiler_params=params, name="edges",
    )(ends, inside, *strips)


def solution(mesh):
    spec = P("gx", "gy", "grp")
    return jax.shard_map(
        functools.partial(shards, dict(mesh.shape)),
        mesh=mesh,
        in_specs=(spec,) * 3,
        out_specs=spec,
        check_vma=False,
    )
```

```python
import functools

import jax
import jax.numpy as jnp
from jax import lax
from jax.experimental import pallas as pl
from jax.experimental.pallas import tpu as pltpu
from jax.sharding import PartitionSpec as P

ITERS = 2
HALO = 4 * ITERS
LANES = 128
KEEP = 48.0 / 41.0
SPREAD = 32.0 / 41.0
VMEM = pl.BlockSpec(memory_space=pltpu.VMEM)


def ahead(v, axis, n=1):
    return pltpu.roll(v, v.shape[axis] - n, axis)


def behind(v, axis, n=1):
    return pltpu.roll(v, n, axis)


def swaps(axis, sizes):
    count, fill = sizes[axis], sizes["gx"]
    over = [name for name in sizes if name in (axis, "gx")]
    filled = axis != "gx" and fill % 2 == 0

    def at(i, k):
        return i * fill + k if over[0] == axis else k * count + i

    rounds = []
    for start in (0, 1):
        pairs = [(i, i + 1) for i in range(start, count - 1, 2)]
        left = set(range(count)) - {i for pair in pairs for i in pair}
        if not pairs:
            continue
        if filled:
            pairs = [(at(i, k), at(j, k)) for i, j in pairs for k in range(fill)]
            pairs += [(at(i, k), at(i, k + 1)) for i in sorted(left) for k in range(0, fill, 2)]
        rounds.append(pairs + [(j, i) for i, j in pairs])
    return (tuple(over) if filled else axis), rounds


def is_odd(axis):
    return lax.rem(lax.axis_index(axis), 2)


def beyond(axis):
    at = lax.axis_index(axis)
    return at == 0, at == lax.axis_size(axis) - 1


def is_odd(axis):
    return lax.rem(lax.axis_index(axis), 2)


def far_row(high, distance):
    if isinstance(high, bool):
        return HALO - distance if high else distance - 1
    return jnp.where(high, HALO - distance, distance - 1)


def shifted_rows(high, v, n):
    if isinstance(high, bool):
        return pltpu.roll(v, HALO - n if high else n, 0)
    return jnp.where(high, pltpu.roll(v, HALO - n, 0), pltpu.roll(v, n, 0))


def inward(high, v):
    return shifted_rows(high, v, HALO - 1)


def both_ends(rows):
    width = rows.shape[1]
    lane = lax.broadcasted_iota(jnp.int32, (rows.shape[0], LANES), 1)
    return jnp.where(lane < LANES // 2, rows[:, 0:LANES], rows[:, width - LANES : width])


def prepare(reflect, s, c, f, own, first, second, sems):
    copies = [pltpu.make_async_copy(ref, own.at[a], sems.at[a]) for a, ref in enumerate((s, c, f))]
    for copy in copies:
        copy.start()
    for copy in copies:
        copy.wait()
    _, depth, inner, width = own.shape
    row = lax.broadcasted_iota(jnp.int32, (inner, width), 0)
    column = lax.broadcasted_iota(jnp.int32, (inner, width), 1)
    outer = jnp.where(is_odd("gx") == 1, depth - 1, 0)
    for p in range(depth):
        cond, field = own[1, p], own[2, p]

        def flux(axis):
            return (cond + ahead(cond, axis)) * (field - ahead(field, axis))

        along_y = jnp.where(row < inner - 1, flux(0), 0.0)
        along_z = jnp.where(column < width - 1, flux(1), 0.0)
        total = (along_y - behind(along_y, 0)) + (along_z - behind(along_z, 1))
        for other in (p - 1, p + 1):
            if 0 <= other < depth:
                total += (cond + own[1, other]) * (field - own[2, other])
        if reflect and p in (0, depth - 1):
            total += jnp.where(outer == p, cond * field, 0.0)
        own[0, p] = 2.0 * own[0, p] - total

    odd = is_odd("gy")
    row = lax.broadcasted_iota(jnp.int32, (HALO, width), 0)
    lane = lax.broadcasted_iota(jnp.int32, (HALO, LANES), 1)
    for message, high in ((first, odd == 0), (second, odd == 1)):
        rows = pl.ds(pl.multiple_of(jnp.where(high, inner - HALO, 0), 8), HALO)
        at = functools.partial(far_row, high)
        sides = jnp.zeros((HALO, LANES), jnp.float32)
        for p in range(0, depth, 2):
            sums = own[1, p, rows, :] + own[1, p + 1, rows, :]
            sums = sums + inward(high, sums)
            rests = own[0, p, rows, :] + own[0, p + 1, rows, :]
            rests = shifted_rows(high, rests + inward(high, rests), 2)
            for i, seventh in enumerate((sums, rests)):
                field = own[2, p + i, rows, :]
                cond = jnp.where(row == at(7), seventh, own[1, p + i, rows, :])
                message[p + i] = jnp.where(row == at(8), inward(high, field), cond)
                ends = pltpu.roll(both_ends(field), 2 * (p + i) + 1, 1)
                sides = jnp.where(lane // 2 == p + i, ends, sides)
            near = jnp.where(high, HALO - 1 - row, row) < 4
            message[depth + p // 2] = jnp.where(near, own[0, p, rows, :], pltpu.roll(own[0, p + 1, rows, :], 4, 0))
        planes = depth + depth // 2
        if reflect:
            message[planes] = own[2, depth - 1 - outer, rows, :]
        else:
            message[planes] = own[2, 0, rows, :]
            message[planes + 1] = own[2, depth - 1, rows, :]
        message[message.shape[0] - 1] = jnp.zeros((HALO, width), jnp.float32)
        message[message.shape[0] - 1, :, 0:LANES] = sides


def head_lane(a, g):
    return 8 + 16 * a + LANES // 2 * (g % 2) + 8 * (g // 2)


def tail_lane(a, g):
    return 8 + 16 * a + LANES // 2 * (g % 2) + 8 * (1 - g // 2)


def pack_columns(reflect, own, got_a, got_b, strips, rim):
    odd_y, odd_z = is_odd("gy"), is_odd("grp")
    first_y, last_y = beyond("gy")
    _, depth, inner, width = own.shape
    groups = inner // 8 + 2
    odd_x = is_odd("gx")
    lane = lax.broadcasted_iota(jnp.int32, (8, LANES), 1)
    row = lax.broadcasted_iota(jnp.int32, (8, width), 0)
    wide = lax.broadcasted_iota(jnp.int32, (8, width), 1)

    def spread_out(v):
        return jnp.concatenate([v] * (width // LANES), 1)

    for p in range(depth):
        for side, (low, outside) in enumerate(((True, first_y), (False, last_y))):

            at = functools.partial(far_row, low)

            def take(i):
                strip = jnp.where(odd_y == (1 if low else 0), got_a[i], got_b[i])
                return jnp.where(outside, 0.0, strip)

            cond, mixed = take(p), take(depth + p // 2)
            g = mixed if p % 2 == 0 else pltpu.roll(mixed, 4, 0)
            g = jnp.where(row >= 4 if low else row < 4, g, 0.0)
            if p % 2:
                g = jnp.where(row == at(5), shifted_rows(low, cond, HALO - 2), g)
            sides = take(got_a.shape[0] - 1)[:, 0:LANES]
            ends = spread_out(pltpu.roll(sides, LANES - 1 - 2 * p, 1))
            field = jnp.where((wide == 0) | (wide == width - 1), ends, 0.0)
            field = jnp.where(row == at(1), shifted_rows(low, cond, 1), field)
            planes = depth + depth // 2
            if reflect and p in (0, depth - 1):
                field = jnp.where(odd_x == (1 if p == 0 else 0), take(planes), field)
            elif not reflect and p in (0, depth - 1):
                field = take(planes + (0 if p == 0 else 1))
            cond = jnp.where(row == at(8), 0.0, cond)
            if p % 2:
                cond = jnp.where(row == at(7), 0.0, cond)
            rim[side, 0, p] = g
            rim[side, 1, p] = cond
            rim[side, 2, p] = field
        head = tail = jnp.zeros((8, LANES), jnp.float32)
        for a in range(3):
            for g in range(groups):
                if g == 0 or g == groups - 1:
                    rows = rim[min(g, 1), a, p]
                else:
                    rows = own[a, p, 8 * g - 8 : 8 * g, :]
                to_head, to_tail = head_lane(a, g), tail_lane(a, g)
                if to_head == to_tail + HALO:
                    first_moved = last_moved = pltpu.roll(both_ends(rows), to_head, 1)
                else:
                    first_moved = pltpu.roll(rows[:, 0:LANES], to_head, 1)
                    last_moved = pltpu.roll(rows[:, width - LANES : width], (to_tail + HALO) % LANES, 1)
                head = jnp.where((lane >= to_head) & (lane < to_head + HALO), first_moved, head)
                tail = jnp.where((lane >= to_tail) & (lane < to_tail + HALO), last_moved, tail)
        strips[0, p] = jnp.where(odd_z == 1, head, tail)
        strips[1, p] = jnp.where(odd_z == 1, tail, head)


def shifts(parts, step):
    if parts == 1:
        return (lambda v: [ahead(v[0], 1, step)]), (lambda v: [behind(v[0], 1, step)])
    return (lambda v: [v[1], ahead(v[0], 1)]), (lambda v: [behind(v[1], 1), v[0]])


def each(op, *lists):
    return [op(*values) for values in zip(*lists)]


def add(*lists):
    return each(lambda *values: functools.reduce(lambda x, y: x + y, values), *lists)


def times(x, y):
    return each(lambda v, w: v * w, x, y)


def solve(cells, own_at, own, out, seams):
    (src, cond, field, wx, wy, wz, vy, vz, diag, inv, sum8, cwx, cwy, cwz, cvy, cvz, cinv, res, q, cq, err) = cells
    total, parts, rows, lanes = cond.shape

    def load(ref, p):
        return [ref[p, i] for i in range(ref.shape[1])]

    def store(ref, p, values):
        for i, v in enumerate(values):
            ref[p, i] = v

    def reach(halo):
        low = max(1, own_at - halo)
        high = min(total, own_at + own + halo)
        return range((low + 1) // 2, (high + 1) // 2)

    fine = (1, *shifts(parts, 1))
    coarse = (2, *shifts(1, 3 - parts))
    zero = jnp.zeros((rows, lanes), jnp.float32)
    for ref in (q, cq, err, sum8):
        store(ref, 0, [zero] * ref.shape[1])

    even_row = lax.rem(lax.broadcasted_iota(jnp.int32, (rows, lanes), 0), 2) == 0
    even_lane = lax.rem(lax.broadcasted_iota(jnp.int32, (rows, lanes), 1), 2) == 0

    def gather(v):
        t = v[0] + (v[1] if parts == 2 else ahead(v[0], 1))
        return [t + ahead(t, 0)]

    for k in reach(HALO):
        store(sum8, k, gather(add(load(cond, 2 * k - 1), load(cond, 2 * k))))

    def weights(ref, p, level):
        step, ahead_z, behind_z = level
        c = load(ref, p)
        x = add(c, load(ref, p + 1))
        y, yb = ([v + shift(v, 0, step) for v in c] for shift in (ahead, behind))
        z, zb = add(c, ahead_z(c)), add(c, behind_z(c))
        k = add(add(c, load(ref, p - 1), x), add(y, yb), add(z, zb))
        return x, y, z, yb, zb, k, each(lambda v, w: jnp.where(v > 0.0, 1.0 / w, 0.0), c, k)

    low = reach(HALO - 2).start
    store(wx, 2 * low - 2, add(load(cond, 2 * low - 2), load(cond, 2 * low - 1)))
    store(cwx, low - 1, add(load(sum8, low - 1), load(sum8, low)))
    for k in reach(HALO - 2):
        for p in (2 * k - 1, 2 * k):
            for ref, v in zip((wx, wy, wz, vy, vz, diag, inv), weights(cond, p, fine)):
                store(ref, p, v)
        for ref, v in zip((cwx, cwy, cwz, cvy, cvz, None, cinv), weights(sum8, k, coarse)):
            if ref is not None:
                store(ref, k, v)

    def spread(v, p, refs, level):
        x, y, z, yb, zb = refs
        step, ahead_z, behind_z = level
        here = load(v, p)
        n = add(times(load(x, p - 1), load(v, p - 1)), times(load(x, p), load(v, p + 1)))
        n = add(n, times(load(y, p), [ahead(u, 0, step) for u in here]))
        n = add(n, times(load(yb, p), [behind(u, 0, step) for u in here]))
        return add(n, add(times(load(z, p), ahead_z(here)), times(load(zb, p), behind_z(here))))

    def smooth(v, p, refs, scale, level):
        n = times(load(scale, p), spread(v, p, refs, level))
        return each(lambda u, w: KEEP * u + SPREAD * w, load(v, p), n)

    def between(p):
        planes, along_y, along_z = seams
        here = load(field, p)
        r = load(src, p)

        def less(r, weights, there, where=None):
            flux = each(lambda w, u, v: w * (u - v), weights, here, there)
            return each(lambda x, y: x - (y if where is None else jnp.where(where, y, 0.0)), r, flux)

        if p in planes:
            r = less(r, load(wx, p), load(field, p + 1))
        if p - 1 in planes:
            r = less(r, load(wx, p - 1), load(field, p - 1))
        r = less(r, load(wy, p), [ahead(v, 0) for v in here], along_y[0])
        r = less(r, load(vy, p), [behind(v, 0) for v in here], along_y[1])
        if along_z is not None:
            r = less(r, load(wz, p), fine[1](here), along_z[0])
            r = less(r, load(vz, p), fine[2](here), along_z[1])
        return r

    around, coarse_around = (wx, wy, wz, vy, vz), (cwx, cwy, cwz, cvy, cvz)

    for it in range(ITERS):
        halo = 4 * (ITERS - 1 - it)
        for k in reach(halo + 2):
            found = []
            for p in (2 * k - 1, 2 * k):
                if it == 0:
                    r = between(p)
                else:
                    n = spread(err, p, around, fine)
                    r = each(lambda u, d, w, m: u - (d * w - m), load(res, p), load(diag, p), load(err, p), n)
                if it < ITERS - 1:
                    store(res, p, r)
                store(q, p, times(r, load(inv, p)))
                found.append(r)
            store(cq, k, times([4.0 * gather(add(*found))[0]], load(cinv, k)))

        for k in reach(halo):
            (c,) = smooth(cq, k, coarse_around, cinv, coarse)
            if parts == 1:
                c = jnp.where(even_lane, c, behind(c, 1))
            c = jnp.where(even_row, c, behind(c, 0))
            for p in (2 * k - 1, 2 * k):
                e = [u + c for u in smooth(q, p, around, inv, fine)]
                if it:
                    e = add(load(err, p), e)
                if it < ITERS - 1:
                    store(err, p, e)
                else:
                    out(p, add(load(field, p), e))


def layout(reflect, depth):
    return (1, depth + HALO + 2) if reflect else (1 + HALO, depth + 2 * HALO + 2)


def each_plane(reflect, depth, place):
    odd_x = is_odd("gx")
    own_at, _ = layout(reflect, depth)

    for p in range(depth):
        place(None, jnp.where(odd_x == 1, depth - 1 - p, p) if reflect else p, own_at + p)
    for p in range(HALO):
        if reflect:
            place(0, jnp.where(odd_x == 1, depth - 1 - p, p), own_at + depth + p)
            continue
        for i in range(2):
            above = odd_x == i
            at = jnp.where(above, p, depth - HALO + p)
            place(i, at, jnp.where(above, own_at + depth + p, 1 + p))


def x_seams(reflect, depth):
    own_at, _ = layout(reflect, depth)
    return (own_at + depth - 1,) if reflect else (own_at - 1, own_at + depth - 1)


def out_plane(reflect, depth, p):
    own_at, _ = layout(reflect, depth)
    at = p - own_at
    return jnp.where(is_odd("gx") == 1, depth - 1 - at, at) if reflect else at


def parting(width, lanes):
    column = lax.broadcasted_iota(jnp.int32, (width, 2 * lanes), 0)
    lane = lax.broadcasted_iota(jnp.int32, (width, 2 * lanes), 1)
    wanted = jnp.where(lane < lanes, 2 * lane, 2 * (lane - lanes) + 1)
    return jnp.where((column == wanted) & (wanted < width), 1.0, 0.0)


def ending(width):
    column = lax.broadcasted_iota(jnp.int32, (width, 2 * LANES), 0)
    lane = lax.broadcasted_iota(jnp.int32, (width, 2 * LANES), 1)
    lane = jnp.where(lane < LANES, lane, lane - LANES - LANES // 2)
    last = (lane >= 8) & (lane < 24) & (column == lane + width - 24)
    first = (lane >= 40) & (lane < 56) & (column == lane - 40)
    return jnp.where(last | first, 1.0, 0.0)


def rearranged(v, matrix):
    bf16, f32 = jnp.bfloat16, jnp.float32
    matrix = matrix.astype(bf16)
    result = None
    for _ in range(3):
        part = v.astype(bf16)
        v = v - part.astype(f32)
        moved = jnp.dot(part, matrix, preferred_element_type=f32)
        result = moved if result is None else result + moved
    return result


def interior(reflect, n_x, *refs):
    own, rim = refs[0], refs[1]
    near, near_rim = refs[2 : 2 + n_x], refs[2 + n_x : 2 + 2 * n_x]
    result, ends = refs[2 + 2 * n_x : 4 + 2 * n_x]
    whole, halves, *cells = refs[4 + 2 * n_x :]
    _, depth, inner, width = own.shape
    rows = inner + 2 * HALO
    lanes = cells[0].shape[3]

    def place(i, p_from, p_to):
        block, halo = (own, rim) if i is None else (near[i], near_rim[i])
        for a in range(3):
            tile = whole.at[a, p_to]
            tile[0:HALO, :] = halo[0, a, p_from]
            tile[HALO : HALO + inner, :] = block[a, p_from]
            tile[HALO + inner : rows, :] = halo[1, a, p_from]

    own_at, total = layout(reflect, depth)
    for a in range(3):
        for p in (0, total - 1):
            whole[a, p] = jnp.zeros((rows, width), jnp.float32)
    each_plane(reflect, depth, place)
    apart = parting(width, lanes)
    target = jnp.concatenate([apart, ending(width)], 1)
    for a in range(3):
        parts = rearranged(whole[a].reshape(total * rows, width), target).reshape(total, rows, -1)
        for i in range(2):
            cells[a][:, i] = parts[:, :, i * lanes : (i + 1) * lanes]
        low = parts[:, 0 : rows - 8, 2 * lanes : 2 * lanes + LANES]
        ends[a] = low + parts[:, 8:rows, 2 * lanes + LANES :]

    def out(p, v):
        for i in range(2):
            halves[p - own_at, :, i * lanes : (i + 1) * lanes] = v[i][HALO : rows - HALO, :]

    row = lax.broadcasted_iota(jnp.int32, (rows, lanes), 0)
    along_y = (row == HALO - 1) | (row == HALO + inner - 1), (row == HALO) | (row == HALO + inner)
    solve(cells, own_at, depth, out, (x_seams(reflect, depth), along_y, None))
    together = rearranged(halves[...].reshape(depth * inner, 2 * lanes), apart.T)
    together = together.reshape(depth, inner, width)
    for p in range(depth):
        result[out_plane(reflect, depth, own_at + p)] = together[p]


def edges(reflect, ends, inside, got_a, got_b, result, *cells):
    depth, inner, width = inside.shape
    groups = ends.shape[2] // 8
    odd_z = is_odd("grp")
    first_z, last_z = beyond("grp")
    lane = lax.broadcasted_iota(jnp.int32, (8, LANES), 1)
    half = LANES // 2
    own_at, total = layout(reflect, depth)
    for p in (0, total - 1):
        for a in range(3):
            cells[a][p, 0] = ends[a, p]

    def place(i, p_from, p_to):
        at_plane = p_from if i is None else (i + 1) * depth + p_from
        va, vb = got_a[at_plane], got_b[at_plane]
        right = jnp.where(last_z, 0.0, jnp.where(odd_z == 1, vb, va))
        left = jnp.where(first_z, 0.0, jnp.where(odd_z == 1, va, vb))
        side = lax.rem(lane, 16) >= 8
        lower = jnp.where(side, right, left)
        upper = jnp.where(side, pltpu.roll(right, LANES - 8, 1), pltpu.roll(left, 8, 1))
        middle = pltpu.roll(jnp.where(lane < half, upper, lower), half, 1)
        for a in range(3):
            for t, groups_of in enumerate((lower, middle, upper)):
                moved = groups_of if a == 1 else pltpu.roll(groups_of, (16 - 16 * a) % LANES, 1)
                here = lax.rem(lane, half)
                part = slice(8 * t, 8 * t + 8)
                cells[a][p_to, 0, part, :] = jnp.where((here >= 24) & (here < 40), moved, ends[a, p_to, part, :])

    each_plane(reflect, depth, place)

    def out(p, v):
        at = out_plane(reflect, depth, p)
        v = v[0][8:16]
        for i in range(2):
            part = slice(8 * i, 8 * i + 8)
            head = pltpu.roll(v, (LANES - 40 - half * i) % LANES, 1)
            tail = pltpu.roll(v, (LANES - 24 - half * i) % LANES, 1)
            for c in range(0, width, LANES):
                tile = inside[at, part, c : c + LANES]
                if c == 0:
                    tile = jnp.where(lane < HALO, head, tile)
                if c == width - LANES:
                    tile = jnp.where(lane >= LANES - HALO, tail, tile)
                result[at, part, c : c + LANES] = tile

    row = lax.broadcasted_iota(jnp.int32, ends.shape[2:], 0)
    lane_in_half = lax.rem(lax.broadcasted_iota(jnp.int32, ends.shape[2:], 1), half)
    upper_half = lax.broadcasted_iota(jnp.int32, ends.shape[2:], 1) >= half
    face = jnp.where(upper_half, inner, HALO)
    along_z = tuple((lane_in_half == at) | (lane_in_half == at + 16) for at in (23, 24))
    solve(cells, own_at, depth, out, (x_seams(reflect, depth), (row == face - 1, row == face), along_z))


def shards(sizes, source_term, conductivity, initial_field):
    depth, inner, width = source_term.shape
    assert inner == 16 and depth >= HALO and depth % 2 == 0 and width % LANES == 0
    rows = inner + 2 * HALO
    f32 = jnp.float32
    params = pltpu.CompilerParams(vmem_limit_bytes=48 * 1024 * 1024)
    args = (source_term, conductivity, initial_field)

    def exchange(values, axis):
        over, rounds = swaps(axis, sizes)
        found = [lax.ppermute(v, over, pairs) for v, pairs in reversed(list(zip(values, rounds)))]
        return found[::-1] + [jnp.zeros_like(v) for v in values[len(found) :]]

    def work(parts, rows, lanes):
        total = layout(reflect, depth)[1]
        fine = pltpu.VMEM((total, parts, rows, lanes), f32)
        coarse = pltpu.VMEM((total // 2 + 1, 1, rows, lanes), f32)
        return [fine] * 10 + [coarse] * 7 + [fine] * 2 + [coarse] + [fine]

    reflect = sizes["gx"] == 2
    n_x = 1 if reflect else 2
    args = [pltpu.with_memory_space_constraint(v, pltpu.HBM) for v in args]
    face = jax.ShapeDtypeStruct((depth + depth // 2 + n_x + 1, HALO, width), f32)
    own, *msgs = pl.pallas_call(
        functools.partial(prepare, reflect),
        out_shape=(jax.ShapeDtypeStruct((3, depth, inner, width), f32), face, face),
        in_specs=[pl.BlockSpec(memory_space=pltpu.HBM)] * 3, out_specs=(VMEM,) * 3,
        scratch_shapes=[pltpu.SemaphoreType.DMA((3,))], compiler_params=params, name="prepare",
    )(*args)
    got = exchange(msgs, "gy")
    near = exchange([own] * n_x, "gx")
    strips, rim = pl.pallas_call(
        functools.partial(pack_columns, reflect),
        out_shape=(
            jax.ShapeDtypeStruct((2, depth, 8, LANES), f32),
            jax.ShapeDtypeStruct((2, 3, depth, HALO, width), f32),
        ),
        in_specs=[VMEM] * 3, out_specs=(VMEM, VMEM),
        compiler_params=params, name="pack_columns",
    )(own, *got)
    strips = jnp.concatenate([strips] + exchange([strips] * n_x, "gx"), axis=1)
    strips, rim = lax.optimization_barrier((strips, rim))
    near_rim = exchange([rim] * n_x, "gx")
    strips = exchange([strips[0], strips[1]], "grp")

    block = jax.ShapeDtypeStruct(source_term.shape, f32)
    total = layout(reflect, depth)[1]
    lanes = -(-width // (2 * LANES)) * LANES
    apart = [pltpu.VMEM((3, total, rows, width), f32), pltpu.VMEM((depth, inner, 2 * lanes), f32)]
    inside, ends = pl.pallas_call(
        functools.partial(interior, reflect, n_x),
        out_shape=(block, jax.ShapeDtypeStruct((3, total, rows - 8, LANES), f32)),
        in_specs=[VMEM] * (2 + 2 * n_x), out_specs=(VMEM, VMEM), scratch_shapes=apart + work(2, rows, lanes),
        compiler_params=params, name="interior",
        cost_estimate=pl.CostEstimate(flops=20_000_000, bytes_accessed=20_000_000, transcendentals=0),
    )(own, rim, *near, *near_rim)
    inside, ends, *strips = lax.optimization_barrier((inside, ends, *strips[::-1]))
    strips = strips[::-1]
    return pl.pallas_call(
        functools.partial(edges, reflect),
        out_shape=block,
        in_specs=[VMEM] * 4, out_specs=VMEM, scratch_shapes=work(1, rows - 8, LANES),
        compiler_params=params, name="edges",
    )(ends, inside, *strips)


def solution(mesh):
    spec = P("gx", "gy", "grp")
    return jax.shard_map(
        functools.partial(shards, dict(mesh.shape)),
        mesh=mesh,
        in_specs=(spec,) * 3,
        out_specs=spec,
        check_vma=False,
    )
```

```python
import functools

import jax
import jax.numpy as jnp
from jax import lax
from jax.experimental import pallas as pl
from jax.experimental.pallas import tpu as pltpu
from jax.sharding import PartitionSpec as P

ITERS = 2
HALO = 4 * ITERS
LANES = 128
KEEP = 48.0 / 41.0
SPREAD = 32.0 / 41.0
VMEM = pl.BlockSpec(memory_space=pltpu.VMEM)


def ahead(v, axis, n=1):
    return pltpu.roll(v, v.shape[axis] - n, axis)


def behind(v, axis, n=1):
    return pltpu.roll(v, n, axis)


def swaps(axis, sizes):
    count, fill = sizes[axis], sizes["gx"]
    over = [name for name in sizes if name in (axis, "gx")]
    filled = axis != "gx" and fill % 2 == 0

    def at(i, k):
        return i * fill + k if over[0] == axis else k * count + i

    rounds = []
    for start in (0, 1):
        pairs = [(i, i + 1) for i in range(start, count - 1, 2)]
        left = set(range(count)) - {i for pair in pairs for i in pair}
        if not pairs:
            continue
        if filled:
            pairs = [(at(i, k), at(j, k)) for i, j in pairs for k in range(fill)]
            pairs += [(at(i, k), at(i, k + 1)) for i in sorted(left) for k in range(0, fill, 2)]
        rounds.append(pairs + [(j, i) for i, j in pairs])
    return (tuple(over) if filled else axis), rounds


def is_odd(axis):
    return lax.rem(lax.axis_index(axis), 2)


def beyond(axis):
    at = lax.axis_index(axis)
    return at == 0, at == lax.axis_size(axis) - 1


def is_odd(axis):
    return lax.rem(lax.axis_index(axis), 2)


def far_row(high, distance):
    if isinstance(high, bool):
        return HALO - distance if high else distance - 1
    return jnp.where(high, HALO - distance, distance - 1)


def shifted_rows(high, v, n):
    if isinstance(high, bool):
        return pltpu.roll(v, HALO - n if high else n, 0)
    return jnp.where(high, pltpu.roll(v, HALO - n, 0), pltpu.roll(v, n, 0))


def inward(high, v):
    return shifted_rows(high, v, HALO - 1)


def both_ends(rows):
    width = rows.shape[1]
    lane = lax.broadcasted_iota(jnp.int32, (rows.shape[0], LANES), 1)
    return jnp.where(lane < LANES // 2, rows[:, 0:LANES], rows[:, width - LANES : width])


def prepare(reflect, s, c, f, own, first, second, sems):
    copies = [pltpu.make_async_copy(ref, own.at[a], sems.at[a]) for a, ref in enumerate((s, c, f))]
    for copy in copies:
        copy.start()
    for copy in copies:
        copy.wait()
    _, depth, inner, width = own.shape
    row = lax.broadcasted_iota(jnp.int32, (inner, width), 0)
    column = lax.broadcasted_iota(jnp.int32, (inner, width), 1)
    outer = jnp.where(is_odd("gx") == 1, depth - 1, 0)
    conds, fields = ([own[a, p] for p in range(depth)] for a in (1, 2))
    next_conds, next_fields = ([ahead(v, 1) for v in values] for values in (conds, fields))
    along_z = [
        jnp.where(column < width - 1, (c + c_next) * (f - f_next), 0.0)
        for c, f, c_next, f_next in zip(conds, fields, next_conds, next_fields)
    ]
    arriving = [behind(v, 1) for v in along_z]
    for p, (cond, field) in enumerate(zip(conds, fields)):
        along_y = jnp.where(row < inner - 1, (cond + ahead(cond, 0)) * (field - ahead(field, 0)), 0.0)
        total = (along_y - behind(along_y, 0)) + (along_z[p] - arriving[p])
        for other in (p - 1, p + 1):
            if 0 <= other < depth:
                total += (cond + conds[other]) * (field - fields[other])
        if reflect and p in (0, depth - 1):
            total += jnp.where(outer == p, cond * field, 0.0)
        own[0, p] = 2.0 * own[0, p] - total

    odd = is_odd("gy")
    row = lax.broadcasted_iota(jnp.int32, (HALO, width), 0)
    lane = lax.broadcasted_iota(jnp.int32, (HALO, LANES), 1)
    for message, high in ((first, odd == 0), (second, odd == 1)):
        rows = pl.ds(pl.multiple_of(jnp.where(high, inner - HALO, 0), 8), HALO)
        at = functools.partial(far_row, high)
        sides = jnp.zeros((HALO, LANES), jnp.float32)
        for p in range(0, depth, 2):
            sums = own[1, p, rows, :] + own[1, p + 1, rows, :]
            sums = sums + inward(high, sums)
            rests = own[0, p, rows, :] + own[0, p + 1, rows, :]
            rests = shifted_rows(high, rests + inward(high, rests), 2)
            for i, seventh in enumerate((sums, rests)):
                field = own[2, p + i, rows, :]
                cond = jnp.where(row == at(7), seventh, own[1, p + i, rows, :])
                message[p + i] = jnp.where(row == at(8), inward(high, field), cond)
                ends = pltpu.roll(both_ends(field), 2 * (p + i) + 1, 1)
                sides = jnp.where(lane // 2 == p + i, ends, sides)
            near = jnp.where(high, HALO - 1 - row, row) < 4
            message[depth + p // 2] = jnp.where(near, own[0, p, rows, :], pltpu.roll(own[0, p + 1, rows, :], 4, 0))
        planes = depth + depth // 2
        if reflect:
            message[planes] = own[2, depth - 1 - outer, rows, :]
        else:
            message[planes] = own[2, 0, rows, :]
            message[planes + 1] = own[2, depth - 1, rows, :]
        message[message.shape[0] - 1] = jnp.zeros((HALO, width), jnp.float32)
        message[message.shape[0] - 1, :, 0:LANES] = sides


def head_lane(a, g):
    return 8 + 16 * a + LANES // 2 * (g % 2) + 8 * (g // 2)


def tail_lane(a, g):
    return 8 + 16 * a + LANES // 2 * (g % 2) + 8 * (1 - g // 2)


def pack_columns(reflect, own, got_a, got_b, strips, rim):
    odd_y, odd_z = is_odd("gy"), is_odd("grp")
    first_y, last_y = beyond("gy")
    _, depth, inner, width = own.shape
    groups = inner // 8 + 2
    odd_x = is_odd("gx")
    lane = lax.broadcasted_iota(jnp.int32, (8, LANES), 1)
    row = lax.broadcasted_iota(jnp.int32, (8, width), 0)
    wide = lax.broadcasted_iota(jnp.int32, (8, width), 1)

    def spread_out(v):
        return jnp.concatenate([v] * (width // LANES), 1)

    for p in range(depth):
        for side, (low, outside) in enumerate(((True, first_y), (False, last_y))):

            at = functools.partial(far_row, low)

            def take(i):
                strip = jnp.where(odd_y == (1 if low else 0), got_a[i], got_b[i])
                return jnp.where(outside, 0.0, strip)

            cond, mixed = take(p), take(depth + p // 2)
            g = mixed if p % 2 == 0 else pltpu.roll(mixed, 4, 0)
            g = jnp.where(row >= 4 if low else row < 4, g, 0.0)
            if p % 2:
                g = jnp.where(row == at(5), shifted_rows(low, cond, HALO - 2), g)
            sides = take(got_a.shape[0] - 1)[:, 0:LANES]
            ends = spread_out(pltpu.roll(sides, LANES - 1 - 2 * p, 1))
            field = jnp.where((wide == 0) | (wide == width - 1), ends, 0.0)
            field = jnp.where(row == at(1), shifted_rows(low, cond, 1), field)
            planes = depth + depth // 2
            if reflect and p in (0, depth - 1):
                field = jnp.where(odd_x == (1 if p == 0 else 0), take(planes), field)
            elif not reflect and p in (0, depth - 1):
                field = take(planes + (0 if p == 0 else 1))
            cond = jnp.where(row == at(8), 0.0, cond)
            if p % 2:
                cond = jnp.where(row == at(7), 0.0, cond)
            rim[side, 0, p] = g
            rim[side, 1, p] = cond
            rim[side, 2, p] = field
    moved = {}
    for p in range(depth):
        for a in range(3):
            for g in range(groups):
                if g == 0 or g == groups - 1:
                    rows = rim[min(g, 1), a, p]
                else:
                    rows = own[a, p, 8 * g - 8 : 8 * g, :]
                to_head, to_tail = head_lane(a, g), tail_lane(a, g)
                if to_head == to_tail + HALO:
                    ends = pltpu.roll(both_ends(rows), to_head, 1)
                    moved[p, a, g] = ends, ends
                else:
                    last = pltpu.roll(rows[:, width - LANES : width], (to_tail + HALO) % LANES, 1)
                    moved[p, a, g] = pltpu.roll(rows[:, 0:LANES], to_head, 1), last
    for p in range(depth):
        head = tail = jnp.zeros((8, LANES), jnp.float32)
        for a in range(3):
            for g in range(groups):
                to_head, to_tail = head_lane(a, g), tail_lane(a, g)
                head = jnp.where((lane >= to_head) & (lane < to_head + HALO), moved[p, a, g][0], head)
                tail = jnp.where((lane >= to_tail) & (lane < to_tail + HALO), moved[p, a, g][1], tail)
        strips[0, p] = jnp.where(odd_z == 1, head, tail)
        strips[1, p] = jnp.where(odd_z == 1, tail, head)


def shifts(parts, step):
    if parts == 1:
        return (lambda v: [ahead(v[0], 1, step)]), (lambda v: [behind(v[0], 1, step)])
    return (lambda v: [v[1], ahead(v[0], 1)]), (lambda v: [behind(v[1], 1), v[0]])


def each(op, *lists):
    return [op(*values) for values in zip(*lists)]


def add(*lists):
    return each(lambda *values: functools.reduce(lambda x, y: x + y, values), *lists)


def times(x, y):
    return each(lambda v, w: v * w, x, y)


def solve(cells, own_at, own, out, seams):
    (src, cond, field, wx, wy, wz, vy, vz, diag, inv, sum8, cwx, cwy, cwz, cvy, cvz, cinv, res, q, cq, err) = cells
    total, parts, rows, lanes = cond.shape

    def load(ref, p):
        return [ref[p, i] for i in range(ref.shape[1])]

    def store(ref, p, values):
        for i, v in enumerate(values):
            ref[p, i] = v

    def reach(halo):
        low = max(1, own_at - halo)
        high = min(total, own_at + own + halo)
        return range((low + 1) // 2, (high + 1) // 2)

    fine = (1, *shifts(parts, 1))
    coarse = (2, *shifts(1, 3 - parts))
    zero = jnp.zeros((rows, lanes), jnp.float32)
    for ref in (q, cq, err, sum8):
        store(ref, 0, [zero] * ref.shape[1])

    even_row = lax.rem(lax.broadcasted_iota(jnp.int32, (rows, lanes), 0), 2) == 0
    even_lane = lax.rem(lax.broadcasted_iota(jnp.int32, (rows, lanes), 1), 2) == 0

    def turned(ref, planes, level):
        here = {p: load(ref, p) for p in planes}
        return {p: (level[1](v), level[2](v)) for p, v in here.items()}

    def planes_of(blocks):
        return [p for k in blocks for p in (2 * k - 1, 2 * k)]

    def gather(sums):
        sums = {k: [v[0] + ahead(v[0], 0)] if parts == 1 else [v[0] + v[1]] for k, v in sums.items()}
        if parts == 1:
            return {k: [v[0] + u] for (k, v), u in zip(sums.items(), [ahead(v[0], 1) for v in sums.values()])}
        return {k: [v[0] + ahead(v[0], 0)] for k, v in sums.items()}

    for k, v in gather({k: add(load(cond, 2 * k - 1), load(cond, 2 * k)) for k in reach(HALO)}).items():
        store(sum8, k, v)

    def weights(ref, p, level, around_z):
        step = level[0]
        c = load(ref, p)
        x = add(c, load(ref, p + 1))
        y, yb = ([v + shift(v, 0, step) for v in c] for shift in (ahead, behind))
        z, zb = (add(c, v) for v in around_z)
        k = add(add(c, load(ref, p - 1), x), add(y, yb), add(z, zb))
        return x, y, z, yb, zb, k, each(lambda v, w: jnp.where(v > 0.0, 1.0 / w, 0.0), c, k)

    low = reach(HALO - 2).start
    store(wx, 2 * low - 2, add(load(cond, 2 * low - 2), load(cond, 2 * low - 1)))
    store(cwx, low - 1, add(load(sum8, low - 1), load(sum8, low)))
    z_fine = turned(cond, planes_of(reach(HALO - 2)), fine)
    z_coarse = turned(sum8, reach(HALO - 2), coarse)
    for k in reach(HALO - 2):
        for p in (2 * k - 1, 2 * k):
            for ref, v in zip((wx, wy, wz, vy, vz, diag, inv), weights(cond, p, fine, z_fine[p])):
                store(ref, p, v)
        for ref, v in zip((cwx, cwy, cwz, cvy, cvz, None, cinv), weights(sum8, k, coarse, z_coarse[k])):
            if ref is not None:
                store(ref, k, v)

    def spread(v, p, refs, level, around_z):
        x, y, z, yb, zb = refs
        step = level[0]
        here = load(v, p)
        n = add(times(load(x, p - 1), load(v, p - 1)), times(load(x, p), load(v, p + 1)))
        n = add(n, times(load(y, p), [ahead(u, 0, step) for u in here]))
        n = add(n, times(load(yb, p), [behind(u, 0, step) for u in here]))
        return add(n, add(times(load(z, p), around_z[0]), times(load(zb, p), around_z[1])))

    def smooth(v, p, refs, scale, level, around_z):
        n = times(load(scale, p), spread(v, p, refs, level, around_z))
        return each(lambda u, w: KEEP * u + SPREAD * w, load(v, p), n)

    def between(p, around_z):
        planes, along_y, along_z = seams
        here = load(field, p)
        r = load(src, p)

        def less(r, weights, there, where=None):
            flux = each(lambda w, u, v: w * (u - v), weights, here, there)
            return each(lambda x, y: x - (y if where is None else jnp.where(where, y, 0.0)), r, flux)

        if p in planes:
            r = less(r, load(wx, p), load(field, p + 1))
        if p - 1 in planes:
            r = less(r, load(wx, p - 1), load(field, p - 1))
        r = less(r, load(wy, p), [ahead(v, 0) for v in here], along_y[0])
        r = less(r, load(vy, p), [behind(v, 0) for v in here], along_y[1])
        if along_z is not None:
            r = less(r, load(wz, p), around_z[0], along_z[0])
            r = less(r, load(vz, p), around_z[1], along_z[1])
        return r

    around, coarse_around = (wx, wy, wz, vy, vz), (cwx, cwy, cwz, cvy, cvz)

    for it in range(ITERS):
        halo = 4 * (ITERS - 1 - it)
        blocks = reach(halo + 2)
        rounds = turned(err if it else field, planes_of(blocks), fine) if it or seams[2] is not None else {}
        sums = {}
        for k in blocks:
            found = []
            for p in (2 * k - 1, 2 * k):
                if it == 0:
                    r = between(p, rounds.get(p))
                else:
                    n = spread(err, p, around, fine, rounds[p])
                    r = each(lambda u, d, w, m: u - (d * w - m), load(res, p), load(diag, p), load(err, p), n)
                if it < ITERS - 1:
                    store(res, p, r)
                store(q, p, times(r, load(inv, p)))
                found.append(r)
            sums[k] = add(*found)
        near = reach(halo)
        sums = gather(sums)
        rounds = turned(q, planes_of(near), fine)
        for k, v in sums.items():
            store(cq, k, times([4.0 * v[0]], load(cinv, k)))
        coarse_rounds = turned(cq, near, coarse)
        found = {k: smooth(cq, k, coarse_around, cinv, coarse, coarse_rounds[k])[0] for k in near}
        if parts == 1:
            beside = {k: behind(c, 1) for k, c in found.items()}
            found = {k: jnp.where(even_lane, c, beside[k]) for k, c in found.items()}
        smoothed = {p: smooth(q, p, around, inv, fine, rounds[p]) for p in planes_of(near)}
        for k in near:
            c = jnp.where(even_row, found[k], behind(found[k], 0))
            for p in (2 * k - 1, 2 * k):
                e = [u + c for u in smoothed[p]]
                if it:
                    e = add(load(err, p), e)
                if it < ITERS - 1:
                    store(err, p, e)
                else:
                    out(p, add(load(field, p), e))


def layout(reflect, depth):
    return (1, depth + HALO + 2) if reflect else (1 + HALO, depth + 2 * HALO + 2)


def each_plane(reflect, depth, place):
    odd_x = is_odd("gx")
    own_at, _ = layout(reflect, depth)

    for p in range(depth):
        place(None, jnp.where(odd_x == 1, depth - 1 - p, p) if reflect else p, own_at + p)
    for p in range(HALO):
        if reflect:
            place(0, jnp.where(odd_x == 1, depth - 1 - p, p), own_at + depth + p)
            continue
        for i in range(2):
            above = odd_x == i
            at = jnp.where(above, p, depth - HALO + p)
            place(i, at, jnp.where(above, own_at + depth + p, 1 + p))


def x_seams(reflect, depth):
    own_at, _ = layout(reflect, depth)
    return (own_at + depth - 1,) if reflect else (own_at - 1, own_at + depth - 1)


def out_plane(reflect, depth, p):
    own_at, _ = layout(reflect, depth)
    at = p - own_at
    return jnp.where(is_odd("gx") == 1, depth - 1 - at, at) if reflect else at


def parting(width, lanes):
    column = lax.broadcasted_iota(jnp.int32, (width, 2 * lanes), 0)
    lane = lax.broadcasted_iota(jnp.int32, (width, 2 * lanes), 1)
    wanted = jnp.where(lane < lanes, 2 * lane, 2 * (lane - lanes) + 1)
    return jnp.where((column == wanted) & (wanted < width), 1.0, 0.0)


def ending(width):
    column = lax.broadcasted_iota(jnp.int32, (width, 2 * LANES), 0)
    lane = lax.broadcasted_iota(jnp.int32, (width, 2 * LANES), 1)
    lane = jnp.where(lane < LANES, lane, lane - LANES - LANES // 2)
    last = (lane >= 8) & (lane < 24) & (column == lane + width - 24)
    first = (lane >= 40) & (lane < 56) & (column == lane - 40)
    return jnp.where(last | first, 1.0, 0.0)


def rearranged(v, matrix):
    bf16, f32 = jnp.bfloat16, jnp.float32
    matrix = matrix.astype(bf16)
    result = None
    for _ in range(3):
        part = v.astype(bf16)
        v = v - part.astype(f32)
        moved = jnp.dot(part, matrix, preferred_element_type=f32)
        result = moved if result is None else result + moved
    return result


def interior(reflect, n_x, *refs):
    own, rim = refs[0], refs[1]
    near, near_rim = refs[2 : 2 + n_x], refs[2 + n_x : 2 + 2 * n_x]
    result, ends = refs[2 + 2 * n_x : 4 + 2 * n_x]
    whole, halves, *cells = refs[4 + 2 * n_x :]
    _, depth, inner, width = own.shape
    rows = inner + 2 * HALO
    lanes = cells[0].shape[3]

    def place(i, p_from, p_to):
        block, halo = (own, rim) if i is None else (near[i], near_rim[i])
        for a in range(3):
            tile = whole.at[a, p_to]
            tile[0:HALO, :] = halo[0, a, p_from]
            tile[HALO : HALO + inner, :] = block[a, p_from]
            tile[HALO + inner : rows, :] = halo[1, a, p_from]

    own_at, total = layout(reflect, depth)
    for a in range(3):
        for p in (0, total - 1):
            whole[a, p] = jnp.zeros((rows, width), jnp.float32)
    each_plane(reflect, depth, place)
    apart = parting(width, lanes)
    target = jnp.concatenate([apart, ending(width)], 1)
    for a in range(3):
        parts = rearranged(whole[a].reshape(total * rows, width), target).reshape(total, rows, -1)
        for i in range(2):
            cells[a][:, i] = parts[:, :, i * lanes : (i + 1) * lanes]
        low = parts[:, 0 : rows - 8, 2 * lanes : 2 * lanes + LANES]
        ends[a] = low + parts[:, 8:rows, 2 * lanes + LANES :]

    def out(p, v):
        for i in range(2):
            halves[p - own_at, :, i * lanes : (i + 1) * lanes] = v[i][HALO : rows - HALO, :]

    row = lax.broadcasted_iota(jnp.int32, (rows, lanes), 0)
    along_y = (row == HALO - 1) | (row == HALO + inner - 1), (row == HALO) | (row == HALO + inner)
    solve(cells, own_at, depth, out, (x_seams(reflect, depth), along_y, None))
    together = rearranged(halves[...].reshape(depth * inner, 2 * lanes), apart.T)
    together = together.reshape(depth, inner, width)
    for p in range(depth):
        result[out_plane(reflect, depth, own_at + p)] = together[p]


def edges(reflect, ends, inside, got_a, got_b, result, staged, sems, *cells):
    depth, inner, width = inside.shape
    odd_z = is_odd("grp")
    first_z, last_z = beyond("grp")
    lane = lax.broadcasted_iota(jnp.int32, (8, LANES), 1)
    half = LANES // 2
    own_at, total = layout(reflect, depth)
    for p in (0, total - 1):
        for a in range(3):
            cells[a][p, 0] = ends[a, p]

    windows = []

    def place(i, p_from, p_to):
        at_plane = p_from if i is None else (i + 1) * depth + p_from
        va, vb = got_a[at_plane], got_b[at_plane]
        right = jnp.where(last_z, 0.0, jnp.where(odd_z == 1, vb, va))
        left = jnp.where(first_z, 0.0, jnp.where(odd_z == 1, va, vb))
        windows.append((p_to, right, left, pltpu.roll(right, LANES - 8, 1), pltpu.roll(left, 8, 1)))

    here = lax.rem(lane, half)
    in_halo = (here >= 24) & (here < 40)
    each_plane(reflect, depth, place)
    side = lax.rem(lane, 16) >= 8
    groups = []
    for p, right, left, right_moved, left_moved in windows:
        lower, upper = jnp.where(side, right, left), jnp.where(side, right_moved, left_moved)
        groups.append((p, lower, pltpu.roll(jnp.where(lane < half, upper, lower), half, 1), upper))
    for a in (1, 0, 2):
        for p, *tiles in groups:
            for t, tile in enumerate(tiles):
                moved = tile if a == 1 else pltpu.roll(tile, (16 - 16 * a) % LANES, 1)
                part = slice(8 * t, 8 * t + 8)
                cells[a][p, 0, part, :] = jnp.where(in_halo, moved, ends[a, p, part, :])

    row = lax.broadcasted_iota(jnp.int32, ends.shape[2:], 0)
    lane_in_half = lax.rem(lax.broadcasted_iota(jnp.int32, ends.shape[2:], 1), half)
    upper_half = lax.broadcasted_iota(jnp.int32, ends.shape[2:], 1) >= half
    face = jnp.where(upper_half, inner, HALO)
    along_z = tuple((lane_in_half == at) | (lane_in_half == at + 16) for at in (23, 24))
    finals = []
    solve(cells, own_at, depth, lambda p, v: finals.append((p - own_at, v[0][8:16])), (x_seams(reflect, depth), (row == face - 1, row == face), along_z))
    moved = [
        (p, i, pltpu.roll(v, (LANES - 40 - half * i) % LANES, 1), pltpu.roll(v, (LANES - 24 - half * i) % LANES, 1))
        for p, v in finals
        for i in range(2)
    ]
    copies = []
    for p, i, head, tail in moved:
        at, part = out_plane(reflect, depth, own_at + p), slice(8 * i, 8 * i + 8)
        for c in range(0, width, LANES):
            tile = inside[at, part, c : c + LANES]
            if c == 0:
                tile = jnp.where(lane < HALO, head, tile)
            if c == width - LANES:
                tile = jnp.where(lane >= LANES - HALO, tail, tile)
            staged[p, part, c : c + LANES] = tile
        if i:
            copies.append(pltpu.make_async_copy(staged.at[p], result.at[at], sems.at[p]))
            copies[-1].start()
    for copy in copies:
        copy.wait()


def shards(sizes, source_term, conductivity, initial_field):
    depth, inner, width = source_term.shape
    assert inner == 16 and depth >= HALO and depth % 2 == 0 and width % LANES == 0
    rows = inner + 2 * HALO
    f32 = jnp.float32
    params = pltpu.CompilerParams(vmem_limit_bytes=48 * 1024 * 1024)
    args = (source_term, conductivity, initial_field)

    def exchange(values, axis):
        over, rounds = swaps(axis, sizes)
        found = [lax.ppermute(v, over, pairs) for v, pairs in reversed(list(zip(values, rounds)))]
        return found[::-1] + [jnp.zeros_like(v) for v in values[len(found) :]]

    def work(parts, rows, lanes):
        total = layout(reflect, depth)[1]
        fine = pltpu.VMEM((total, parts, rows, lanes), f32)
        coarse = pltpu.VMEM((total // 2 + 1, 1, rows, lanes), f32)
        return [fine] * 10 + [coarse] * 7 + [fine] * 2 + [coarse] + [fine]

    reflect = sizes["gx"] == 2
    n_x = 1 if reflect else 2
    args = [pltpu.with_memory_space_constraint(v, pltpu.HBM) for v in args]
    face = jax.ShapeDtypeStruct((depth + depth // 2 + n_x + 1, HALO, width), f32)
    own, *msgs = pl.pallas_call(
        functools.partial(prepare, reflect),
        out_shape=(jax.ShapeDtypeStruct((3, depth, inner, width), f32), face, face),
        in_specs=[pl.BlockSpec(memory_space=pltpu.HBM)] * 3, out_specs=(VMEM,) * 3,
        scratch_shapes=[pltpu.SemaphoreType.DMA((3,))], compiler_params=params, name="prepare",
    )(*args)
    got = exchange(msgs, "gy")
    near = exchange([own] * n_x, "gx")
    strips, rim = pl.pallas_call(
        functools.partial(pack_columns, reflect),
        out_shape=(
            jax.ShapeDtypeStruct((2, depth, 8, LANES), f32),
            jax.ShapeDtypeStruct((2, 3, depth, HALO, width), f32),
        ),
        in_specs=[VMEM] * 3, out_specs=(VMEM, VMEM),
        compiler_params=params, name="pack_columns",
    )(own, *got)
    strips = jnp.concatenate([strips] + exchange([strips] * n_x, "gx"), axis=1)
    strips, rim = lax.optimization_barrier((strips, rim))
    near_rim = exchange([rim] * n_x, "gx")
    strips = exchange([strips[0], strips[1]], "grp")

    block = jax.ShapeDtypeStruct(source_term.shape, f32)
    total = layout(reflect, depth)[1]
    lanes = -(-width // (2 * LANES)) * LANES
    apart = [pltpu.VMEM((3, total, rows, width), f32), pltpu.VMEM((depth, inner, 2 * lanes), f32)]
    inside, ends = pl.pallas_call(
        functools.partial(interior, reflect, n_x),
        out_shape=(block, jax.ShapeDtypeStruct((3, total, rows - 8, LANES), f32)),
        in_specs=[VMEM] * (2 + 2 * n_x), out_specs=(VMEM, VMEM), scratch_shapes=apart + work(2, rows, lanes),
        compiler_params=params, name="interior",
        cost_estimate=pl.CostEstimate(flops=20_000_000, bytes_accessed=20_000_000, transcendentals=0),
    )(own, rim, *near, *near_rim)
    inside, ends, *strips = lax.optimization_barrier((inside, ends, *strips[::-1]))
    strips = strips[::-1]
    return pl.pallas_call(
        functools.partial(edges, reflect),
        out_shape=block,
        in_specs=[VMEM] * 4, out_specs=pl.BlockSpec(memory_space=pltpu.HBM),
        scratch_shapes=[pltpu.VMEM((depth, inner, width), f32), pltpu.SemaphoreType.DMA((depth,))] + work(1, rows - 8, LANES),
        compiler_params=params, name="edges",
    )(ends, inside, *strips)


def solution(mesh):
    spec = P("gx", "gy", "grp")
    return jax.shard_map(
        functools.partial(shards, dict(mesh.shape)),
        mesh=mesh,
        in_specs=(spec,) * 3,
        out_specs=spec,
        check_vma=False,
    )
```

```python
import functools

import jax
import jax.numpy as jnp
from jax import lax
from jax.experimental import pallas as pl
from jax.experimental.pallas import tpu as pltpu
from jax.sharding import PartitionSpec as P

ITERS = 2
HALO = 4 * ITERS
LANES = 128
KEEP = 48.0 / 41.0
SPREAD = 32.0 / 41.0
VMEM = pl.BlockSpec(memory_space=pltpu.VMEM)


def ahead(v, axis, n=1):
    return pltpu.roll(v, v.shape[axis] - n, axis)


def behind(v, axis, n=1):
    return pltpu.roll(v, n, axis)


def swaps(axis, sizes):
    count, fill = sizes[axis], sizes["gx"]
    over = [name for name in sizes if name in (axis, "gx")]
    filled = axis != "gx" and fill % 2 == 0

    def at(i, k):
        return i * fill + k if over[0] == axis else k * count + i

    rounds = []
    for start in (0, 1):
        pairs = [(i, i + 1) for i in range(start, count - 1, 2)]
        left = set(range(count)) - {i for pair in pairs for i in pair}
        if not pairs:
            continue
        if filled:
            pairs = [(at(i, k), at(j, k)) for i, j in pairs for k in range(fill)]
            pairs += [(at(i, k), at(i, k + 1)) for i in sorted(left) for k in range(0, fill, 2)]
        rounds.append(pairs + [(j, i) for i, j in pairs])
    return (tuple(over) if filled else axis), rounds


def crossing(sizes):
    names = list(sizes)

    def at(**place):
        index = 0
        for name in names:
            index = index * sizes[name] + place[name]
        return index

    last = sizes["grp"] - 1
    pairs = [
        (at(grp=g, gx=1, gy=y), at(grp=g + 1, gx=0, gy=y)) for g in range(last) for y in range(sizes["gy"])
    ]
    pairs += [
        (at(grp=g, gx=x, gy=y), at(grp=g, gx=x, gy=y + 1))
        for g, x in ((0, 0), (last, 1))
        for y in range(0, sizes["gy"] - 1, 2)
    ]
    return pairs + [(j, i) for i, j in pairs]


def is_odd(axis):
    return lax.rem(lax.axis_index(axis), 2)


def beyond(axis):
    at = lax.axis_index(axis)
    return at == 0, at == lax.axis_size(axis) - 1


def is_odd(axis):
    return lax.rem(lax.axis_index(axis), 2)


def far_row(high, distance):
    if isinstance(high, bool):
        return HALO - distance if high else distance - 1
    return jnp.where(high, HALO - distance, distance - 1)


def shifted_rows(high, v, n):
    if isinstance(high, bool):
        return pltpu.roll(v, HALO - n if high else n, 0)
    return jnp.where(high, pltpu.roll(v, HALO - n, 0), pltpu.roll(v, n, 0))


def inward(high, v):
    return shifted_rows(high, v, HALO - 1)


def both_ends(rows):
    width = rows.shape[1]
    lane = lax.broadcasted_iota(jnp.int32, (rows.shape[0], LANES), 1)
    return jnp.where(lane < LANES // 2, rows[:, 0:LANES], rows[:, width - LANES : width])


def prepare(reflect, s, c, f, own, first, second, sems):
    copies = [pltpu.make_async_copy(ref, own.at[a], sems.at[a]) for a, ref in enumerate((s, c, f))]
    for copy in copies:
        copy.start()
    for copy in copies:
        copy.wait()
    _, depth, inner, width = own.shape
    row = lax.broadcasted_iota(jnp.int32, (inner, width), 0)
    column = lax.broadcasted_iota(jnp.int32, (inner, width), 1)
    outer = jnp.where(is_odd("gx") == 1, depth - 1, 0)
    conds, fields = ([own[a, p] for p in range(depth)] for a in (1, 2))
    next_conds, next_fields = ([ahead(v, 1) for v in values] for values in (conds, fields))
    along_z = [
        jnp.where(column < width - 1, (c + c_next) * (f - f_next), 0.0)
        for c, f, c_next, f_next in zip(conds, fields, next_conds, next_fields)
    ]
    arriving = [behind(v, 1) for v in along_z]
    for p, (cond, field) in enumerate(zip(conds, fields)):
        along_y = jnp.where(row < inner - 1, (cond + ahead(cond, 0)) * (field - ahead(field, 0)), 0.0)
        total = (along_y - behind(along_y, 0)) + (along_z[p] - arriving[p])
        for other in (p - 1, p + 1):
            if 0 <= other < depth:
                total += (cond + conds[other]) * (field - fields[other])
        if reflect and p in (0, depth - 1):
            total += jnp.where(outer == p, cond * field, 0.0)
        own[0, p] = 2.0 * own[0, p] - total

    odd = is_odd("gy")
    row = lax.broadcasted_iota(jnp.int32, (HALO, width), 0)
    lane = lax.broadcasted_iota(jnp.int32, (HALO, LANES), 1)
    for message, high in ((first, odd == 0), (second, odd == 1)):
        rows = pl.ds(pl.multiple_of(jnp.where(high, inner - HALO, 0), 8), HALO)
        at = functools.partial(far_row, high)
        sides = jnp.zeros((HALO, LANES), jnp.float32)
        for p in range(0, depth, 2):
            sums = own[1, p, rows, :] + own[1, p + 1, rows, :]
            sums = sums + inward(high, sums)
            rests = own[0, p, rows, :] + own[0, p + 1, rows, :]
            rests = shifted_rows(high, rests + inward(high, rests), 2)
            for i, seventh in enumerate((sums, rests)):
                field = own[2, p + i, rows, :]
                cond = jnp.where(row == at(7), seventh, own[1, p + i, rows, :])
                message[p + i] = jnp.where(row == at(8), inward(high, field), cond)
                ends = pltpu.roll(both_ends(field), 2 * (p + i) + 1, 1)
                sides = jnp.where(lane // 2 == p + i, ends, sides)
            near = jnp.where(high, HALO - 1 - row, row) < 4
            message[depth + p // 2] = jnp.where(near, own[0, p, rows, :], pltpu.roll(own[0, p + 1, rows, :], 4, 0))
        planes = depth + depth // 2
        if reflect:
            message[planes] = own[2, depth - 1 - outer, rows, :]
        else:
            message[planes] = own[2, 0, rows, :]
            message[planes + 1] = own[2, depth - 1, rows, :]
        message[message.shape[0] - 1] = jnp.zeros((HALO, width), jnp.float32)
        message[message.shape[0] - 1, :, 0:LANES] = sides


def head_lane(a, g):
    return 8 + 16 * a + LANES // 2 * (g % 2) + 8 * (g // 2)


def tail_lane(a, g):
    return 8 + 16 * a + LANES // 2 * (g % 2) + 8 * (1 - g // 2)


def pack_columns(reflect, own, got_a, got_b, strips, rim):
    odd_y, odd_z = is_odd("gy"), is_odd("grp")
    first_y, last_y = beyond("gy")
    _, depth, inner, width = own.shape
    groups = inner // 8 + 2
    odd_x = is_odd("gx")
    lane = lax.broadcasted_iota(jnp.int32, (8, LANES), 1)
    row = lax.broadcasted_iota(jnp.int32, (8, width), 0)
    wide = lax.broadcasted_iota(jnp.int32, (8, width), 1)

    def spread_out(v):
        return jnp.concatenate([v] * (width // LANES), 1)

    for p in range(depth):
        for side, (low, outside) in enumerate(((True, first_y), (False, last_y))):

            at = functools.partial(far_row, low)

            def take(i):
                strip = jnp.where(odd_y == (1 if low else 0), got_a[i], got_b[i])
                return jnp.where(outside, 0.0, strip)

            cond, mixed = take(p), take(depth + p // 2)
            g = mixed if p % 2 == 0 else pltpu.roll(mixed, 4, 0)
            g = jnp.where(row >= 4 if low else row < 4, g, 0.0)
            if p % 2:
                g = jnp.where(row == at(5), shifted_rows(low, cond, HALO - 2), g)
            sides = take(got_a.shape[0] - 1)[:, 0:LANES]
            ends = spread_out(pltpu.roll(sides, LANES - 1 - 2 * p, 1))
            field = jnp.where((wide == 0) | (wide == width - 1), ends, 0.0)
            field = jnp.where(row == at(1), shifted_rows(low, cond, 1), field)
            planes = depth + depth // 2
            if reflect and p in (0, depth - 1):
                field = jnp.where(odd_x == (1 if p == 0 else 0), take(planes), field)
            elif not reflect and p in (0, depth - 1):
                field = take(planes + (0 if p == 0 else 1))
            cond = jnp.where(row == at(8), 0.0, cond)
            if p % 2:
                cond = jnp.where(row == at(7), 0.0, cond)
            rim[side, 0, p] = g
            rim[side, 1, p] = cond
            rim[side, 2, p] = field
    moved = {}
    for p in range(depth):
        for a in range(3):
            for g in range(groups):
                if g == 0 or g == groups - 1:
                    rows = rim[min(g, 1), a, p]
                else:
                    rows = own[a, p, 8 * g - 8 : 8 * g, :]
                to_head, to_tail = head_lane(a, g), tail_lane(a, g)
                if to_head == to_tail + HALO:
                    ends = pltpu.roll(both_ends(rows), to_head, 1)
                    moved[p, a, g] = ends, ends
                else:
                    last = pltpu.roll(rows[:, width - LANES : width], (to_tail + HALO) % LANES, 1)
                    moved[p, a, g] = pltpu.roll(rows[:, 0:LANES], to_head, 1), last
    for p in range(depth):
        head = tail = jnp.zeros((8, LANES), jnp.float32)
        for a in range(3):
            for g in range(groups):
                to_head, to_tail = head_lane(a, g), tail_lane(a, g)
                head = jnp.where((lane >= to_head) & (lane < to_head + HALO), moved[p, a, g][0], head)
                tail = jnp.where((lane >= to_tail) & (lane < to_tail + HALO), moved[p, a, g][1], tail)
        swapped = (odd_x if reflect else odd_z) == 1
        strips[0, p] = jnp.where(swapped, tail, head) if reflect else jnp.where(swapped, head, tail)
        strips[1, p] = jnp.where(swapped, head, tail) if reflect else jnp.where(swapped, tail, head)


def shifts(parts, step):
    if parts == 1:
        return (lambda v: [ahead(v[0], 1, step)]), (lambda v: [behind(v[0], 1, step)])
    return (lambda v: [v[1], ahead(v[0], 1)]), (lambda v: [behind(v[1], 1), v[0]])


def each(op, *lists):
    return [op(*values) for values in zip(*lists)]


def add(*lists):
    return each(lambda *values: functools.reduce(lambda x, y: x + y, values), *lists)


def times(x, y):
    return each(lambda v, w: v * w, x, y)


def solve(cells, own_at, own, out, seams):
    (src, cond, field, wx, wy, wz, vy, vz, diag, inv, sum8, cwx, cwy, cwz, cvy, cvz, cinv, res, q, cq, err) = cells
    total, parts, rows, lanes = cond.shape

    def load(ref, p):
        return [ref[p, i] for i in range(ref.shape[1])]

    def store(ref, p, values):
        for i, v in enumerate(values):
            ref[p, i] = v

    def reach(halo):
        low = max(1, own_at - halo)
        high = min(total, own_at + own + halo)
        return range((low + 1) // 2, (high + 1) // 2)

    fine = (1, *shifts(parts, 1))
    coarse = (2, *shifts(1, 3 - parts))
    zero = jnp.zeros((rows, lanes), jnp.float32)
    for ref in (q, cq, err, sum8):
        store(ref, 0, [zero] * ref.shape[1])

    even_row = lax.rem(lax.broadcasted_iota(jnp.int32, (rows, lanes), 0), 2) == 0
    even_lane = lax.rem(lax.broadcasted_iota(jnp.int32, (rows, lanes), 1), 2) == 0

    def turned(ref, planes, level):
        here = {p: load(ref, p) for p in planes}
        return {p: (level[1](v), level[2](v)) for p, v in here.items()}

    def planes_of(blocks):
        return [p for k in blocks for p in (2 * k - 1, 2 * k)]

    def gather(sums):
        sums = {k: [v[0] + ahead(v[0], 0)] if parts == 1 else [v[0] + v[1]] for k, v in sums.items()}
        if parts == 1:
            return {k: [v[0] + u] for (k, v), u in zip(sums.items(), [ahead(v[0], 1) for v in sums.values()])}
        return {k: [v[0] + ahead(v[0], 0)] for k, v in sums.items()}

    for k, v in gather({k: add(load(cond, 2 * k - 1), load(cond, 2 * k)) for k in reach(HALO)}).items():
        store(sum8, k, v)

    def weights(ref, p, level, around_z):
        step = level[0]
        c = load(ref, p)
        x = add(c, load(ref, p + 1))
        y, yb = ([v + shift(v, 0, step) for v in c] for shift in (ahead, behind))
        z, zb = (add(c, v) for v in around_z)
        k = add(add(c, load(ref, p - 1), x), add(y, yb), add(z, zb))
        return x, y, z, yb, zb, k, each(lambda v, w: jnp.where(v > 0.0, 1.0 / w, 0.0), c, k)

    low = reach(HALO - 2).start
    store(wx, 2 * low - 2, add(load(cond, 2 * low - 2), load(cond, 2 * low - 1)))
    store(cwx, low - 1, add(load(sum8, low - 1), load(sum8, low)))
    z_fine = turned(cond, planes_of(reach(HALO - 2)), fine)
    z_coarse = turned(sum8, reach(HALO - 2), coarse)
    for k in reach(HALO - 2):
        for p in (2 * k - 1, 2 * k):
            for ref, v in zip((wx, wy, wz, vy, vz, diag, inv), weights(cond, p, fine, z_fine[p])):
                store(ref, p, v)
        for ref, v in zip((cwx, cwy, cwz, cvy, cvz, None, cinv), weights(sum8, k, coarse, z_coarse[k])):
            if ref is not None:
                store(ref, k, v)

    def spread(v, p, refs, level, around_z):
        x, y, z, yb, zb = refs
        step = level[0]
        here = load(v, p)
        n = add(times(load(x, p - 1), load(v, p - 1)), times(load(x, p), load(v, p + 1)))
        n = add(n, times(load(y, p), [ahead(u, 0, step) for u in here]))
        n = add(n, times(load(yb, p), [behind(u, 0, step) for u in here]))
        return add(n, add(times(load(z, p), around_z[0]), times(load(zb, p), around_z[1])))

    def smooth(v, p, refs, scale, level, around_z):
        n = times(load(scale, p), spread(v, p, refs, level, around_z))
        return each(lambda u, w: KEEP * u + SPREAD * w, load(v, p), n)

    def between(p, around_z):
        planes, along_y, along_z = seams
        here = load(field, p)
        r = load(src, p)

        def less(r, weights, there, where=None):
            flux = each(lambda w, u, v: w * (u - v), weights, here, there)
            return each(lambda x, y: x - (y if where is None else jnp.where(where, y, 0.0)), r, flux)

        if p in planes:
            r = less(r, load(wx, p), load(field, p + 1))
        if p - 1 in planes:
            r = less(r, load(wx, p - 1), load(field, p - 1))
        r = less(r, load(wy, p), [ahead(v, 0) for v in here], along_y[0])
        r = less(r, load(vy, p), [behind(v, 0) for v in here], along_y[1])
        if along_z is not None:
            r = less(r, load(wz, p), around_z[0], along_z[0])
            r = less(r, load(vz, p), around_z[1], along_z[1])
        return r

    around, coarse_around = (wx, wy, wz, vy, vz), (cwx, cwy, cwz, cvy, cvz)

    for it in range(ITERS):
        halo = 4 * (ITERS - 1 - it)
        blocks = reach(halo + 2)
        rounds = turned(err if it else field, planes_of(blocks), fine) if it or seams[2] is not None else {}
        sums = {}
        for k in blocks:
            found = []
            for p in (2 * k - 1, 2 * k):
                if it == 0:
                    r = between(p, rounds.get(p))
                else:
                    n = spread(err, p, around, fine, rounds[p])
                    r = each(lambda u, d, w, m: u - (d * w - m), load(res, p), load(diag, p), load(err, p), n)
                if it < ITERS - 1:
                    store(res, p, r)
                store(q, p, times(r, load(inv, p)))
                found.append(r)
            sums[k] = add(*found)
        near = reach(halo)
        sums = gather(sums)
        rounds = turned(q, planes_of(near), fine)
        for k, v in sums.items():
            store(cq, k, times([4.0 * v[0]], load(cinv, k)))
        coarse_rounds = turned(cq, near, coarse)
        found = {k: smooth(cq, k, coarse_around, cinv, coarse, coarse_rounds[k])[0] for k in near}
        if parts == 1:
            beside = {k: behind(c, 1) for k, c in found.items()}
            found = {k: jnp.where(even_lane, c, beside[k]) for k, c in found.items()}
        smoothed = {p: smooth(q, p, around, inv, fine, rounds[p]) for p in planes_of(near)}
        for k in near:
            c = jnp.where(even_row, found[k], behind(found[k], 0))
            for p in (2 * k - 1, 2 * k):
                e = [u + c for u in smoothed[p]]
                if it:
                    e = add(load(err, p), e)
                if it < ITERS - 1:
                    store(err, p, e)
                else:
                    out(p, add(load(field, p), e))


def layout(reflect, depth):
    return (1, depth + HALO + 2) if reflect else (1 + HALO, depth + 2 * HALO + 2)


def each_plane(reflect, depth, place):
    odd_x = is_odd("gx")
    own_at, _ = layout(reflect, depth)

    for p in range(depth):
        place(None, jnp.where(odd_x == 1, depth - 1 - p, p) if reflect else p, own_at + p)
    for p in range(HALO):
        if reflect:
            place(0, jnp.where(odd_x == 1, depth - 1 - p, p), own_at + depth + p)
            continue
        for i in range(2):
            above = odd_x == i
            at = jnp.where(above, p, depth - HALO + p)
            place(i, at, jnp.where(above, own_at + depth + p, 1 + p))


def x_seams(reflect, depth):
    own_at, _ = layout(reflect, depth)
    return (own_at + depth - 1,) if reflect else (own_at - 1, own_at + depth - 1)


def out_plane(reflect, depth, p):
    own_at, _ = layout(reflect, depth)
    at = p - own_at
    return jnp.where(is_odd("gx") == 1, depth - 1 - at, at) if reflect else at


def parting(width, lanes):
    column = lax.broadcasted_iota(jnp.int32, (width, 2 * lanes), 0)
    lane = lax.broadcasted_iota(jnp.int32, (width, 2 * lanes), 1)
    wanted = jnp.where(lane < lanes, 2 * lane, 2 * (lane - lanes) + 1)
    return jnp.where((column == wanted) & (wanted < width), 1.0, 0.0)


def ending(width):
    column = lax.broadcasted_iota(jnp.int32, (width, 2 * LANES), 0)
    lane = lax.broadcasted_iota(jnp.int32, (width, 2 * LANES), 1)
    lane = jnp.where(lane < LANES, lane, lane - LANES - LANES // 2)
    last = (lane >= 8) & (lane < 24) & (column == lane + width - 24)
    first = (lane >= 40) & (lane < 56) & (column == lane - 40)
    return jnp.where(last | first, 1.0, 0.0)


def rearranged(v, matrix):
    bf16, f32 = jnp.bfloat16, jnp.float32
    matrix = matrix.astype(bf16)
    result = None
    for _ in range(3):
        part = v.astype(bf16)
        v = v - part.astype(f32)
        moved = jnp.dot(part, matrix, preferred_element_type=f32)
        result = moved if result is None else result + moved
    return result


def interior(reflect, n_x, *refs):
    own, rim = refs[0], refs[1]
    near, near_rim = refs[2 : 2 + n_x], refs[2 + n_x : 2 + 2 * n_x]
    result, ends = refs[2 + 2 * n_x : 4 + 2 * n_x]
    whole, halves, *cells = refs[4 + 2 * n_x :]
    _, depth, inner, width = own.shape
    rows = inner + 2 * HALO
    lanes = cells[0].shape[3]

    def place(i, p_from, p_to):
        block, halo = (own, rim) if i is None else (near[i], near_rim[i])
        for a in range(3):
            tile = whole.at[a, p_to]
            tile[0:HALO, :] = halo[0, a, p_from]
            tile[HALO : HALO + inner, :] = block[a, p_from]
            tile[HALO + inner : rows, :] = halo[1, a, p_from]

    own_at, total = layout(reflect, depth)
    for a in range(3):
        for p in (0, total - 1):
            whole[a, p] = jnp.zeros((rows, width), jnp.float32)
    each_plane(reflect, depth, place)
    apart = parting(width, lanes)
    target = jnp.concatenate([apart, ending(width)], 1)
    for a in range(3):
        parts = rearranged(whole[a].reshape(total * rows, width), target).reshape(total, rows, -1)
        for i in range(2):
            cells[a][:, i] = parts[:, :, i * lanes : (i + 1) * lanes]
        low = parts[:, 0 : rows - 8, 2 * lanes : 2 * lanes + LANES]
        ends[a] = low + parts[:, 8:rows, 2 * lanes + LANES :]

    def out(p, v):
        for i in range(2):
            halves[p - own_at, :, i * lanes : (i + 1) * lanes] = v[i][HALO : rows - HALO, :]

    row = lax.broadcasted_iota(jnp.int32, (rows, lanes), 0)
    along_y = (row == HALO - 1) | (row == HALO + inner - 1), (row == HALO) | (row == HALO + inner)
    solve(cells, own_at, depth, out, (x_seams(reflect, depth), along_y, None))
    together = rearranged(halves[...].reshape(depth * inner, 2 * lanes), apart.T)
    together = together.reshape(depth, inner, width)
    for p in range(depth):
        result[out_plane(reflect, depth, own_at + p)] = together[p]


def edges(reflect, ends, inside, got_a, got_b, result, staged, sems, *cells):
    depth, inner, width = inside.shape
    odd_x, odd_z = is_odd("gx"), is_odd("grp")
    first_z, last_z = beyond("grp")
    lane = lax.broadcasted_iota(jnp.int32, (8, LANES), 1)
    half = LANES // 2
    own_at, total = layout(reflect, depth)
    for p in (0, total - 1):
        for a in range(3):
            cells[a][p, 0] = ends[a, p]

    windows = []

    def place(i, p_from, p_to):
        at_plane = p_from if i is None else (i + 1) * depth + p_from
        if reflect:
            va, vb = got_a[depth + p_from if i is None else p_from], got_b[at_plane]
            swapped = odd_x == 0
        else:
            va, vb = got_a[at_plane], got_b[at_plane]
            swapped = odd_z == 1
        right = jnp.where(last_z, 0.0, jnp.where(swapped, vb, va))
        left = jnp.where(first_z, 0.0, jnp.where(swapped, va, vb))
        windows.append((p_to, right, left, pltpu.roll(right, LANES - 8, 1), pltpu.roll(left, 8, 1)))

    here = lax.rem(lane, half)
    in_halo = (here >= 24) & (here < 40)
    each_plane(reflect, depth, place)
    side = lax.rem(lane, 16) >= 8
    groups = []
    for p, right, left, right_moved, left_moved in windows:
        lower, upper = jnp.where(side, right, left), jnp.where(side, right_moved, left_moved)
        groups.append((p, lower, pltpu.roll(jnp.where(lane < half, upper, lower), half, 1), upper))
    for a in (1, 0, 2):
        for p, *tiles in groups:
            for t, tile in enumerate(tiles):
                moved = tile if a == 1 else pltpu.roll(tile, (16 - 16 * a) % LANES, 1)
                part = slice(8 * t, 8 * t + 8)
                cells[a][p, 0, part, :] = jnp.where(in_halo, moved, ends[a, p, part, :])

    row = lax.broadcasted_iota(jnp.int32, ends.shape[2:], 0)
    lane_in_half = lax.rem(lax.broadcasted_iota(jnp.int32, ends.shape[2:], 1), half)
    upper_half = lax.broadcasted_iota(jnp.int32, ends.shape[2:], 1) >= half
    face = jnp.where(upper_half, inner, HALO)
    along_z = tuple((lane_in_half == at) | (lane_in_half == at + 16) for at in (23, 24))
    finals = []
    solve(cells, own_at, depth, lambda p, v: finals.append((p - own_at, v[0][8:16])), (x_seams(reflect, depth), (row == face - 1, row == face), along_z))
    moved = [
        (p, i, pltpu.roll(v, (LANES - 40 - half * i) % LANES, 1), pltpu.roll(v, (LANES - 24 - half * i) % LANES, 1))
        for p, v in finals
        for i in range(2)
    ]
    copies = []
    for p, i, head, tail in moved:
        at, part = out_plane(reflect, depth, own_at + p), slice(8 * i, 8 * i + 8)
        for c in range(0, width, LANES):
            tile = inside[at, part, c : c + LANES]
            if c == 0:
                tile = jnp.where(lane < HALO, head, tile)
            if c == width - LANES:
                tile = jnp.where(lane >= LANES - HALO, tail, tile)
            staged[p, part, c : c + LANES] = tile
        if i:
            copies.append(pltpu.make_async_copy(staged.at[p], result.at[at], sems.at[p]))
            copies[-1].start()
    for copy in copies:
        copy.wait()


def shards(sizes, source_term, conductivity, initial_field):
    depth, inner, width = source_term.shape
    assert inner == 16 and depth >= HALO and depth % 2 == 0 and width % LANES == 0
    rows = inner + 2 * HALO
    f32 = jnp.float32
    params = pltpu.CompilerParams(vmem_limit_bytes=48 * 1024 * 1024)
    args = (source_term, conductivity, initial_field)

    def exchange(values, axis):
        over, rounds = swaps(axis, sizes)
        found = [lax.ppermute(v, over, pairs) for v, pairs in reversed(list(zip(values, rounds)))]
        return found[::-1] + [jnp.zeros_like(v) for v in values[len(found) :]]

    def work(parts, rows, lanes):
        total = layout(reflect, depth)[1]
        fine = pltpu.VMEM((total, parts, rows, lanes), f32)
        coarse = pltpu.VMEM((total // 2 + 1, 1, rows, lanes), f32)
        return [fine] * 10 + [coarse] * 7 + [fine] * 2 + [coarse] + [fine]

    reflect = sizes["gx"] == 2
    n_x = 1 if reflect else 2
    args = [pltpu.with_memory_space_constraint(v, pltpu.HBM) for v in args]
    face = jax.ShapeDtypeStruct((depth + depth // 2 + n_x + 1, HALO, width), f32)
    own, *msgs = pl.pallas_call(
        functools.partial(prepare, reflect),
        out_shape=(jax.ShapeDtypeStruct((3, depth, inner, width), f32), face, face),
        in_specs=[pl.BlockSpec(memory_space=pltpu.HBM)] * 3, out_specs=(VMEM,) * 3,
        scratch_shapes=[pltpu.SemaphoreType.DMA((3,))], compiler_params=params, name="prepare",
    )(*args)
    got = exchange(msgs, "gy")
    near = exchange([own] * n_x, "gx")
    strips, rim = pl.pallas_call(
        functools.partial(pack_columns, reflect),
        out_shape=(
            jax.ShapeDtypeStruct((2, depth, 8, LANES), f32),
            jax.ShapeDtypeStruct((2, 3, depth, HALO, width), f32),
        ),
        in_specs=[VMEM] * 3, out_specs=(VMEM, VMEM),
        compiler_params=params, name="pack_columns",
    )(own, *got)
    if reflect:
        strips = jnp.concatenate([strips[0]] + exchange([strips[1]], "gx"), axis=0)
    else:
        strips = jnp.concatenate([strips] + exchange([strips] * n_x, "gx"), axis=1)
    strips, rim = lax.optimization_barrier((strips, rim))
    near_rim = exchange([rim] * n_x, "gx")
    if reflect:
        strips = [lax.ppermute(strips, tuple(sizes), crossing(sizes))]
    else:
        strips = exchange([strips[0], strips[1]], "grp")

    block = jax.ShapeDtypeStruct(source_term.shape, f32)
    total = layout(reflect, depth)[1]
    lanes = -(-width // (2 * LANES)) * LANES
    apart = [pltpu.VMEM((3, total, rows, width), f32), pltpu.VMEM((depth, inner, 2 * lanes), f32)]
    inside, ends = pl.pallas_call(
        functools.partial(interior, reflect, n_x),
        out_shape=(block, jax.ShapeDtypeStruct((3, total, rows - 8, LANES), f32)),
        in_specs=[VMEM] * (2 + 2 * n_x), out_specs=(VMEM, VMEM), scratch_shapes=apart + work(2, rows, lanes),
        compiler_params=params, name="interior",
        cost_estimate=pl.CostEstimate(flops=20_000_000, bytes_accessed=20_000_000, transcendentals=0),
    )(own, rim, *near, *near_rim)
    inside, ends, *strips = lax.optimization_barrier((inside, ends, *strips[::-1]))
    strips = strips[::-1]
    if reflect:
        strips += exchange(strips, "gx")
    return pl.pallas_call(
        functools.partial(edges, reflect),
        out_shape=block,
        in_specs=[VMEM] * 4, out_specs=pl.BlockSpec(memory_space=pltpu.HBM),
        scratch_shapes=[pltpu.VMEM((depth, inner, width), f32), pltpu.SemaphoreType.DMA((depth,))] + work(1, rows - 8, LANES),
        compiler_params=params, name="edges",
    )(ends, inside, *strips)


def solution(mesh):
    spec = P("gx", "gy", "grp")
    return jax.shard_map(
        functools.partial(shards, dict(mesh.shape)),
        mesh=mesh,
        in_specs=(spec,) * 3,
        out_specs=spec,
        check_vma=False,
    )
```

```python
import functools

import jax
import jax.numpy as jnp
from jax import lax
from jax.experimental import pallas as pl
from jax.experimental.pallas import tpu as pltpu
from jax.sharding import PartitionSpec as P

ITERS = 2
HALO = 4 * ITERS
LANES = 128
KEEP = 48.0 / 41.0
SPREAD_OVER_KEEP = 2.0 / 3.0
VMEM = pl.BlockSpec(memory_space=pltpu.VMEM)


def ahead(v, axis, n=1):
    return pltpu.roll(v, v.shape[axis] - n, axis)


def behind(v, axis, n=1):
    return pltpu.roll(v, n, axis)


def swaps(axis, sizes):
    count, fill = sizes[axis], sizes["gx"]
    over = [name for name in sizes if name in (axis, "gx")]
    filled = axis != "gx" and fill % 2 == 0

    def at(i, k):
        return i * fill + k if over[0] == axis else k * count + i

    rounds = []
    for start in (0, 1):
        pairs = [(i, i + 1) for i in range(start, count - 1, 2)]
        left = set(range(count)) - {i for pair in pairs for i in pair}
        if not pairs:
            continue
        if filled:
            pairs = [(at(i, k), at(j, k)) for i, j in pairs for k in range(fill)]
            pairs += [(at(i, k), at(i, k + 1)) for i in sorted(left) for k in range(0, fill, 2)]
        rounds.append(pairs + [(j, i) for i, j in pairs])
    return (tuple(over) if filled else axis), rounds


def crossing(sizes):
    names = list(sizes)

    def at(**place):
        index = 0
        for name in names:
            index = index * sizes[name] + place[name]
        return index

    last = sizes["grp"] - 1
    pairs = [
        (at(grp=g, gx=1, gy=y), at(grp=g + 1, gx=0, gy=y)) for g in range(last) for y in range(sizes["gy"])
    ]
    pairs += [
        (at(grp=g, gx=x, gy=y), at(grp=g, gx=x, gy=y + 1))
        for g, x in ((0, 0), (last, 1))
        for y in range(0, sizes["gy"] - 1, 2)
    ]
    return pairs + [(j, i) for i, j in pairs]


def is_odd(axis):
    return lax.rem(lax.axis_index(axis), 2)


def beyond(axis):
    at = lax.axis_index(axis)
    return at == 0, at == lax.axis_size(axis) - 1


def is_odd(axis):
    return lax.rem(lax.axis_index(axis), 2)


def far_row(high, distance):
    if isinstance(high, bool):
        return HALO - distance if high else distance - 1
    return jnp.where(high, HALO - distance, distance - 1)


def shifted_rows(high, v, n):
    if isinstance(high, bool):
        return pltpu.roll(v, HALO - n if high else n, 0)
    return jnp.where(high, pltpu.roll(v, HALO - n, 0), pltpu.roll(v, n, 0))


def inward(high, v):
    return shifted_rows(high, v, HALO - 1)


def both_ends(rows):
    width = rows.shape[1]
    lane = lax.broadcasted_iota(jnp.int32, (rows.shape[0], LANES), 1)
    return jnp.where(lane < LANES // 2, rows[:, 0:LANES], rows[:, width - LANES : width])


def prepare(reflect, s, c, f, own, first, second, sems):
    copies = [pltpu.make_async_copy(ref, own.at[a], sems.at[a]) for a, ref in enumerate((s, c, f))]
    for copy in copies:
        copy.start()
    for copy in copies:
        copy.wait()
    _, depth, inner, width = own.shape
    row = lax.broadcasted_iota(jnp.int32, (inner, width), 0)
    column = lax.broadcasted_iota(jnp.int32, (inner, width), 1)
    outer = jnp.where(is_odd("gx") == 1, depth - 1, 0)
    conds, fields = ([own[a, p] for p in range(depth)] for a in (1, 2))
    next_conds, next_fields = ([ahead(v, 1) for v in values] for values in (conds, fields))
    along_z = [
        jnp.where(column < width - 1, (c + c_next) * (f - f_next), 0.0)
        for c, f, c_next, f_next in zip(conds, fields, next_conds, next_fields)
    ]
    arriving = [behind(v, 1) for v in along_z]
    for p, (cond, field) in enumerate(zip(conds, fields)):
        along_y = jnp.where(row < inner - 1, (cond + ahead(cond, 0)) * (field - ahead(field, 0)), 0.0)
        total = (along_y - behind(along_y, 0)) + (along_z[p] - arriving[p])
        for other in (p - 1, p + 1):
            if 0 <= other < depth:
                total += (cond + conds[other]) * (field - fields[other])
        if reflect and p in (0, depth - 1):
            total += jnp.where(outer == p, cond * field, 0.0)
        own[0, p] = 2.0 * own[0, p] - total

    odd = is_odd("gy")
    row = lax.broadcasted_iota(jnp.int32, (HALO, width), 0)
    lane = lax.broadcasted_iota(jnp.int32, (HALO, LANES), 1)
    for message, high in ((first, odd == 0), (second, odd == 1)):
        rows = pl.ds(pl.multiple_of(jnp.where(high, inner - HALO, 0), 8), HALO)
        at = functools.partial(far_row, high)
        sides = jnp.zeros((HALO, LANES), jnp.float32)
        for p in range(0, depth, 2):
            sums = own[1, p, rows, :] + own[1, p + 1, rows, :]
            sums = sums + inward(high, sums)
            rests = own[0, p, rows, :] + own[0, p + 1, rows, :]
            rests = shifted_rows(high, rests + inward(high, rests), 2)
            for i, seventh in enumerate((sums, rests)):
                field = own[2, p + i, rows, :]
                cond = jnp.where(row == at(7), seventh, own[1, p + i, rows, :])
                message[p + i] = jnp.where(row == at(8), inward(high, field), cond)
                ends = pltpu.roll(both_ends(field), 2 * (p + i) + 1, 1)
                sides = jnp.where(lane // 2 == p + i, ends, sides)
            near = jnp.where(high, HALO - 1 - row, row) < 4
            message[depth + p // 2] = jnp.where(near, own[0, p, rows, :], pltpu.roll(own[0, p + 1, rows, :], 4, 0))
        planes = depth + depth // 2
        if reflect:
            message[planes] = own[2, depth - 1 - outer, rows, :]
        else:
            message[planes] = own[2, 0, rows, :]
            message[planes + 1] = own[2, depth - 1, rows, :]
        message[message.shape[0] - 1] = jnp.zeros((HALO, width), jnp.float32)
        message[message.shape[0] - 1, :, 0:LANES] = sides


def head_lane(a, g):
    return 8 + 16 * a + LANES // 2 * (g % 2) + 8 * (g // 2)


def tail_lane(a, g):
    return 8 + 16 * a + LANES // 2 * (g % 2) + 8 * (1 - g // 2)


def pack_columns(reflect, own, got_a, got_b, strips, rim):
    odd_y, odd_z = is_odd("gy"), is_odd("grp")
    first_y, last_y = beyond("gy")
    _, depth, inner, width = own.shape
    groups = inner // 8 + 2
    odd_x = is_odd("gx")
    lane = lax.broadcasted_iota(jnp.int32, (8, LANES), 1)
    row = lax.broadcasted_iota(jnp.int32, (8, width), 0)
    wide = lax.broadcasted_iota(jnp.int32, (8, width), 1)

    def spread_out(v):
        return jnp.concatenate([v] * (width // LANES), 1)

    for p in range(depth):
        for side, (low, outside) in enumerate(((True, first_y), (False, last_y))):

            at = functools.partial(far_row, low)

            def take(i):
                strip = jnp.where(odd_y == (1 if low else 0), got_a[i], got_b[i])
                return jnp.where(outside, 0.0, strip)

            cond, mixed = take(p), take(depth + p // 2)
            g = mixed if p % 2 == 0 else pltpu.roll(mixed, 4, 0)
            g = jnp.where(row >= 4 if low else row < 4, g, 0.0)
            if p % 2:
                g = jnp.where(row == at(5), shifted_rows(low, cond, HALO - 2), g)
            sides = take(got_a.shape[0] - 1)[:, 0:LANES]
            ends = spread_out(pltpu.roll(sides, LANES - 1 - 2 * p, 1))
            field = jnp.where((wide == 0) | (wide == width - 1), ends, 0.0)
            field = jnp.where(row == at(1), shifted_rows(low, cond, 1), field)
            planes = depth + depth // 2
            if reflect and p in (0, depth - 1):
                field = jnp.where(odd_x == (1 if p == 0 else 0), take(planes), field)
            elif not reflect and p in (0, depth - 1):
                field = take(planes + (0 if p == 0 else 1))
            cond = jnp.where(row == at(8), 0.0, cond)
            if p % 2:
                cond = jnp.where(row == at(7), 0.0, cond)
            rim[side, 0, p] = g
            rim[side, 1, p] = cond
            rim[side, 2, p] = field
    moved = {}
    for p in range(depth):
        for a in range(3):
            for g in range(groups):
                if g == 0 or g == groups - 1:
                    rows = rim[min(g, 1), a, p]
                else:
                    rows = own[a, p, 8 * g - 8 : 8 * g, :]
                to_head, to_tail = head_lane(a, g), tail_lane(a, g)
                if to_head == to_tail + HALO:
                    ends = pltpu.roll(both_ends(rows), to_head, 1)
                    moved[p, a, g] = ends, ends
                else:
                    last = pltpu.roll(rows[:, width - LANES : width], (to_tail + HALO) % LANES, 1)
                    moved[p, a, g] = pltpu.roll(rows[:, 0:LANES], to_head, 1), last
    for p in range(depth):
        head = tail = jnp.zeros((8, LANES), jnp.float32)
        for a in range(3):
            for g in range(groups):
                to_head, to_tail = head_lane(a, g), tail_lane(a, g)
                head = jnp.where((lane >= to_head) & (lane < to_head + HALO), moved[p, a, g][0], head)
                tail = jnp.where((lane >= to_tail) & (lane < to_tail + HALO), moved[p, a, g][1], tail)
        swapped = (odd_x if reflect else odd_z) == 1
        strips[0, p] = jnp.where(swapped, tail, head) if reflect else jnp.where(swapped, head, tail)
        strips[1, p] = jnp.where(swapped, head, tail) if reflect else jnp.where(swapped, tail, head)


def shifts(parts, step):
    if parts == 1:
        return (lambda v: [ahead(v[0], 1, step)]), (lambda v: [behind(v[0], 1, step)])
    return (lambda v: [v[1], ahead(v[0], 1)]), (lambda v: [behind(v[1], 1), v[0]])


def each(op, *lists):
    return [op(*values) for values in zip(*lists)]


def add(*lists):
    return each(lambda *values: functools.reduce(lambda x, y: x + y, values), *lists)


def times(x, y):
    return each(lambda v, w: v * w, x, y)


def solve(cells, own_at, own, out, seams):
    (src, cond, field, wx, wy, wz, vy, vz, diag, inv, sum8, cwx, cwy, cwz, cvy, cvz, cinv, res, q, cq, err) = cells
    total, parts, rows, lanes = cond.shape

    def load(ref, p):
        return [ref[p, i] for i in range(ref.shape[1])]

    def store(ref, p, values):
        for i, v in enumerate(values):
            ref[p, i] = v

    def reach(halo):
        low = max(1, own_at - halo)
        high = min(total, own_at + own + halo)
        return range((low + 1) // 2, (high + 1) // 2)

    fine = (1, *shifts(parts, 1))
    coarse = (2, *shifts(1, 3 - parts))
    zero = jnp.zeros((rows, lanes), jnp.float32)
    for ref in (q, cq, err, sum8):
        store(ref, 0, [zero] * ref.shape[1])

    even_row = lax.rem(lax.broadcasted_iota(jnp.int32, (rows, lanes), 0), 2) == 0
    even_lane = lax.rem(lax.broadcasted_iota(jnp.int32, (rows, lanes), 1), 2) == 0

    def turned(ref, planes, level):
        here = {p: load(ref, p) for p in planes}
        return {p: (level[1](v), level[2](v)) for p, v in here.items()}

    def planes_of(blocks):
        return [p for k in blocks for p in (2 * k - 1, 2 * k)]

    def gather(sums):
        sums = {k: [v[0] + ahead(v[0], 0)] if parts == 1 else [v[0] + v[1]] for k, v in sums.items()}
        if parts == 1:
            return {k: [v[0] + u] for (k, v), u in zip(sums.items(), [ahead(v[0], 1) for v in sums.values()])}
        return {k: [v[0] + ahead(v[0], 0)] for k, v in sums.items()}

    z_fine = turned(cond, planes_of(reach(HALO - 2)), fine)
    for k, v in gather({k: add(load(cond, 2 * k - 1), load(cond, 2 * k)) for k in reach(HALO)}).items():
        store(sum8, k, v)
    z_field = turned(field, planes_of(reach(HALO - 2)), fine) if seams[2] is not None else {}

    def weights(ref, p, level, around_z):
        step = level[0]
        c = load(ref, p)
        x = add(c, load(ref, p + 1))
        y, yb = ([v + shift(v, 0, step) for v in c] for shift in (ahead, behind))
        z, zb = (add(c, v) for v in around_z)
        k = add(add(c, load(ref, p - 1), x), add(y, yb), add(z, zb))
        return x, y, z, yb, zb, k, each(lambda v, w: jnp.where(v > 0.0, KEEP / w, 0.0), c, k)

    low = reach(HALO - 2).start
    store(wx, 2 * low - 2, add(load(cond, 2 * low - 2), load(cond, 2 * low - 1)))
    store(cwx, low - 1, add(load(sum8, low - 1), load(sum8, low)))
    z_coarse = turned(sum8, reach(HALO - 2), coarse)
    for k in reach(HALO - 2):
        for p in (2 * k - 1, 2 * k):
            for ref, v in zip((wx, wy, wz, vy, vz, diag, inv), weights(cond, p, fine, z_fine[p])):
                store(ref, p, v)
        for ref, v in zip((cwx, cwy, cwz, cvy, cvz, None, cinv), weights(sum8, k, coarse, z_coarse[k])):
            if ref is not None:
                store(ref, k, v)

    def spread(v, p, refs, level, around_z):
        x, y, z, yb, zb = refs
        step = level[0]
        here = load(v, p)
        n = add(times(load(x, p - 1), load(v, p - 1)), times(load(x, p), load(v, p + 1)))
        n = add(n, times(load(y, p), [ahead(u, 0, step) for u in here]))
        n = add(n, times(load(yb, p), [behind(u, 0, step) for u in here]))
        return add(n, add(times(load(z, p), around_z[0]), times(load(zb, p), around_z[1])))

    def smooth(v, p, refs, scale, level, around_z):
        n = times([(SPREAD_OVER_KEEP / KEEP) * u for u in load(scale, p)], spread(v, p, refs, level, around_z))
        return add(load(v, p), n)

    def between(p, around_z):
        planes, along_y, along_z = seams
        here = load(field, p)
        r = load(src, p)

        def less(r, weights, there, where=None):
            flux = each(lambda w, u, v: w * (u - v), weights, here, there)
            return each(lambda x, y: x - (y if where is None else jnp.where(where, y, 0.0)), r, flux)

        if p in planes:
            r = less(r, load(wx, p), load(field, p + 1))
        if p - 1 in planes:
            r = less(r, load(wx, p - 1), load(field, p - 1))
        r = less(r, load(wy, p), [ahead(v, 0) for v in here], along_y[0])
        r = less(r, load(vy, p), [behind(v, 0) for v in here], along_y[1])
        if along_z is not None:
            r = less(r, load(wz, p), around_z[0], along_z[0])
            r = less(r, load(vz, p), around_z[1], along_z[1])
        return r

    around, coarse_around = (wx, wy, wz, vy, vz), (cwx, cwy, cwz, cvy, cvz)

    for it in range(ITERS):
        halo = 4 * (ITERS - 1 - it)
        blocks = reach(halo + 2)
        rounds = turned(err, planes_of(blocks), fine) if it else z_field
        sums = {}
        for k in blocks:
            found = []
            for p in (2 * k - 1, 2 * k):
                if it == 0:
                    r = between(p, rounds.get(p))
                else:
                    n = spread(err, p, around, fine, rounds[p])
                    r = each(lambda u, d, w, m: u - (d * w - m), load(res, p), load(diag, p), load(err, p), n)
                if it < ITERS - 1:
                    store(res, p, r)
                store(q, p, times(r, load(inv, p)))
                found.append(r)
            sums[k] = add(*found)
        near = reach(halo)
        sums = gather(sums)
        rounds = turned(q, planes_of(near), fine)
        for k, v in sums.items():
            store(cq, k, times([4.0 * v[0]], load(cinv, k)))
        coarse_rounds = turned(cq, near, coarse)
        found = {k: smooth(cq, k, coarse_around, cinv, coarse, coarse_rounds[k])[0] for k in near}
        if parts == 1:
            beside = {k: behind(c, 1) for k, c in found.items()}
            found = {k: jnp.where(even_lane, c, beside[k]) for k, c in found.items()}
        smoothed = {p: smooth(q, p, around, inv, fine, rounds[p]) for p in planes_of(near)}
        for k in near:
            c = jnp.where(even_row, found[k], behind(found[k], 0))
            for p in (2 * k - 1, 2 * k):
                e = [u + c for u in smoothed[p]]
                if it:
                    e = add(load(err, p), e)
                if it < ITERS - 1:
                    store(err, p, e)
                else:
                    out(p, add(load(field, p), e))


def layout(reflect, depth):
    return (1, depth + HALO + 2) if reflect else (1 + HALO, depth + 2 * HALO + 2)


def each_plane(reflect, depth, place):
    odd_x = is_odd("gx")
    own_at, _ = layout(reflect, depth)

    for p in range(depth):
        place(None, jnp.where(odd_x == 1, depth - 1 - p, p) if reflect else p, own_at + p)
    for p in range(HALO):
        if reflect:
            place(0, jnp.where(odd_x == 1, depth - 1 - p, p), own_at + depth + p)
            continue
        for i in range(2):
            above = odd_x == i
            at = jnp.where(above, p, depth - HALO + p)
            place(i, at, jnp.where(above, own_at + depth + p, 1 + p))


def x_seams(reflect, depth):
    own_at, _ = layout(reflect, depth)
    return (own_at + depth - 1,) if reflect else (own_at - 1, own_at + depth - 1)


def out_plane(reflect, depth, p):
    own_at, _ = layout(reflect, depth)
    at = p - own_at
    return jnp.where(is_odd("gx") == 1, depth - 1 - at, at) if reflect else at


def parting(width, lanes):
    column = lax.broadcasted_iota(jnp.int32, (width, 2 * lanes), 0)
    lane = lax.broadcasted_iota(jnp.int32, (width, 2 * lanes), 1)
    wanted = jnp.where(lane < lanes, 2 * lane, 2 * (lane - lanes) + 1)
    return jnp.where((column == wanted) & (wanted < width), 1.0, 0.0)


def ending(width):
    column = lax.broadcasted_iota(jnp.int32, (width, 2 * LANES), 0)
    lane = lax.broadcasted_iota(jnp.int32, (width, 2 * LANES), 1)
    lane = jnp.where(lane < LANES, lane, lane - LANES - LANES // 2)
    last = (lane >= 8) & (lane < 24) & (column == lane + width - 24)
    first = (lane >= 40) & (lane < 56) & (column == lane - 40)
    return jnp.where(last | first, 1.0, 0.0)


def rearranged(v, matrix):
    bf16, f32 = jnp.bfloat16, jnp.float32
    parts = []
    for _ in range(3):
        parts.append(v.astype(bf16))
        v = v - parts[-1].astype(f32)
    matrix = matrix.astype(bf16)
    return jnp.dot(jnp.concatenate(parts, 1), jnp.concatenate([matrix] * 3, 0), preferred_element_type=f32)


def interior(reflect, n_x, *refs):
    own, rim = refs[0], refs[1]
    near, near_rim = refs[2 : 2 + n_x], refs[2 + n_x : 2 + 2 * n_x]
    result, ends = refs[2 + 2 * n_x : 4 + 2 * n_x]
    whole, halves, *cells = refs[4 + 2 * n_x :]
    _, depth, inner, width = own.shape
    rows = inner + 2 * HALO
    lanes = cells[0].shape[3]

    def place(i, p_from, p_to):
        block, halo = (own, rim) if i is None else (near[i], near_rim[i])
        for a in range(3):
            tile = whole.at[a, p_to]
            tile[0:HALO, :] = halo[0, a, p_from]
            tile[HALO : HALO + inner, :] = block[a, p_from]
            tile[HALO + inner : rows, :] = halo[1, a, p_from]

    own_at, total = layout(reflect, depth)
    for a in range(3):
        for p in (0, total - 1):
            cells[a][p] = jnp.zeros((2, rows, lanes), jnp.float32)
            ends[a, p] = jnp.zeros((rows - 8, LANES), jnp.float32)
    each_plane(reflect, depth, place)
    apart = parting(width, lanes)
    target = jnp.concatenate([apart, ending(width)], 1)
    for a in range(3):
        inside = slice(1, total - 1)
        parts = rearranged(whole[a, inside].reshape((total - 2) * rows, width), target).reshape(total - 2, rows, -1)
        for i in range(2):
            cells[a][inside, i] = parts[:, :, i * lanes : (i + 1) * lanes]
        low = parts[:, 0 : rows - 8, 2 * lanes : 2 * lanes + LANES]
        ends[a, inside] = low + parts[:, 8:rows, 2 * lanes + LANES :]

    def out(p, v):
        for i in range(2):
            halves[p - own_at, :, i * lanes : (i + 1) * lanes] = v[i][HALO : rows - HALO, :]

    row = lax.broadcasted_iota(jnp.int32, (rows, lanes), 0)
    along_y = (row == HALO - 1) | (row == HALO + inner - 1), (row == HALO) | (row == HALO + inner)
    solve(cells, own_at, depth, out, (x_seams(reflect, depth), along_y, None))
    together = rearranged(halves[...].reshape(depth * inner, 2 * lanes), apart.T)
    together = together.reshape(depth, inner, width)
    for p in range(depth):
        result[out_plane(reflect, depth, own_at + p)] = together[p]


def edges(reflect, ends, inside, got_a, got_b, result, staged, sems, *cells):
    depth, inner, width = inside.shape
    odd_x, odd_z = is_odd("gx"), is_odd("grp")
    first_z, last_z = beyond("grp")
    lane = lax.broadcasted_iota(jnp.int32, (8, LANES), 1)
    half = LANES // 2
    own_at, total = layout(reflect, depth)
    for p in (0, total - 1):
        for a in range(3):
            cells[a][p, 0] = ends[a, p]

    windows = []

    def place(i, p_from, p_to):
        at_plane = p_from if i is None else (i + 1) * depth + p_from
        if reflect:
            va, vb = got_a[depth + p_from if i is None else p_from], got_b[at_plane]
            swapped = odd_x == 0
        else:
            va, vb = got_a[at_plane], got_b[at_plane]
            swapped = odd_z == 1
        right = jnp.where(last_z, 0.0, jnp.where(swapped, vb, va))
        left = jnp.where(first_z, 0.0, jnp.where(swapped, va, vb))
        windows.append((p_to, right, left, pltpu.roll(right, LANES - 8, 1), pltpu.roll(left, 8, 1)))

    here = lax.rem(lane, half)
    in_halo = (here >= 24) & (here < 40)
    each_plane(reflect, depth, place)
    side = lax.rem(lane, 16) >= 8
    groups = []
    for p, right, left, right_moved, left_moved in windows:
        lower, upper = jnp.where(side, right, left), jnp.where(side, right_moved, left_moved)
        groups.append((p, lower, pltpu.roll(jnp.where(lane < half, upper, lower), half, 1), upper))
    for a in (1, 2, 0):
        for p, *tiles in groups:
            for t, tile in enumerate(tiles):
                moved = tile if a == 1 else pltpu.roll(tile, (16 - 16 * a) % LANES, 1)
                part = slice(8 * t, 8 * t + 8)
                cells[a][p, 0, part, :] = jnp.where(in_halo, moved, ends[a, p, part, :])

    row = lax.broadcasted_iota(jnp.int32, ends.shape[2:], 0)
    lane_in_half = lax.rem(lax.broadcasted_iota(jnp.int32, ends.shape[2:], 1), half)
    upper_half = lax.broadcasted_iota(jnp.int32, ends.shape[2:], 1) >= half
    face = jnp.where(upper_half, inner, HALO)
    along_z = tuple((lane_in_half == at) | (lane_in_half == at + 16) for at in (23, 24))
    finals = []
    solve(cells, own_at, depth, lambda p, v: finals.append((p - own_at, v[0][8:16])), (x_seams(reflect, depth), (row == face - 1, row == face), along_z))
    moved = [
        (p, i, pltpu.roll(v, (LANES - 40 - half * i) % LANES, 1), pltpu.roll(v, (LANES - 24 - half * i) % LANES, 1))
        for p, v in finals
        for i in range(2)
    ]
    copies = []
    for p, i, head, tail in moved:
        at, part = out_plane(reflect, depth, own_at + p), slice(8 * i, 8 * i + 8)
        for c in range(0, width, LANES):
            tile = inside[at, part, c : c + LANES]
            if c == 0:
                tile = jnp.where(lane < HALO, head, tile)
            if c == width - LANES:
                tile = jnp.where(lane >= LANES - HALO, tail, tile)
            staged[p, part, c : c + LANES] = tile
        if i:
            copies.append(pltpu.make_async_copy(staged.at[p], result.at[at], sems.at[p]))
            copies[-1].start()
    for copy in copies:
        copy.wait()


def shards(sizes, source_term, conductivity, initial_field):
    depth, inner, width = source_term.shape
    assert inner == 16 and depth >= HALO and depth % 2 == 0 and width % LANES == 0
    rows = inner + 2 * HALO
    f32 = jnp.float32
    params = pltpu.CompilerParams(vmem_limit_bytes=48 * 1024 * 1024)
    args = (source_term, conductivity, initial_field)

    def exchange(values, axis):
        over, rounds = swaps(axis, sizes)
        found = [lax.ppermute(v, over, pairs) for v, pairs in reversed(list(zip(values, rounds)))]
        return found[::-1] + [jnp.zeros_like(v) for v in values[len(found) :]]

    def work(parts, rows, lanes):
        total = layout(reflect, depth)[1]
        fine = pltpu.VMEM((total, parts, rows, lanes), f32)
        coarse = pltpu.VMEM((total // 2 + 1, 1, rows, lanes), f32)
        return [fine] * 10 + [coarse] * 7 + [fine] * 2 + [coarse] + [fine]

    reflect = sizes["gx"] == 2
    n_x = 1 if reflect else 2
    args = [pltpu.with_memory_space_constraint(v, pltpu.HBM) for v in args]
    face = jax.ShapeDtypeStruct((depth + depth // 2 + n_x + 1, HALO, width), f32)
    own, *msgs = pl.pallas_call(
        functools.partial(prepare, reflect),
        out_shape=(jax.ShapeDtypeStruct((3, depth, inner, width), f32), face, face),
        in_specs=[pl.BlockSpec(memory_space=pltpu.HBM)] * 3, out_specs=(VMEM,) * 3,
        scratch_shapes=[pltpu.SemaphoreType.DMA((3,))], compiler_params=params, name="prepare",
    )(*args)
    got = exchange(msgs, "gy")
    near = exchange([own] * n_x, "gx")
    strips, rim = pl.pallas_call(
        functools.partial(pack_columns, reflect),
        out_shape=(
            jax.ShapeDtypeStruct((2, depth, 8, LANES), f32),
            jax.ShapeDtypeStruct((2, 3, depth, HALO, width), f32),
        ),
        in_specs=[VMEM] * 3, out_specs=(VMEM, VMEM),
        compiler_params=params, name="pack_columns",
    )(own, *got)
    if reflect:
        strips = jnp.concatenate([strips[0]] + exchange([strips[1]], "gx"), axis=0)
    else:
        strips = jnp.concatenate([strips] + exchange([strips] * n_x, "gx"), axis=1)
    strips, rim = lax.optimization_barrier((strips, rim))
    near_rim = exchange([rim] * n_x, "gx")
    if reflect:
        strips = [lax.ppermute(strips, tuple(sizes), crossing(sizes))]
    else:
        strips = exchange([strips[0], strips[1]], "grp")

    block = jax.ShapeDtypeStruct(source_term.shape, f32)
    total = layout(reflect, depth)[1]
    lanes = -(-width // (2 * LANES)) * LANES
    apart = [pltpu.VMEM((3, total, rows, width), f32), pltpu.VMEM((depth, inner, 2 * lanes), f32)]
    inside, ends = pl.pallas_call(
        functools.partial(interior, reflect, n_x),
        out_shape=(block, jax.ShapeDtypeStruct((3, total, rows - 8, LANES), f32)),
        in_specs=[VMEM] * (2 + 2 * n_x), out_specs=(VMEM, VMEM), scratch_shapes=apart + work(2, rows, lanes),
        compiler_params=params, name="interior",
        cost_estimate=pl.CostEstimate(flops=20_000_000, bytes_accessed=20_000_000, transcendentals=0),
    )(own, rim, *near, *near_rim)
    inside, ends, *strips = lax.optimization_barrier((inside, ends, *strips[::-1]))
    strips = strips[::-1]
    if reflect:
        strips += exchange(strips, "gx")
    return pl.pallas_call(
        functools.partial(edges, reflect),
        out_shape=block,
        in_specs=[VMEM] * 4, out_specs=pl.BlockSpec(memory_space=pltpu.HBM),
        scratch_shapes=[pltpu.VMEM((depth, inner, width), f32), pltpu.SemaphoreType.DMA((depth,))] + work(1, rows - 8, LANES),
        compiler_params=params, name="edges",
    )(ends, inside, *strips)


def solution(mesh):
    spec = P("gx", "gy", "grp")
    return jax.shard_map(
        functools.partial(shards, dict(mesh.shape)),
        mesh=mesh,
        in_specs=(spec,) * 3,
        out_specs=spec,
        check_vma=False,
    )
```

```python
import functools

import jax
import jax.numpy as jnp
from jax import lax
from jax.experimental import pallas as pl
from jax.experimental.pallas import tpu as pltpu
from jax.sharding import PartitionSpec as P

ITERS = 2
HALO = 4 * ITERS
LANES = 128
KEEP = 48.0 / 41.0
SPREAD_OVER_KEEP = 2.0 / 3.0
VMEM = pl.BlockSpec(memory_space=pltpu.VMEM)


def ahead(v, axis, n=1):
    return pltpu.roll(v, v.shape[axis] - n, axis)


def behind(v, axis, n=1):
    return pltpu.roll(v, n, axis)


def swaps(axis, sizes):
    count, fill = sizes[axis], sizes["gx"]
    over = [name for name in sizes if name in (axis, "gx")]
    filled = axis != "gx" and fill % 2 == 0

    def at(i, k):
        return i * fill + k if over[0] == axis else k * count + i

    rounds = []
    for start in (0, 1):
        pairs = [(i, i + 1) for i in range(start, count - 1, 2)]
        left = set(range(count)) - {i for pair in pairs for i in pair}
        if not pairs:
            continue
        if filled:
            pairs = [(at(i, k), at(j, k)) for i, j in pairs for k in range(fill)]
            pairs += [(at(i, k), at(i, k + 1)) for i in sorted(left) for k in range(0, fill, 2)]
        rounds.append(pairs + [(j, i) for i, j in pairs])
    return (tuple(over) if filled else axis), rounds


def crossing(sizes):
    names = list(sizes)

    def at(**place):
        index = 0
        for name in names:
            index = index * sizes[name] + place[name]
        return index

    last = sizes["grp"] - 1
    pairs = [
        (at(grp=g, gx=1, gy=y), at(grp=g + 1, gx=0, gy=y)) for g in range(last) for y in range(sizes["gy"])
    ]
    pairs += [
        (at(grp=g, gx=x, gy=y), at(grp=g, gx=x, gy=y + 1))
        for g, x in ((0, 0), (last, 1))
        for y in range(0, sizes["gy"] - 1, 2)
    ]
    return pairs + [(j, i) for i, j in pairs]


def is_odd(axis):
    return lax.rem(lax.axis_index(axis), 2)


def beyond(axis):
    at = lax.axis_index(axis)
    return at == 0, at == lax.axis_size(axis) - 1


def is_odd(axis):
    return lax.rem(lax.axis_index(axis), 2)


def far_row(high, distance):
    if isinstance(high, bool):
        return HALO - distance if high else distance - 1
    return jnp.where(high, HALO - distance, distance - 1)


def shifted_rows(high, v, n):
    if isinstance(high, bool):
        return pltpu.roll(v, HALO - n if high else n, 0)
    return jnp.where(high, pltpu.roll(v, HALO - n, 0), pltpu.roll(v, n, 0))


def inward(high, v):
    return shifted_rows(high, v, HALO - 1)


def both_ends(rows):
    width = rows.shape[1]
    lane = lax.broadcasted_iota(jnp.int32, (rows.shape[0], LANES), 1)
    return jnp.where(lane < LANES // 2, rows[:, 0:LANES], rows[:, width - LANES : width])


def prepare(reflect, s, c, f, own, first, second, sems):
    copies = [pltpu.make_async_copy(ref, own.at[a], sems.at[a]) for a, ref in enumerate((s, c, f))]
    for copy in copies:
        copy.start()
    for copy in copies:
        copy.wait()
    _, depth, inner, width = own.shape
    row = lax.broadcasted_iota(jnp.int32, (inner, width), 0)
    column = lax.broadcasted_iota(jnp.int32, (inner, width), 1)
    outer = jnp.where(is_odd("gx") == 1, depth - 1, 0)
    conds, fields = ([own[a, p] for p in range(depth)] for a in (1, 2))
    next_conds, next_fields = ([ahead(v, 1) for v in values] for values in (conds, fields))
    along_z = [
        jnp.where(column < width - 1, (c + c_next) * (f - f_next), 0.0)
        for c, f, c_next, f_next in zip(conds, fields, next_conds, next_fields)
    ]
    arriving = [behind(v, 1) for v in along_z]
    for p, (cond, field) in enumerate(zip(conds, fields)):
        along_y = jnp.where(row < inner - 1, (cond + ahead(cond, 0)) * (field - ahead(field, 0)), 0.0)
        total = (along_y - behind(along_y, 0)) + (along_z[p] - arriving[p])
        for other in (p - 1, p + 1):
            if 0 <= other < depth:
                total += (cond + conds[other]) * (field - fields[other])
        if reflect and p in (0, depth - 1):
            total += jnp.where(outer == p, cond * field, 0.0)
        own[0, p] = 2.0 * own[0, p] - total

    odd = is_odd("gy")
    row = lax.broadcasted_iota(jnp.int32, (HALO, width), 0)
    lane = lax.broadcasted_iota(jnp.int32, (HALO, LANES), 1)
    for message, high in ((first, odd == 0), (second, odd == 1)):
        rows = pl.ds(pl.multiple_of(jnp.where(high, inner - HALO, 0), 8), HALO)
        at = functools.partial(far_row, high)
        sides = jnp.zeros((HALO, LANES), jnp.float32)
        for p in range(0, depth, 2):
            sums = own[1, p, rows, :] + own[1, p + 1, rows, :]
            sums = sums + inward(high, sums)
            rests = own[0, p, rows, :] + own[0, p + 1, rows, :]
            rests = shifted_rows(high, rests + inward(high, rests), 2)
            for i, seventh in enumerate((sums, rests)):
                field = own[2, p + i, rows, :]
                cond = jnp.where(row == at(7), seventh, own[1, p + i, rows, :])
                message[p + i] = jnp.where(row == at(8), inward(high, field), cond)
                ends = pltpu.roll(both_ends(field), 2 * (p + i) + 1, 1)
                sides = jnp.where(lane // 2 == p + i, ends, sides)
            near = jnp.where(high, HALO - 1 - row, row) < 4
            message[depth + p // 2] = jnp.where(near, own[0, p, rows, :], pltpu.roll(own[0, p + 1, rows, :], 4, 0))
        planes = depth + depth // 2
        if reflect:
            message[planes] = own[2, depth - 1 - outer, rows, :]
        else:
            message[planes] = own[2, 0, rows, :]
            message[planes + 1] = own[2, depth - 1, rows, :]
        message[message.shape[0] - 1] = jnp.zeros((HALO, width), jnp.float32)
        message[message.shape[0] - 1, :, 0:LANES] = sides


def head_lane(a, g):
    return 8 + 16 * a + LANES // 2 * (g % 2) + 8 * (g // 2)


def tail_lane(a, g):
    return 8 + 16 * a + LANES // 2 * (g % 2) + 8 * (1 - g // 2)


def pack_columns(reflect, own, got_a, got_b, strips, rim):
    odd_y, odd_z = is_odd("gy"), is_odd("grp")
    first_y, last_y = beyond("gy")
    _, depth, inner, width = own.shape
    groups = inner // 8 + 2
    odd_x = is_odd("gx")
    lane = lax.broadcasted_iota(jnp.int32, (8, LANES), 1)
    row = lax.broadcasted_iota(jnp.int32, (8, width), 0)
    wide = lax.broadcasted_iota(jnp.int32, (8, width), 1)

    def spread_out(v):
        return jnp.concatenate([v] * (width // LANES), 1)

    for p in range(depth):
        for side, (low, outside) in enumerate(((True, first_y), (False, last_y))):

            at = functools.partial(far_row, low)

            def take(i):
                strip = jnp.where(odd_y == (1 if low else 0), got_a[i], got_b[i])
                return jnp.where(outside, 0.0, strip)

            cond, mixed = take(p), take(depth + p // 2)
            g = mixed if p % 2 == 0 else pltpu.roll(mixed, 4, 0)
            g = jnp.where(row >= 4 if low else row < 4, g, 0.0)
            if p % 2:
                g = jnp.where(row == at(5), shifted_rows(low, cond, HALO - 2), g)
            sides = take(got_a.shape[0] - 1)[:, 0:LANES]
            ends = spread_out(pltpu.roll(sides, LANES - 1 - 2 * p, 1))
            field = jnp.where((wide == 0) | (wide == width - 1), ends, 0.0)
            field = jnp.where(row == at(1), shifted_rows(low, cond, 1), field)
            planes = depth + depth // 2
            if reflect and p in (0, depth - 1):
                field = jnp.where(odd_x == (1 if p == 0 else 0), take(planes), field)
            elif not reflect and p in (0, depth - 1):
                field = take(planes + (0 if p == 0 else 1))
            cond = jnp.where(row == at(8), 0.0, cond)
            if p % 2:
                cond = jnp.where(row == at(7), 0.0, cond)
            rim[side, 0, p] = g
            rim[side, 1, p] = cond
            rim[side, 2, p] = field
    moved = {}
    for p in range(depth):
        for a in range(3):
            for g in range(groups):
                if g == 0 or g == groups - 1:
                    rows = rim[min(g, 1), a, p]
                else:
                    rows = own[a, p, 8 * g - 8 : 8 * g, :]
                to_head, to_tail = head_lane(a, g), tail_lane(a, g)
                if to_head == to_tail + HALO:
                    ends = pltpu.roll(both_ends(rows), to_head, 1)
                    moved[p, a, g] = ends, ends
                else:
                    last = pltpu.roll(rows[:, width - LANES : width], (to_tail + HALO) % LANES, 1)
                    moved[p, a, g] = pltpu.roll(rows[:, 0:LANES], to_head, 1), last
    for p in range(depth):
        head = tail = jnp.zeros((8, LANES), jnp.float32)
        for a in range(3):
            for g in range(groups):
                to_head, to_tail = head_lane(a, g), tail_lane(a, g)
                head = jnp.where((lane >= to_head) & (lane < to_head + HALO), moved[p, a, g][0], head)
                tail = jnp.where((lane >= to_tail) & (lane < to_tail + HALO), moved[p, a, g][1], tail)
        swapped = (odd_x if reflect else odd_z) == 1
        strips[0, p] = jnp.where(swapped, tail, head) if reflect else jnp.where(swapped, head, tail)
        strips[1, p] = jnp.where(swapped, head, tail) if reflect else jnp.where(swapped, tail, head)


def shifts(parts, step):
    if parts == 1:
        return (lambda v: [ahead(v[0], 1, step)]), (lambda v: [behind(v[0], 1, step)])
    return (lambda v: [v[1], ahead(v[0], 1)]), (lambda v: [behind(v[1], 1), v[0]])


def each(op, *lists):
    return [op(*values) for values in zip(*lists)]


def add(*lists):
    return each(lambda *values: functools.reduce(lambda x, y: x + y, values), *lists)


def times(x, y):
    return each(lambda v, w: v * w, x, y)


def solve(cells, own_at, own, out, seams):
    (src, cond, field, wx, wy, wz, vy, vz, diag, inv, sum8, cwx, cwy, cwz, cvy, cvz, cinv, res, q, cq, err) = cells
    total, parts, rows, lanes = cond.shape

    def load(ref, p):
        return [ref[p, i] for i in range(ref.shape[1])]

    def store(ref, p, values):
        for i, v in enumerate(values):
            ref[p, i] = v

    def reach(halo):
        low = max(1, own_at - halo)
        high = min(total, own_at + own + halo)
        return range((low + 1) // 2, (high + 1) // 2)

    fine = (1, *shifts(parts, 1))
    coarse = (2, *shifts(1, 3 - parts))
    zero = jnp.zeros((rows, lanes), jnp.float32)
    for ref in (q, cq, err, sum8):
        store(ref, 0, [zero] * ref.shape[1])

    even_row = lax.rem(lax.broadcasted_iota(jnp.int32, (rows, lanes), 0), 2) == 0
    even_lane = lax.rem(lax.broadcasted_iota(jnp.int32, (rows, lanes), 1), 2) == 0

    def turned(ref, planes, level):
        here = {p: load(ref, p) for p in planes}
        return {p: (level[1](v), level[2](v)) for p, v in here.items()}

    def planes_of(blocks):
        return [p for k in blocks for p in (2 * k - 1, 2 * k)]

    def gather(sums):
        sums = {k: [v[0] + ahead(v[0], 0)] if parts == 1 else [v[0] + v[1]] for k, v in sums.items()}
        if parts == 1:
            nexts, lasts = ([shift(v[0], 1) for v in sums.values()] for shift in (ahead, behind))
            return {
                k: [v[0] + jnp.where(even_lane, u, w)] for (k, v), u, w in zip(sums.items(), nexts, lasts)
            }
        return {k: [v[0] + ahead(v[0], 0)] for k, v in sums.items()}

    z_fine = turned(cond, planes_of(reach(HALO - 2)), fine)
    for k, v in gather({k: add(load(cond, 2 * k - 1), load(cond, 2 * k)) for k in reach(HALO)}).items():
        store(sum8, k, v)
    z_field = turned(field, planes_of(reach(HALO - 2)), fine) if seams[2] is not None else {}

    def weights(ref, p, level, around_z):
        step = level[0]
        c = load(ref, p)
        x = add(c, load(ref, p + 1))
        y, yb = ([v + shift(v, 0, step) for v in c] for shift in (ahead, behind))
        z, zb = (add(c, v) for v in around_z)
        k = add(add(c, load(ref, p - 1), x), add(y, yb), add(z, zb))
        return x, y, z, yb, zb, k, each(lambda v, w: jnp.where(v > 0.0, KEEP / w, 0.0), c, k)

    low = reach(HALO - 2).start
    store(wx, 2 * low - 2, add(load(cond, 2 * low - 2), load(cond, 2 * low - 1)))
    store(cwx, low - 1, add(load(sum8, low - 1), load(sum8, low)))
    z_coarse = turned(sum8, reach(HALO - 2), coarse)
    for k in reach(HALO - 2):
        for p in (2 * k - 1, 2 * k):
            for ref, v in zip((wx, wy, wz, vy, vz, diag, inv), weights(cond, p, fine, z_fine[p])):
                store(ref, p, v)
        for ref, v in zip((cwx, cwy, cwz, cvy, cvz, None, cinv), weights(sum8, k, coarse, z_coarse[k])):
            if ref is not None:
                store(ref, k, v)

    def spread(v, p, refs, level, around_z):
        x, y, z, yb, zb = refs
        step = level[0]
        here = load(v, p)
        n = add(times(load(x, p - 1), load(v, p - 1)), times(load(x, p), load(v, p + 1)))
        n = add(n, times(load(y, p), [ahead(u, 0, step) for u in here]))
        n = add(n, times(load(yb, p), [behind(u, 0, step) for u in here]))
        return add(n, add(times(load(z, p), around_z[0]), times(load(zb, p), around_z[1])))

    def smooth(v, p, refs, scale, level, around_z):
        n = times([(SPREAD_OVER_KEEP / KEEP) * u for u in load(scale, p)], spread(v, p, refs, level, around_z))
        return add(load(v, p), n)

    def between(p, around_z):
        planes, along_y, along_z = seams
        here = load(field, p)
        r = load(src, p)

        def less(r, weights, there, where=None):
            flux = each(lambda w, u, v: w * (u - v), weights, here, there)
            return each(lambda x, y: x - (y if where is None else jnp.where(where, y, 0.0)), r, flux)

        if p in planes:
            r = less(r, load(wx, p), load(field, p + 1))
        if p - 1 in planes:
            r = less(r, load(wx, p - 1), load(field, p - 1))
        r = less(r, load(wy, p), [ahead(v, 0) for v in here], along_y[0])
        r = less(r, load(vy, p), [behind(v, 0) for v in here], along_y[1])
        if along_z is not None:
            r = less(r, load(wz, p), around_z[0], along_z[0])
            r = less(r, load(vz, p), around_z[1], along_z[1])
        return r

    around, coarse_around = (wx, wy, wz, vy, vz), (cwx, cwy, cwz, cvy, cvz)

    for it in range(ITERS):
        halo = 4 * (ITERS - 1 - it)
        blocks = reach(halo + 2)
        rounds = turned(err, planes_of(blocks), fine) if it else z_field
        sums = {}
        for k in blocks:
            found = []
            for p in (2 * k - 1, 2 * k):
                if it == 0:
                    r = between(p, rounds.get(p))
                else:
                    n = spread(err, p, around, fine, rounds[p])
                    r = each(lambda u, d, w, m: u - (d * w - m), load(res, p), load(diag, p), load(err, p), n)
                if it < ITERS - 1:
                    store(res, p, r)
                store(q, p, times(r, load(inv, p)))
                found.append(r)
            sums[k] = add(*found)
        near = reach(halo)
        sums = gather(sums)
        rounds = turned(q, planes_of(near), fine)
        for k, v in sums.items():
            store(cq, k, times([4.0 * v[0]], load(cinv, k)))
        coarse_rounds = turned(cq, near, coarse)
        found = {k: smooth(cq, k, coarse_around, cinv, coarse, coarse_rounds[k])[0] for k in near}
        smoothed = {p: smooth(q, p, around, inv, fine, rounds[p]) for p in planes_of(near)}
        for k in near:
            c = jnp.where(even_row, found[k], behind(found[k], 0))
            for p in (2 * k - 1, 2 * k):
                e = [u + c for u in smoothed[p]]
                if it:
                    e = add(load(err, p), e)
                if it < ITERS - 1:
                    store(err, p, e)
                else:
                    out(p, add(load(field, p), e))


def layout(reflect, depth):
    return (1, depth + HALO + 2) if reflect else (1 + HALO, depth + 2 * HALO + 2)


def each_plane(reflect, depth, place):
    odd_x = is_odd("gx")
    own_at, _ = layout(reflect, depth)

    for p in range(depth):
        place(None, jnp.where(odd_x == 1, depth - 1 - p, p) if reflect else p, own_at + p)
    for p in range(HALO):
        if reflect:
            place(0, jnp.where(odd_x == 1, depth - 1 - p, p), own_at + depth + p)
            continue
        for i in range(2):
            above = odd_x == i
            at = jnp.where(above, p, depth - HALO + p)
            place(i, at, jnp.where(above, own_at + depth + p, 1 + p))


def x_seams(reflect, depth):
    own_at, _ = layout(reflect, depth)
    return (own_at + depth - 1,) if reflect else (own_at - 1, own_at + depth - 1)


def out_plane(reflect, depth, p):
    own_at, _ = layout(reflect, depth)
    at = p - own_at
    return jnp.where(is_odd("gx") == 1, depth - 1 - at, at) if reflect else at


def parting(width, lanes):
    column = lax.broadcasted_iota(jnp.int32, (width, 2 * lanes), 0)
    lane = lax.broadcasted_iota(jnp.int32, (width, 2 * lanes), 1)
    wanted = jnp.where(lane < lanes, 2 * lane, 2 * (lane - lanes) + 1)
    return jnp.where((column == wanted) & (wanted < width), 1.0, 0.0)


def ending(width):
    column = lax.broadcasted_iota(jnp.int32, (width, 2 * LANES), 0)
    lane = lax.broadcasted_iota(jnp.int32, (width, 2 * LANES), 1)
    lane = jnp.where(lane < LANES, lane, lane - LANES - LANES // 2)
    last = (lane >= 8) & (lane < 24) & (column == lane + width - 24)
    first = (lane >= 40) & (lane < 56) & (column == lane - 40)
    return jnp.where(last | first, 1.0, 0.0)


def rearranged(v, matrix):
    bf16, f32 = jnp.bfloat16, jnp.float32
    parts = []
    for _ in range(3):
        parts.append(v.astype(bf16))
        v = v - parts[-1].astype(f32)
    matrix = matrix.astype(bf16)
    return jnp.dot(jnp.concatenate(parts, 1), jnp.concatenate([matrix] * 3, 0), preferred_element_type=f32)


def interior(reflect, n_x, *refs):
    own, rim = refs[0], refs[1]
    near, near_rim = refs[2 : 2 + n_x], refs[2 + n_x : 2 + 2 * n_x]
    result, ends = refs[2 + 2 * n_x : 4 + 2 * n_x]
    whole, halves, *cells = refs[4 + 2 * n_x :]
    _, depth, inner, width = own.shape
    rows = inner + 2 * HALO
    lanes = cells[0].shape[3]

    def place(i, p_from, p_to):
        block, halo = (own, rim) if i is None else (near[i], near_rim[i])
        for a in range(3):
            tile = whole.at[a, p_to]
            tile[0:HALO, :] = halo[0, a, p_from]
            tile[HALO : HALO + inner, :] = block[a, p_from]
            tile[HALO + inner : rows, :] = halo[1, a, p_from]

    own_at, total = layout(reflect, depth)
    for a in range(3):
        for p in (0, total - 1):
            cells[a][p] = jnp.zeros((2, rows, lanes), jnp.float32)
            ends[a, p] = jnp.zeros((rows - 8, LANES), jnp.float32)
    each_plane(reflect, depth, place)
    apart = parting(width, lanes)
    target = jnp.concatenate([apart, ending(width)], 1)
    for a in range(3):
        inside = slice(1, total - 1)
        parts = rearranged(whole[a, inside].reshape((total - 2) * rows, width), target).reshape(total - 2, rows, -1)
        for i in range(2):
            cells[a][inside, i] = parts[:, :, i * lanes : (i + 1) * lanes]
        low = parts[:, 0 : rows - 8, 2 * lanes : 2 * lanes + LANES]
        ends[a, inside] = low + parts[:, 8:rows, 2 * lanes + LANES :]

    def out(p, v):
        for i in range(2):
            halves[p - own_at, :, i * lanes : (i + 1) * lanes] = v[i][HALO : rows - HALO, :]

    row = lax.broadcasted_iota(jnp.int32, (rows, lanes), 0)
    along_y = (row == HALO - 1) | (row == HALO + inner - 1), (row == HALO) | (row == HALO + inner)
    solve(cells, own_at, depth, out, (x_seams(reflect, depth), along_y, None))
    together = rearranged(halves[...].reshape(depth * inner, 2 * lanes), apart.T)
    together = together.reshape(depth, inner, width)
    for p in range(depth):
        result[out_plane(reflect, depth, own_at + p)] = together[p]


def edges(reflect, ends, inside, got_a, got_b, result, staged, sems, *cells):
    depth, inner, width = inside.shape
    odd_x, odd_z = is_odd("gx"), is_odd("grp")
    first_z, last_z = beyond("grp")
    lane = lax.broadcasted_iota(jnp.int32, (8, LANES), 1)
    half = LANES // 2
    own_at, total = layout(reflect, depth)
    for p in (0, total - 1):
        for a in range(3):
            cells[a][p, 0] = ends[a, p]

    windows = []

    def place(i, p_from, p_to):
        at_plane = p_from if i is None else (i + 1) * depth + p_from
        if reflect:
            va, vb = got_a[depth + p_from if i is None else p_from], got_b[at_plane]
            swapped = odd_x == 0
        else:
            va, vb = got_a[at_plane], got_b[at_plane]
            swapped = odd_z == 1
        right = jnp.where(last_z, 0.0, jnp.where(swapped, vb, va))
        left = jnp.where(first_z, 0.0, jnp.where(swapped, va, vb))
        windows.append((p_to, right, left, pltpu.roll(right, LANES - 8, 1), pltpu.roll(left, 8, 1)))

    here = lax.rem(lane, half)
    in_halo = (here >= 24) & (here < 40)
    each_plane(reflect, depth, place)
    side = lax.rem(lane, 16) >= 8
    groups = []
    for p, right, left, right_moved, left_moved in windows:
        lower, upper = jnp.where(side, right, left), jnp.where(side, right_moved, left_moved)
        groups.append((p, lower, pltpu.roll(jnp.where(lane < half, upper, lower), half, 1), upper))
    for a in (1, 2, 0):
        for p, *tiles in groups:
            for t, tile in enumerate(tiles):
                moved = tile if a == 1 else pltpu.roll(tile, (16 - 16 * a) % LANES, 1)
                part = slice(8 * t, 8 * t + 8)
                cells[a][p, 0, part, :] = jnp.where(in_halo, moved, ends[a, p, part, :])

    row = lax.broadcasted_iota(jnp.int32, ends.shape[2:], 0)
    lane_in_half = lax.rem(lax.broadcasted_iota(jnp.int32, ends.shape[2:], 1), half)
    upper_half = lax.broadcasted_iota(jnp.int32, ends.shape[2:], 1) >= half
    face = jnp.where(upper_half, inner, HALO)
    along_z = tuple((lane_in_half == at) | (lane_in_half == at + 16) for at in (23, 24))
    finals = []
    solve(cells, own_at, depth, lambda p, v: finals.append((p - own_at, v[0][8:16])), (x_seams(reflect, depth), (row == face - 1, row == face), along_z))
    moved = [
        (p, i, pltpu.roll(v, (LANES - 40 - half * i) % LANES, 1), pltpu.roll(v, (LANES - 24 - half * i) % LANES, 1))
        for p, v in finals
        for i in range(2)
    ]
    copies = []
    for p, i, head, tail in moved:
        at, part = out_plane(reflect, depth, own_at + p), slice(8 * i, 8 * i + 8)
        for c in range(0, width, LANES):
            tile = inside[at, part, c : c + LANES]
            if c == 0:
                tile = jnp.where(lane < HALO, head, tile)
            if c == width - LANES:
                tile = jnp.where(lane >= LANES - HALO, tail, tile)
            staged[p, part, c : c + LANES] = tile
        if i:
            copies.append(pltpu.make_async_copy(staged.at[p], result.at[at], sems.at[p]))
            copies[-1].start()
    for copy in copies:
        copy.wait()


def shards(sizes, source_term, conductivity, initial_field):
    depth, inner, width = source_term.shape
    assert inner == 16 and depth >= HALO and depth % 2 == 0 and width % LANES == 0
    rows = inner + 2 * HALO
    f32 = jnp.float32
    params = pltpu.CompilerParams(vmem_limit_bytes=48 * 1024 * 1024)
    args = (source_term, conductivity, initial_field)

    def exchange(values, axis):
        over, rounds = swaps(axis, sizes)
        found = [lax.ppermute(v, over, pairs) for v, pairs in reversed(list(zip(values, rounds)))]
        return found[::-1] + [jnp.zeros_like(v) for v in values[len(found) :]]

    def work(parts, rows, lanes):
        total = layout(reflect, depth)[1]
        fine = pltpu.VMEM((total, parts, rows, lanes), f32)
        coarse = pltpu.VMEM((total // 2 + 1, 1, rows, lanes), f32)
        return [fine] * 10 + [coarse] * 7 + [fine] * 2 + [coarse] + [fine]

    reflect = sizes["gx"] == 2
    n_x = 1 if reflect else 2
    args = [pltpu.with_memory_space_constraint(v, pltpu.HBM) for v in args]
    face = jax.ShapeDtypeStruct((depth + depth // 2 + n_x + 1, HALO, width), f32)
    own, *msgs = pl.pallas_call(
        functools.partial(prepare, reflect),
        out_shape=(jax.ShapeDtypeStruct((3, depth, inner, width), f32), face, face),
        in_specs=[pl.BlockSpec(memory_space=pltpu.HBM)] * 3, out_specs=(VMEM,) * 3,
        scratch_shapes=[pltpu.SemaphoreType.DMA((3,))], compiler_params=params, name="prepare",
    )(*args)
    got = exchange(msgs, "gy")
    near = exchange([own] * n_x, "gx")
    strips, rim = pl.pallas_call(
        functools.partial(pack_columns, reflect),
        out_shape=(
            jax.ShapeDtypeStruct((2, depth, 8, LANES), f32),
            jax.ShapeDtypeStruct((2, 3, depth, HALO, width), f32),
        ),
        in_specs=[VMEM] * 3, out_specs=(VMEM, VMEM),
        compiler_params=params, name="pack_columns",
    )(own, *got)
    if reflect:
        strips = jnp.concatenate([strips[0]] + exchange([strips[1]], "gx"), axis=0)
    else:
        strips = jnp.concatenate([strips] + exchange([strips] * n_x, "gx"), axis=1)
    strips, rim = lax.optimization_barrier((strips, rim))
    near_rim = exchange([rim] * n_x, "gx")
    if reflect:
        strips = [lax.ppermute(strips, tuple(sizes), crossing(sizes))]
    else:
        strips = exchange([strips[0], strips[1]], "grp")

    block = jax.ShapeDtypeStruct(source_term.shape, f32)
    total = layout(reflect, depth)[1]
    lanes = -(-width // (2 * LANES)) * LANES
    apart = [pltpu.VMEM((3, total, rows, width), f32), pltpu.VMEM((depth, inner, 2 * lanes), f32)]
    inside, ends = pl.pallas_call(
        functools.partial(interior, reflect, n_x),
        out_shape=(block, jax.ShapeDtypeStruct((3, total, rows - 8, LANES), f32)),
        in_specs=[VMEM] * (2 + 2 * n_x), out_specs=(VMEM, VMEM), scratch_shapes=apart + work(2, rows, lanes),
        compiler_params=params, name="interior",
        cost_estimate=pl.CostEstimate(flops=20_000_000, bytes_accessed=20_000_000, transcendentals=0),
    )(own, rim, *near, *near_rim)
    inside, ends, *strips = lax.optimization_barrier((inside, ends, *strips[::-1]))
    strips = strips[::-1]
    if reflect:
        strips += exchange(strips, "gx")
    return pl.pallas_call(
        functools.partial(edges, reflect),
        out_shape=block,
        in_specs=[VMEM] * 4, out_specs=pl.BlockSpec(memory_space=pltpu.HBM),
        scratch_shapes=[pltpu.VMEM((depth, inner, width), f32), pltpu.SemaphoreType.DMA((depth,))] + work(1, rows - 8, LANES),
        compiler_params=params, name="edges",
    )(ends, inside, *strips)


def solution(mesh):
    spec = P("gx", "gy", "grp")
    return jax.shard_map(
        functools.partial(shards, dict(mesh.shape)),
        mesh=mesh,
        in_specs=(spec,) * 3,
        out_specs=spec,
        check_vma=False,
    )
```

```python
import functools

import jax
import jax.numpy as jnp
from jax import lax
from jax.experimental import pallas as pl
from jax.experimental.pallas import tpu as pltpu
from jax.sharding import PartitionSpec as P

ITERS = 2
HALO = 4 * ITERS
LANES = 128
KEEP = 48.0 / 41.0
SPREAD_OVER_KEEP = 2.0 / 3.0
VMEM = pl.BlockSpec(memory_space=pltpu.VMEM)


def ahead(v, axis, n=1):
    return pltpu.roll(v, v.shape[axis] - n, axis)


def behind(v, axis, n=1):
    return pltpu.roll(v, n, axis)


def swaps(axis, sizes):
    count, fill = sizes[axis], sizes["gx"]
    over = [name for name in sizes if name in (axis, "gx")]
    filled = axis != "gx" and fill % 2 == 0

    def at(i, k):
        return i * fill + k if over[0] == axis else k * count + i

    rounds = []
    for start in (0, 1):
        pairs = [(i, i + 1) for i in range(start, count - 1, 2)]
        left = set(range(count)) - {i for pair in pairs for i in pair}
        if not pairs:
            continue
        if filled:
            pairs = [(at(i, k), at(j, k)) for i, j in pairs for k in range(fill)]
            pairs += [(at(i, k), at(i, k + 1)) for i in sorted(left) for k in range(0, fill, 2)]
        rounds.append(pairs + [(j, i) for i, j in pairs])
    return (tuple(over) if filled else axis), rounds


def crossing(sizes):
    names = list(sizes)

    def at(**place):
        index = 0
        for name in names:
            index = index * sizes[name] + place[name]
        return index

    last = sizes["grp"] - 1
    pairs = [
        (at(grp=g, gx=1, gy=y), at(grp=g + 1, gx=0, gy=y)) for g in range(last) for y in range(sizes["gy"])
    ]
    pairs += [
        (at(grp=g, gx=x, gy=y), at(grp=g, gx=x, gy=y + 1))
        for g, x in ((0, 0), (last, 1))
        for y in range(0, sizes["gy"] - 1, 2)
    ]
    return pairs + [(j, i) for i, j in pairs]


def is_odd(axis):
    return lax.rem(lax.axis_index(axis), 2)


def beyond(axis):
    at = lax.axis_index(axis)
    return at == 0, at == lax.axis_size(axis) - 1


def is_odd(axis):
    return lax.rem(lax.axis_index(axis), 2)


def far_row(high, distance):
    if isinstance(high, bool):
        return HALO - distance if high else distance - 1
    return jnp.where(high, HALO - distance, distance - 1)


def shifted_rows(high, v, n):
    if isinstance(high, bool):
        return pltpu.roll(v, HALO - n if high else n, 0)
    return jnp.where(high, pltpu.roll(v, HALO - n, 0), pltpu.roll(v, n, 0))


def inward(high, v):
    return shifted_rows(high, v, HALO - 1)


def both_ends(rows):
    width = rows.shape[1]
    lane = lax.broadcasted_iota(jnp.int32, (rows.shape[0], LANES), 1)
    return jnp.where(lane < LANES // 2, rows[:, 0:LANES], rows[:, width - LANES : width])


def prepare(reflect, s, c, f, own, first, second, sems):
    copies = [pltpu.make_async_copy(ref, own.at[a], sems.at[a]) for a, ref in enumerate((s, c, f))]
    for copy in copies:
        copy.start()
    for copy in copies:
        copy.wait()
    _, depth, inner, width = own.shape
    row = lax.broadcasted_iota(jnp.int32, (inner, width), 0)
    column = lax.broadcasted_iota(jnp.int32, (inner, width), 1)
    outer = jnp.where(is_odd("gx") == 1, depth - 1, 0)
    conds, fields = ([own[a, p] for p in range(depth)] for a in (1, 2))
    next_conds, next_fields = ([ahead(v, 1) for v in values] for values in (conds, fields))
    along_z = [
        jnp.where(column < width - 1, (c + c_next) * (f - f_next), 0.0)
        for c, f, c_next, f_next in zip(conds, fields, next_conds, next_fields)
    ]
    arriving = [behind(v, 1) for v in along_z]
    for p, (cond, field) in enumerate(zip(conds, fields)):
        along_y = jnp.where(row < inner - 1, (cond + ahead(cond, 0)) * (field - ahead(field, 0)), 0.0)
        total = (along_y - behind(along_y, 0)) + (along_z[p] - arriving[p])
        for other in (p - 1, p + 1):
            if 0 <= other < depth:
                total += (cond + conds[other]) * (field - fields[other])
        if reflect and p in (0, depth - 1):
            total += jnp.where(outer == p, cond * field, 0.0)
        own[0, p] = 2.0 * own[0, p] - total

    odd = is_odd("gy")
    row = lax.broadcasted_iota(jnp.int32, (HALO, width), 0)
    lane = lax.broadcasted_iota(jnp.int32, (HALO, LANES), 1)
    for message, high in ((first, odd == 0), (second, odd == 1)):
        rows = pl.ds(pl.multiple_of(jnp.where(high, inner - HALO, 0), 8), HALO)
        at = functools.partial(far_row, high)
        sides = jnp.zeros((HALO, LANES), jnp.float32)
        for p in range(0, depth, 2):
            sums = own[1, p, rows, :] + own[1, p + 1, rows, :]
            sums = sums + inward(high, sums)
            rests = own[0, p, rows, :] + own[0, p + 1, rows, :]
            rests = shifted_rows(high, rests + inward(high, rests), 2)
            for i, seventh in enumerate((sums, rests)):
                field = own[2, p + i, rows, :]
                cond = jnp.where(row == at(7), seventh, own[1, p + i, rows, :])
                message[p + i] = jnp.where(row == at(8), inward(high, field), cond)
                ends = pltpu.roll(both_ends(field), 2 * (p + i) + 1, 1)
                sides = jnp.where(lane // 2 == p + i, ends, sides)
            near = jnp.where(high, HALO - 1 - row, row) < 4
            message[depth + p // 2] = jnp.where(near, own[0, p, rows, :], pltpu.roll(own[0, p + 1, rows, :], 4, 0))
        planes = depth + depth // 2
        if reflect:
            message[planes] = own[2, depth - 1 - outer, rows, :]
        else:
            message[planes] = own[2, 0, rows, :]
            message[planes + 1] = own[2, depth - 1, rows, :]
        message[message.shape[0] - 1] = jnp.zeros((HALO, width), jnp.float32)
        message[message.shape[0] - 1, :, 0:LANES] = sides


def head_lane(a, g):
    return 8 + 16 * a + LANES // 2 * (g % 2) + 8 * (g // 2)


def tail_lane(a, g):
    return 8 + 16 * a + LANES // 2 * (g % 2) + 8 * (1 - g // 2)


def pack_columns(reflect, own, got_a, got_b, strips, rim):
    odd_y, odd_z = is_odd("gy"), is_odd("grp")
    first_y, last_y = beyond("gy")
    _, depth, inner, width = own.shape
    groups = inner // 8 + 2
    odd_x = is_odd("gx")
    lane = lax.broadcasted_iota(jnp.int32, (8, LANES), 1)
    row = lax.broadcasted_iota(jnp.int32, (8, width), 0)
    wide = lax.broadcasted_iota(jnp.int32, (8, width), 1)

    def spread_out(v):
        return jnp.concatenate([v] * (width // LANES), 1)

    for p in range(depth):
        for side, (low, outside) in enumerate(((True, first_y), (False, last_y))):

            at = functools.partial(far_row, low)

            def take(i):
                strip = jnp.where(odd_y == (1 if low else 0), got_a[i], got_b[i])
                return jnp.where(outside, 0.0, strip)

            cond, mixed = take(p), take(depth + p // 2)
            g = mixed if p % 2 == 0 else pltpu.roll(mixed, 4, 0)
            g = jnp.where(row >= 4 if low else row < 4, g, 0.0)
            if p % 2:
                g = jnp.where(row == at(5), shifted_rows(low, cond, HALO - 2), g)
            sides = take(got_a.shape[0] - 1)[:, 0:LANES]
            ends = spread_out(pltpu.roll(sides, LANES - 1 - 2 * p, 1))
            field = jnp.where((wide == 0) | (wide == width - 1), ends, 0.0)
            field = jnp.where(row == at(1), shifted_rows(low, cond, 1), field)
            planes = depth + depth // 2
            if reflect and p in (0, depth - 1):
                field = jnp.where(odd_x == (1 if p == 0 else 0), take(planes), field)
            elif not reflect and p in (0, depth - 1):
                field = take(planes + (0 if p == 0 else 1))
            cond = jnp.where(row == at(8), 0.0, cond)
            if p % 2:
                cond = jnp.where(row == at(7), 0.0, cond)
            rim[side, 0, p] = g
            rim[side, 1, p] = cond
            rim[side, 2, p] = field
    moved = {}
    for p in range(depth):
        for a in range(3):
            for g in range(groups):
                if g == 0 or g == groups - 1:
                    rows = rim[min(g, 1), a, p]
                else:
                    rows = own[a, p, 8 * g - 8 : 8 * g, :]
                to_head, to_tail = head_lane(a, g), tail_lane(a, g)
                if to_head == to_tail + HALO:
                    ends = pltpu.roll(both_ends(rows), to_head, 1)
                    moved[p, a, g] = ends, ends
                else:
                    last = pltpu.roll(rows[:, width - LANES : width], (to_tail + HALO) % LANES, 1)
                    moved[p, a, g] = pltpu.roll(rows[:, 0:LANES], to_head, 1), last
    for p in range(depth):
        head = tail = jnp.zeros((8, LANES), jnp.float32)
        for a in range(3):
            for g in range(groups):
                to_head, to_tail = head_lane(a, g), tail_lane(a, g)
                head = jnp.where((lane >= to_head) & (lane < to_head + HALO), moved[p, a, g][0], head)
                tail = jnp.where((lane >= to_tail) & (lane < to_tail + HALO), moved[p, a, g][1], tail)
        swapped = (odd_x if reflect else odd_z) == 1
        strips[0, p] = jnp.where(swapped, tail, head) if reflect else jnp.where(swapped, head, tail)
        strips[1, p] = jnp.where(swapped, head, tail) if reflect else jnp.where(swapped, tail, head)


def shifts(parts, step):
    if parts == 1:
        return (lambda v: [ahead(v[0], 1, step)]), (lambda v: [behind(v[0], 1, step)])
    return (lambda v: [v[1], ahead(v[0], 1)]), (lambda v: [behind(v[1], 1), v[0]])


def each(op, *lists):
    return [op(*values) for values in zip(*lists)]


def add(*lists):
    return each(lambda *values: functools.reduce(lambda x, y: x + y, values), *lists)


def times(x, y):
    return each(lambda v, w: v * w, x, y)


def solve(cells, own_at, own, out, seams):
    (src, cond, field, wx, wy, wz, vy, vz, diag, inv, sum8, cwx, cwy, cwz, cvy, cvz, cinv, res, q, cq, err) = cells
    total, parts, rows, lanes = cond.shape

    def load(ref, p):
        return [ref[p, i] for i in range(ref.shape[1])]

    def store(ref, p, values):
        for i, v in enumerate(values):
            ref[p, i] = v

    def reach(halo):
        low = max(1, own_at - halo)
        high = min(total, own_at + own + halo)
        return range((low + 1) // 2, (high + 1) // 2)

    fine = (1, *shifts(parts, 1))
    coarse = (2, *shifts(1, 3 - parts))
    zero = jnp.zeros((rows, lanes), jnp.float32)
    for ref in (q, cq, err, sum8):
        store(ref, 0, [zero] * ref.shape[1])

    even_row = lax.rem(lax.broadcasted_iota(jnp.int32, (rows, lanes), 0), 2) == 0
    even_lane = lax.rem(lax.broadcasted_iota(jnp.int32, (rows, lanes), 1), 2) == 0

    def turned(ref, planes, level):
        here = {p: load(ref, p) for p in planes}
        return {p: (level[1](v), level[2](v)) for p, v in here.items()}

    def planes_of(blocks):
        return [p for k in blocks for p in (2 * k - 1, 2 * k)]

    def gather(sums):
        sums = {k: [v[0] + ahead(v[0], 0)] if parts == 1 else [v[0] + v[1]] for k, v in sums.items()}
        if parts == 1:
            nexts, lasts = ([shift(v[0], 1) for v in sums.values()] for shift in (ahead, behind))
            return {
                k: [v[0] + jnp.where(even_lane, u, w)] for (k, v), u, w in zip(sums.items(), nexts, lasts)
            }
        return {k: [v[0] + ahead(v[0], 0)] for k, v in sums.items()}

    z_fine = turned(cond, planes_of(reach(HALO - 2)), fine)
    for k, v in gather({k: add(load(cond, 2 * k - 1), load(cond, 2 * k)) for k in reach(HALO)}).items():
        store(sum8, k, v)
    z_field = turned(field, planes_of(reach(HALO - 2)), fine) if seams[2] is not None else {}

    def weights(ref, p, level, around_z):
        step = level[0]
        c = load(ref, p)
        x = add(c, load(ref, p + 1))
        y, yb = ([v + shift(v, 0, step) for v in c] for shift in (ahead, behind))
        z, zb = (add(c, v) for v in around_z)
        k = add(add(c, load(ref, p - 1), x), add(y, yb), add(z, zb))
        return x, y, z, yb, zb, k, each(lambda v, w: jnp.where(v > 0.0, KEEP / w, 0.0), c, k)

    low = reach(HALO - 2).start
    store(wx, 2 * low - 2, add(load(cond, 2 * low - 2), load(cond, 2 * low - 1)))
    store(cwx, low - 1, add(load(sum8, low - 1), load(sum8, low)))
    z_coarse = turned(sum8, reach(HALO - 2), coarse)
    for k in reach(HALO - 2):
        for p in (2 * k - 1, 2 * k):
            for ref, v in zip((wx, wy, wz, vy, vz, diag, inv), weights(cond, p, fine, z_fine[p])):
                store(ref, p, v)
        for ref, v in zip((cwx, cwy, cwz, cvy, cvz, None, cinv), weights(sum8, k, coarse, z_coarse[k])):
            if ref is not None:
                store(ref, k, v)

    def spread(v, p, refs, level, around_z):
        x, y, z, yb, zb = refs
        step = level[0]
        here = load(v, p)
        n = add(times(load(x, p - 1), load(v, p - 1)), times(load(x, p), load(v, p + 1)))
        n = add(n, times(load(y, p), [ahead(u, 0, step) for u in here]))
        n = add(n, times(load(yb, p), [behind(u, 0, step) for u in here]))
        return add(n, add(times(load(z, p), around_z[0]), times(load(zb, p), around_z[1])))

    def smooth(v, p, refs, scale, level, around_z):
        n = times([(SPREAD_OVER_KEEP / KEEP) * u for u in load(scale, p)], spread(v, p, refs, level, around_z))
        return add(load(v, p), n)

    def between(p, around_z):
        planes, along_y, along_z = seams
        here = load(field, p)
        r = load(src, p)

        def less(r, weights, there, where=None):
            flux = each(lambda w, u, v: w * (u - v), weights, here, there)
            return each(lambda x, y: x - (y if where is None else jnp.where(where, y, 0.0)), r, flux)

        if p in planes:
            r = less(r, load(wx, p), load(field, p + 1))
        if p - 1 in planes:
            r = less(r, load(wx, p - 1), load(field, p - 1))
        r = less(r, load(wy, p), [ahead(v, 0) for v in here], along_y[0])
        r = less(r, load(vy, p), [behind(v, 0) for v in here], along_y[1])
        if along_z is not None:
            r = less(r, load(wz, p), around_z[0], along_z[0])
            r = less(r, load(vz, p), around_z[1], along_z[1])
        return r

    around, coarse_around = (wx, wy, wz, vy, vz), (cwx, cwy, cwz, cvy, cvz)

    for it in range(ITERS):
        halo = 4 * (ITERS - 1 - it)
        blocks = reach(halo + 2)
        rounds = turned(err, planes_of(blocks), fine) if it else z_field
        sums = {}
        for k in blocks:
            found = []
            for p in (2 * k - 1, 2 * k):
                if it == 0:
                    r = between(p, rounds.get(p))
                else:
                    n = spread(err, p, around, fine, rounds[p])
                    r = each(lambda u, d, w, m: u - (d * w - m), load(res, p), load(diag, p), load(err, p), n)
                if it < ITERS - 1:
                    store(res, p, r)
                store(q, p, times(r, load(inv, p)))
                found.append(r)
            sums[k] = add(*found)
        near = reach(halo)
        sums = gather(sums)
        rounds = turned(q, planes_of(near), fine)
        for k, v in sums.items():
            store(cq, k, times([4.0 * v[0]], load(cinv, k)))
        coarse_rounds = turned(cq, near, coarse)
        found = {k: smooth(cq, k, coarse_around, cinv, coarse, coarse_rounds[k])[0] for k in near}
        smoothed = {p: smooth(q, p, around, inv, fine, rounds[p]) for p in planes_of(near)}
        for k in near:
            c = jnp.where(even_row, found[k], behind(found[k], 0))
            for p in (2 * k - 1, 2 * k):
                e = [u + c for u in smoothed[p]]
                if it:
                    e = add(load(err, p), e)
                if it < ITERS - 1:
                    store(err, p, e)
                else:
                    out(p, add(load(field, p), e))


def layout(reflect, depth):
    return (1, depth + HALO + 2) if reflect else (1 + HALO, depth + 2 * HALO + 2)


def each_plane(reflect, depth, place):
    odd_x = is_odd("gx")
    own_at, _ = layout(reflect, depth)

    for p in range(depth):
        place(None, jnp.where(odd_x == 1, depth - 1 - p, p) if reflect else p, own_at + p)
    for p in range(HALO):
        if reflect:
            place(0, jnp.where(odd_x == 1, depth - 1 - p, p), own_at + depth + p)
            continue
        for i in range(2):
            above = odd_x == i
            at = jnp.where(above, p, depth - HALO + p)
            place(i, at, jnp.where(above, own_at + depth + p, 1 + p))


def x_seams(reflect, depth):
    own_at, _ = layout(reflect, depth)
    return (own_at + depth - 1,) if reflect else (own_at - 1, own_at + depth - 1)


def out_plane(reflect, depth, p):
    own_at, _ = layout(reflect, depth)
    at = p - own_at
    return jnp.where(is_odd("gx") == 1, depth - 1 - at, at) if reflect else at


def parting(width, lanes):
    column = lax.broadcasted_iota(jnp.int32, (width, 2 * lanes), 0)
    lane = lax.broadcasted_iota(jnp.int32, (width, 2 * lanes), 1)
    wanted = jnp.where(lane < lanes, 2 * lane, 2 * (lane - lanes) + 1)
    return jnp.where((column == wanted) & (wanted < width), 1.0, 0.0)


def ending(width):
    column = lax.broadcasted_iota(jnp.int32, (width, 2 * LANES), 0)
    lane = lax.broadcasted_iota(jnp.int32, (width, 2 * LANES), 1)
    lane = jnp.where(lane < LANES, lane, lane - LANES - LANES // 2)
    last = (lane >= 8) & (lane < 24) & (column == lane + width - 24)
    first = (lane >= 40) & (lane < 56) & (column == lane - 40)
    return jnp.where(last | first, 1.0, 0.0)


def rearranged(v, matrix):
    bf16, f32 = jnp.bfloat16, jnp.float32
    parts = []
    for _ in range(3):
        parts.append(v.astype(bf16))
        v = v - parts[-1].astype(f32)
    matrix = matrix.astype(bf16)
    return jnp.dot(jnp.concatenate(parts, 1), jnp.concatenate([matrix] * 3, 0), preferred_element_type=f32)


def interior(reflect, n_x, *refs):
    own, rim = refs[0], refs[1]
    near, near_rim = refs[2 : 2 + n_x], refs[2 + n_x : 2 + 2 * n_x]
    result, ends = refs[2 + 2 * n_x : 4 + 2 * n_x]
    whole, halves, *cells = refs[4 + 2 * n_x :]
    _, depth, inner, width = own.shape
    rows = inner + 2 * HALO
    lanes = cells[0].shape[3]

    def place(i, p_from, p_to):
        block, halo = (own, rim) if i is None else (near[i], near_rim[i])
        for a in range(3):
            tile = whole.at[a, p_to]
            tile[0:HALO, :] = halo[0, a, p_from]
            tile[HALO : HALO + inner, :] = block[a, p_from]
            tile[HALO + inner : rows, :] = halo[1, a, p_from]

    own_at, total = layout(reflect, depth)
    for a in range(3):
        for p in (0, total - 1):
            cells[a][p] = jnp.zeros((2, rows, lanes), jnp.float32)
            ends[a, p] = jnp.zeros((rows - 8, LANES), jnp.float32)
    each_plane(reflect, depth, place)
    apart = parting(width, lanes)
    target = jnp.concatenate([apart, ending(width)], 1)
    for a in range(3):
        inside = slice(1, total - 1)
        parts = rearranged(whole[a, inside].reshape((total - 2) * rows, width), target).reshape(total - 2, rows, -1)
        for i in range(2):
            cells[a][inside, i] = parts[:, :, i * lanes : (i + 1) * lanes]
        low = parts[:, 0 : rows - 8, 2 * lanes : 2 * lanes + LANES]
        ends[a, inside] = low + parts[:, 8:rows, 2 * lanes + LANES :]

    def out(p, v):
        for i in range(2):
            halves[p - own_at, :, i * lanes : (i + 1) * lanes] = v[i][HALO : rows - HALO, :]

    row = lax.broadcasted_iota(jnp.int32, (rows, lanes), 0)
    along_y = (row == HALO - 1) | (row == HALO + inner - 1), (row == HALO) | (row == HALO + inner)
    solve(cells, own_at, depth, out, (x_seams(reflect, depth), along_y, None))
    together = rearranged(halves[...].reshape(depth * inner, 2 * lanes), apart.T)
    together = together.reshape(depth, inner, width)
    for p in range(depth):
        result[out_plane(reflect, depth, own_at + p)] = together[p]


def edges(reflect, ends, inside, got_a, got_b, result, staged, sems, *cells):
    depth, inner, width = inside.shape
    odd_x, odd_z = is_odd("gx"), is_odd("grp")
    first_z, last_z = beyond("grp")
    lane = lax.broadcasted_iota(jnp.int32, (8, LANES), 1)
    half = LANES // 2
    own_at, total = layout(reflect, depth)
    for p in (0, total - 1):
        for a in range(3):
            cells[a][p, 0] = ends[a, p]

    windows = []

    def place(i, p_from, p_to):
        at_plane = p_from if i is None else (i + 1) * depth + p_from
        if reflect:
            va, vb = got_a[depth + p_from if i is None else p_from], got_b[at_plane]
            swapped = odd_x == 0
        else:
            va, vb = got_a[at_plane], got_b[at_plane]
            swapped = odd_z == 1
        right = jnp.where(last_z, 0.0, jnp.where(swapped, vb, va))
        left = jnp.where(first_z, 0.0, jnp.where(swapped, va, vb))
        windows.append((p_to, right, left, pltpu.roll(right, LANES - 8, 1), pltpu.roll(left, 8, 1)))

    here = lax.rem(lane, half)
    in_halo = (here >= 24) & (here < 40)
    each_plane(reflect, depth, place)
    side = lax.rem(lane, 16) >= 8
    groups = []
    for p, right, left, right_moved, left_moved in windows:
        lower, upper = jnp.where(side, right, left), jnp.where(side, right_moved, left_moved)
        groups.append((p, lower, pltpu.roll(jnp.where(lane < half, upper, lower), half, 1), upper))
    for a in (1, 2, 0):
        for p, *tiles in groups:
            for t, tile in enumerate(tiles):
                moved = tile if a == 1 else pltpu.roll(tile, (16 - 16 * a) % LANES, 1)
                part = slice(8 * t, 8 * t + 8)
                cells[a][p, 0, part, :] = jnp.where(in_halo, moved, ends[a, p, part, :])

    row = lax.broadcasted_iota(jnp.int32, ends.shape[2:], 0)
    lane_in_half = lax.rem(lax.broadcasted_iota(jnp.int32, ends.shape[2:], 1), half)
    upper_half = lax.broadcasted_iota(jnp.int32, ends.shape[2:], 1) >= half
    face = jnp.where(upper_half, inner, HALO)
    along_z = tuple((lane_in_half == at) | (lane_in_half == at + 16) for at in (23, 24))
    finals = []
    solve(cells, own_at, depth, lambda p, v: finals.append((p - own_at, v[0][8:16])), (x_seams(reflect, depth), (row == face - 1, row == face), along_z))
    moved = [
        (p, i, pltpu.roll(v, (LANES - 40 - half * i) % LANES, 1), pltpu.roll(v, (LANES - 24 - half * i) % LANES, 1))
        for p, v in finals
        for i in range(2)
    ]
    copies = []
    for p, i, head, tail in moved:
        at, part = out_plane(reflect, depth, own_at + p), slice(8 * i, 8 * i + 8)
        for c in range(0, width, LANES):
            tile = inside[at, part, c : c + LANES]
            if c == 0:
                tile = jnp.where(lane < HALO, head, tile)
            if c == width - LANES:
                tile = jnp.where(lane >= LANES - HALO, tail, tile)
            staged[p, part, c : c + LANES] = tile
        if i:
            copies.append(pltpu.make_async_copy(staged.at[p], result.at[at], sems.at[p]))
            copies[-1].start()
    for copy in copies:
        copy.wait()


def shards(sizes, source_term, conductivity, initial_field):
    depth, inner, width = source_term.shape
    assert inner == 16 and depth >= HALO and depth % 2 == 0 and width % LANES == 0
    rows = inner + 2 * HALO
    f32 = jnp.float32
    params = pltpu.CompilerParams(vmem_limit_bytes=48 * 1024 * 1024)
    args = (source_term, conductivity, initial_field)

    def exchange(values, axis):
        over, rounds = swaps(axis, sizes)
        found = [lax.ppermute(v, over, pairs) for v, pairs in reversed(list(zip(values, rounds)))]
        return found[::-1] + [jnp.zeros_like(v) for v in values[len(found) :]]

    def work(parts, rows, lanes):
        total = layout(reflect, depth)[1]
        fine = pltpu.VMEM((total, parts, rows, lanes), f32)
        coarse = pltpu.VMEM((total // 2 + 1, 1, rows, lanes), f32)
        return [fine] * 10 + [coarse] * 7 + [fine] * 2 + [coarse] + [fine]

    reflect = sizes["gx"] == 2
    n_x = 1 if reflect else 2
    args = [pltpu.with_memory_space_constraint(v, pltpu.HBM) for v in args]
    face = jax.ShapeDtypeStruct((depth + depth // 2 + n_x + 1, HALO, width), f32)
    own, *msgs = pl.pallas_call(
        functools.partial(prepare, reflect),
        out_shape=(jax.ShapeDtypeStruct((3, depth, inner, width), f32), face, face),
        in_specs=[pl.BlockSpec(memory_space=pltpu.HBM)] * 3, out_specs=(VMEM,) * 3,
        scratch_shapes=[pltpu.SemaphoreType.DMA((3,))], compiler_params=params, name="prepare",
    )(*args)
    got = exchange(msgs, "gy")
    strips, rim = pl.pallas_call(
        functools.partial(pack_columns, reflect),
        out_shape=(
            jax.ShapeDtypeStruct((2, depth, 8, LANES), f32),
            jax.ShapeDtypeStruct((2, 3, depth, HALO, width), f32),
        ),
        in_specs=[VMEM] * 3, out_specs=(VMEM, VMEM),
        compiler_params=params, name="pack_columns",
    )(own, *got)
    if reflect:
        strips = jnp.concatenate([strips[0]] + exchange([strips[1]], "gx"), axis=0)
    else:
        strips = jnp.concatenate([strips] + exchange([strips] * n_x, "gx"), axis=1)
    strips, own = lax.optimization_barrier((strips, own))
    near = exchange([own] * n_x, "gx")
    near_rim = exchange([rim] * n_x, "gx")
    if reflect:
        strips = [lax.ppermute(strips, tuple(sizes), crossing(sizes))]
    else:
        strips = exchange([strips[0], strips[1]], "grp")

    block = jax.ShapeDtypeStruct(source_term.shape, f32)
    total = layout(reflect, depth)[1]
    lanes = -(-width // (2 * LANES)) * LANES
    apart = [pltpu.VMEM((3, total, rows, width), f32), pltpu.VMEM((depth, inner, 2 * lanes), f32)]
    inside, ends = pl.pallas_call(
        functools.partial(interior, reflect, n_x),
        out_shape=(block, jax.ShapeDtypeStruct((3, total, rows - 8, LANES), f32)),
        in_specs=[VMEM] * (2 + 2 * n_x), out_specs=(VMEM, VMEM), scratch_shapes=apart + work(2, rows, lanes),
        compiler_params=params, name="interior",
        cost_estimate=pl.CostEstimate(flops=20_000_000, bytes_accessed=20_000_000, transcendentals=0),
    )(own, rim, *near, *near_rim)
    inside, ends, *strips = lax.optimization_barrier((inside, ends, *strips[::-1]))
    strips = strips[::-1]
    if reflect:
        strips += exchange(strips, "gx")
    return pl.pallas_call(
        functools.partial(edges, reflect),
        out_shape=block,
        in_specs=[VMEM] * 4, out_specs=pl.BlockSpec(memory_space=pltpu.HBM),
        scratch_shapes=[pltpu.VMEM((depth, inner, width), f32), pltpu.SemaphoreType.DMA((depth,))] + work(1, rows - 8, LANES),
        compiler_params=params, name="edges",
    )(ends, inside, *strips)


def solution(mesh):
    spec = P("gx", "gy", "grp")
    return jax.shard_map(
        functools.partial(shards, dict(mesh.shape)),
        mesh=mesh,
        in_specs=(spec,) * 3,
        out_specs=spec,
        check_vma=False,
    )
```
